32 devices in a mesh: shard: 16 (over z, y, x), ctx: 2 (over core).
Axes of the slice: x: 2, y: 2, z: 4, core: 2. Of those that a mesh axis runs over, the one named last changes fastest.
Arguments:
- tokens: bfloat16 [16, 2048, 384], P('shard', 'ctx'), may hold values from -6 to 6
- condition: bfloat16 [16, 384], P('shard'), may hold values from -6 to 6
- cotangent: bfloat16 [16, 2048, 384], P('shard', 'ctx'), may hold values from -6 to 6
- modulate_weight: float32 [384, 2304], P(None, 'shard'), may hold values from -0.3125 to 0.3125
- attend_weight: float32 [384, 1152], P(None, 'shard'), may hold values from -0.3125 to 0.3125
- project_weight: float32 [384, 384], P(None, 'shard'), may hold values from -0.875 to 0.875
- expand_weight: float32 [384, 1536], P(None, 'shard'), may hold values from -0.3125 to 0.3125
- reduce_weight: float32 [384, 1536], P(None, 'shard'), may hold values from -0.15625 to 0.15625
- bias_flat: float32 [5376], P('shard'), may hold values from -4 to 4
- modulate_moment: float32 [384, 2304], P(None, 'shard'), may hold values from -22 to 22, as said below
- attend_moment: float32 [384, 1152], P(None, 'shard'), may hold values from -22 to 22, as said below
- project_moment: float32 [384, 384], P(None, 'shard'), may hold values from -22 to 22, as said below
- expand_moment: float32 [384, 1536], P(None, 'shard'), may hold values from -22 to 22, as said below
- reduce_moment: float32 [384, 1536], P(None, 'shard'), may hold values from -22 to 22, as said below
- bias_moment: float32 [5376], P('shard'), may hold values from -4 to 4
Outputs:
- block_out: bfloat16 [16, 2048, 384], P('shard', 'ctx')
- tokens_grad: float32 [16, 2048, 384], P('shard', 'ctx')
- condition_grad: float32 [16, 384], P('shard')
- modulate_grad: float32 [384, 2304], P(None, 'shard')
- modulate_master: float32 [384, 2304], P(None, 'shard')
- modulate_momentum: float32 [384, 2304], P(None, 'shard')
- attend_grad: float32 [384, 1152], P(None, 'shard')
- attend_master: float32 [384, 1152], P(None, 'shard')
- attend_momentum: float32 [384, 1152], P(None, 'shard')
- project_grad: float32 [384, 384], P(None, 'shard')
- project_master: float32 [384, 384], P(None, 'shard')
- project_momentum: float32 [384, 384], P(None, 'shard')
- expand_grad: float32 [384, 1536], P(None, 'shard')
- expand_master: float32 [384, 1536], P(None, 'shard')
- expand_momentum: float32 [384, 1536], P(None, 'shard')
- reduce_grad: float32 [384, 1536], P(None, 'shard')
- reduce_master: float32 [384, 1536], P(None, 'shard')
- reduce_momentum: float32 [384, 1536], P(None, 'shard')
- bias_grad: float32 [5376], P('shard')
- bias_master: float32 [5376], P('shard')
- bias_momentum: float32 [5376], P('shard')
The draws below stay inside these ranges and needn't reach their ends.
Inputs may be any that keep to these rules, and one draw needn't show every extreme that they name: `modulate_moment`: entries of the old momentum. `attend_moment`: entries of the old momentum. `project_moment`: entries of the old momentum. `expand_moment`: entries of the old momentum. `reduce_moment`: entries of the old momentum.
All inputs are finite; a program needn't handle non-finite values.
Results may differ from the reference program's by a relative error of at most 0.011.
The reference program's roundings to bfloat16 on the way count: a program that leaves them out, or rounds other values in their place, can miss the bound.
Values may be sent and summed in bfloat16 or wider, within the bound.
A program may use at most 320 MiB of HBM per device.

```python
import math
import jax
import jax.numpy as jnp
from jax import lax

D = 384
FF = 1536
HEADS = 6
HEAD_DIM = 64
SEQ = 2048
NS_ITERS = 5
LATENTS = 16
NB = 5376
N_SHARD = 16


def heavy_moment(key, columns):
    block_key, value_key = jax.random.split(key)
    width = columns // N_SHARD
    heavy_block = jax.random.randint(block_key, (), 0, N_SHARD)
    base = jnp.clip(0.3 * jax.random.normal(value_key, (D, columns), jnp.float32), -1.8, 1.8)
    column_block = jnp.arange(columns) // width
    factor = jnp.where(column_block == heavy_block, 12.0, 1.0).astype(jnp.float32)
    return base * factor[None, :]


def draw_modulate_moment(key, part):
    key = jax.random.fold_in(key, 11)
    return heavy_moment(key, 6 * D)


def draw_attend_moment(key, part):
    key = jax.random.fold_in(key, 12)
    return heavy_moment(key, 3 * D)


def draw_project_moment(key, part):
    key = jax.random.fold_in(key, 13)
    return heavy_moment(key, D)


def draw_expand_moment(key, part):
    key = jax.random.fold_in(key, 14)
    return heavy_moment(key, FF)


def draw_reduce_moment(key, part):
    key = jax.random.fold_in(key, 15)
    return heavy_moment(key, FF)


def block_levels(rng, dims, cuts, least, largest):
    factor_of, own = 1.0, jax.random.fold_in(rng, 6)
    for axis_at, parts in cuts:
        draws = jnp.exp(jax.random.uniform(jax.random.fold_in(own, axis_at), (parts,), jnp.float32, least / len(cuts), largest / len(cuts)))
        factor_of = factor_of * jnp.repeat(draws, dims[axis_at] // parts).reshape([-1 if axis == axis_at else 1 for axis in range(len(dims))])
    return factor_of


def bell_draw(key, extent, scale, reach, pieces=(), dtype=jnp.bfloat16):
    values = jax.random.normal(key, extent, jnp.float32) * scale
    if len(pieces) > 0:
        values = block_levels(key, extent, pieces, -0.22, 0.18) * values
    return jnp.clip(values, min=-reach, max=reach).astype(dtype)


def setup_inputs(seed: int = 0) -> dict:
    seeds = jax.random.split(jax.random.key(seed), 16)
    return {
        "tokens": bell_draw(seeds[0], (LATENTS, SEQ, D), 1.0, 6.0, ((0, 16), (1, 2))),
        "condition": bell_draw(seeds[1], (LATENTS, D), 1.0, 6.0, ((0, 16),)),
        "cotangent": bell_draw(seeds[2], (LATENTS, SEQ, D), 1.0, 6.0, ((0, 16), (1, 2))),
        "modulate_weight": bell_draw(seeds[3], (D, 6 * D), D ** -0.5, 0.3125, ((1, 16),), jnp.float32),
        "attend_weight": bell_draw(seeds[4], (D, 3 * D), D ** -0.5, 0.3125, ((1, 16),), jnp.float32),
        "project_weight": bell_draw(seeds[5], (D, D), (D // 8) ** -0.5, 0.875, ((1, 16),), jnp.float32),
        "expand_weight": bell_draw(seeds[6], (D, FF), D ** -0.5, 0.3125, ((1, 16),), jnp.float32),
        "reduce_weight": bell_draw(seeds[7], (D, FF), FF ** -0.5, 0.15625, ((1, 16),), jnp.float32),
        "bias_flat": bell_draw(seeds[8], (NB,), 0.3, 4.0, ((0, 16),), jnp.float32),
        "modulate_moment": draw_modulate_moment(jax.random.fold_in(seeds[15], 71), 0),
        "attend_moment": draw_attend_moment(jax.random.fold_in(seeds[15], 71), 0),
        "project_moment": draw_project_moment(jax.random.fold_in(seeds[15], 71), 0),
        "expand_moment": draw_expand_moment(jax.random.fold_in(seeds[15], 71), 0),
        "reduce_moment": draw_reduce_moment(jax.random.fold_in(seeds[15], 71), 0),
        "bias_moment": bell_draw(seeds[14], (NB,), 0.3, 4.0, ((0, 16),), jnp.float32),
    }


@jax.custom_vjp
def low(v):
    return lax.optimization_barrier(v.astype(jnp.bfloat16)).astype(jnp.float32)

@jax.custom_vjp
def low_back(v):
    return v

def low_keep(v):
    return (low(v), None)

def low_pass(kept, grad):
    return (grad,)

def back_keep(v):
    return (v, None)

def back_low(kept, grad):
    return (low(grad),)
low.defvjp(low_keep, low_pass)
low_back.defvjp(back_keep, back_low)
norm_eps = 1e-06
newton_a = 3.4445
newton_b = -4.775
newton_c = 2.0315
moment_decay = 0.95
matrix_rate = 0.5
bias_rate = 0.1
precise = lax.Precision.HIGHEST

def silu_of(values):
    return values * jax.nn.sigmoid(values)

def gelu_tanh(values):
    return 0.5 * values * (1.0 + jnp.tanh(0.7978845608028654 * (values + 0.044715 * values * values * values)))

def normalize(values):
    centered = values - lax.optimization_barrier(jnp.mean(values, axis=-1, keepdims=True))
    return centered * lax.rsqrt(lax.optimization_barrier(jnp.mean(centered * centered, axis=-1, keepdims=True)) + norm_eps)

def newton_whole(matrix):
    norm_value = jnp.sqrt(jnp.sum(matrix * matrix))
    iterate = matrix / (norm_value + 1e-07)
    for sweep_index in range(NS_ITERS):
        gram_now = jnp.dot(iterate, iterate.T, precision=precise)
        polynomial = newton_b * gram_now + newton_c * jnp.dot(gram_now, gram_now, precision=precise)
        iterate = newton_a * iterate + jnp.dot(polynomial, iterate, precision=precise)
    return iterate

def forward(tok_float, cond_float, params):
    modulate, attend, project, expand, reduce_low, bias = tuple((low(param) for param in params))
    group_size, length = (tok_float.shape[0], tok_float.shape[1])
    silu_low = low(silu_of(cond_float))
    modulation = jnp.dot(silu_low, modulate, precision=precise) + bias[:6 * D]
    shift_one, scale_one, gate_one, shift_two, scale_two, gate_two = jnp.split(modulation[:, None, :], 6, axis=-1)
    attend_in = low(normalize(tok_float) * (1.0 + scale_one) + shift_one)
    qkv_bias = jnp.concatenate([bias[6 * D:7 * D], jnp.zeros((D,), jnp.float32), bias[7 * D:8 * D]])
    qkv = low(low_back(jnp.einsum('gtd,de->gte', attend_in, attend, precision=precise) + qkv_bias))
    queries = qkv[:, :, :D].reshape(group_size, length, HEADS, HEAD_DIM)
    key_rows = qkv[:, :, D:2 * D].reshape(group_size, length, HEADS, HEAD_DIM)
    value_rows = qkv[:, :, 2 * D:].reshape(group_size, length, HEADS, HEAD_DIM)
    scores = low_back(jnp.einsum('gqhd,gkhd->ghqk', queries, key_rows, precision=precise) * HEAD_DIM ** (-0.5))
    row_max = lax.optimization_barrier(jnp.max(scores, axis=-1, keepdims=True))
    shifted = jnp.exp(scores - row_max)
    attn_probs = shifted / lax.optimization_barrier(jnp.sum(shifted, axis=-1, keepdims=True))
    context = low(low_back(jnp.einsum('ghqk,gkhd->gqhd', low(attn_probs), value_rows, precision=precise)))
    context = context.reshape(group_size, length, D)
    attended = low_back(jnp.einsum('gtd,de->gte', context, project, precision=precise) + bias[8 * D:9 * D])
    middle = tok_float + gate_one * attended
    expand_in = low(normalize(middle) * (1.0 + scale_two) + shift_two)
    hidden = low_back(jnp.einsum('gtd,df->gtf', expand_in, expand, precision=precise) + bias[9 * D:9 * D + FF])
    act_low = low(gelu_tanh(hidden))
    mlp_out = low_back(jnp.einsum('gtf,df->gtd', act_low, reduce_low, precision=precise) + bias[9 * D + FF:])
    return middle + gate_two * mlp_out

def add_up(running, fresh):
    return running + fresh

def reference(tokens, condition, cotangent, modulate_weight, attend_weight, project_weight, expand_weight, reduce_weight, bias_flat, modulate_moment, attend_moment, project_moment, expand_moment, reduce_moment, bias_moment):
    masters = (modulate_weight, attend_weight, project_weight, expand_weight, reduce_weight, bias_flat)
    group_size = math.gcd(LATENTS, max(1, 4096 // SEQ))
    block_count = LATENTS // group_size
    tok_blocks = tokens.astype(jnp.float32).reshape(block_count, group_size, SEQ, D)
    cond_blocks = condition.astype(jnp.float32).reshape(block_count, group_size, D)
    cot_blocks = cotangent.astype(jnp.float32).reshape(block_count, group_size, SEQ, D)

    def one_block(totals, inputs):
        tok_block, cond_block, cot_block = inputs
        result, pullback = jax.vjp(forward, tok_block, cond_block, masters)
        tok_grad, cond_grad, param_grads = pullback(cot_block)
        totals = jax.tree.map(add_up, totals, param_grads)
        return (totals, (result.astype(jnp.bfloat16), tok_grad, cond_grad))
    start_totals = tuple((jnp.zeros_like(master) for master in masters))
    totals, (outputs, tok_grads, cond_grads) = lax.scan(one_block, start_totals, (tok_blocks, cond_blocks, cot_blocks))
    grad_scale = 1.0 / math.sqrt(LATENTS * SEQ)
    grads = tuple((total * grad_scale for total in totals))
    old_moments = (modulate_moment, attend_moment, project_moment, expand_moment, reduce_moment, bias_moment)
    new_moments = tuple((moment_decay * old_moment + grad_item for old_moment, grad_item in zip(old_moments, grads)))
    new_masters = tuple((master - matrix_rate * 0.2 * math.sqrt(max(D, master.shape[1])) * newton_whole(moment) for master, moment in zip(masters[:5], new_moments[:5])))
    new_bias = bias_flat - bias_rate * new_moments[5]
    return (outputs.reshape(LATENTS, SEQ, D), tok_grads.reshape(LATENTS, SEQ, D), cond_grads.reshape(LATENTS, D), grads[0], new_masters[0], new_moments[0], grads[1], new_masters[1], new_moments[1], grads[2], new_masters[2], new_moments[2], grads[3], new_masters[3], new_moments[3], grads[4], new_masters[4], new_moments[4], grads[5], new_bias, new_moments[5])
```

```python
import functools
import math

import jax
import jax.numpy as jnp
from jax import lax
from jax.experimental import pallas as pl
from jax.experimental.pallas import tpu as pltpu
from jax.sharding import PartitionSpec as P

D = 384
FF = 1536
HEADS = 6
HEAD_DIM = 64
NS_ITERS = 5
HALF_HEADS = HEADS // 2
HALF = HALF_HEADS * HEAD_DIM

norm_eps = 1e-06
newton_a = 3.4445
newton_b = -4.775
newton_c = 2.0315
moment_decay = 0.95
matrix_rate = 0.5
bias_rate = 0.1
precise = lax.Precision.HIGHEST
LOG2E = 1.4426950408889634

MESH = pl.DeviceIdType.MESH
BF = jnp.bfloat16
F32 = jnp.float32
VMEM_BYTES = 60 * 2**20
VM = pl.BlockSpec(memory_space=pltpu.VMEM)


def params(collective=None):
    if collective is None:
        return pltpu.CompilerParams(vmem_limit_bytes=VMEM_BYTES)
    return pltpu.CompilerParams(
        collective_id=collective, has_side_effects=True, vmem_limit_bytes=VMEM_BYTES
    )


def dot(left, right):
    return jnp.dot(left, right, preferred_element_type=F32)


def dot_nt(left, right):
    return lax.dot_general(left, right, (((1,), (1,)), ((), ())), preferred_element_type=F32)


def dot_tn(left, right):
    return lax.dot_general(left, right, (((0,), (0,)), ((), ())), preferred_element_type=F32)


def split_low(values):
    high = values.astype(BF)
    return high, (values - high.astype(F32)).astype(BF)


def dot_three(left, right, op=dot):
    left_high, left_low = split_low(left)
    right_high, right_low = split_low(right)
    return op(left_high, right_high) + (op(left_high, right_low) + op(left_low, right_high))


def silu_of(values):
    return values * jax.nn.sigmoid(values)


def normalize(values):
    centered = values - jnp.mean(values, axis=-1, keepdims=True)
    inverse = lax.rsqrt(jnp.mean(centered * centered, axis=-1, keepdims=True) + norm_eps)
    return (centered * inverse, inverse)


def norm_back(grad_normed, normed, inverse):
    first = jnp.mean(grad_normed, axis=-1, keepdims=True)
    second = jnp.mean(grad_normed * normed, axis=-1, keepdims=True)
    return (grad_normed - first - normed * second) * inverse


def bit_of(value, bit):
    return lax.rem(value // (1 << bit), 2)


def flip(me, bit):
    return me + (1 - 2 * bit_of(me, bit)) * (1 << bit)


def other_core():
    return {"ctx": 1 - lax.axis_index("ctx")}


def signal_cube(me, nbits):
    sem = pltpu.get_barrier_semaphore()
    for bit in range(nbits):
        pl.semaphore_signal(
            sem, inc=1, device_id={"shard": flip(me, bit)}, device_id_type=MESH
        )
    pl.semaphore_signal(sem, inc=1, device_id=other_core(), device_id_type=MESH)
    pl.semaphore_wait(sem, nbits + 1)


def signal_all(me, count):
    sem = pltpu.get_barrier_semaphore()
    for step in range(1, count):
        pl.semaphore_signal(
            sem, inc=1, device_id={"shard": lax.rem(me + step, count)}, device_id_type=MESH
        )
    pl.semaphore_signal(sem, inc=1, device_id=other_core(), device_id_type=MESH)
    pl.semaphore_wait(sem, count)


def signal_core():
    sem = pltpu.get_barrier_semaphore()
    pl.semaphore_signal(sem, inc=1, device_id=other_core(), device_id_type=MESH)
    pl.semaphore_wait(sem, 1)


def remote(src, dst, send, recv, where):
    return pltpu.make_async_remote_copy(
        src, dst, send, recv, device_id=where, device_id_type=MESH
    )


def orders(nbits):
    up = list(range(nbits))
    return up, ([1, 0] + up[2:] if nbits >= 2 else up)


def cube_index(who, nbits, free, tail=()):
    lead = tuple(
        slice(None) if (nbits - 1 - d) in free else bit_of(who, nbits - 1 - d)
        for d in range(nbits)
    )
    return lead + tuple(tail)


def gather_kernel(
    nbits,
    width,
    own_ref,
    small_ref,
    wmod_ref,
    tok_ref,
    whole_ref,
    small_all,
    mod_all,
    tok_all,
    mod_send,
    send,
    recv,
    psend,
    precv,
    ssend,
    srecv,
    msend,
    mrecv,
    tsem,
    lsem,
):
    count = 1 << nbits
    me = lax.axis_index("shard")
    core = lax.axis_index("ctx")
    signal_all(me, count)
    small_all[me] = small_ref[...]
    spread = []
    for step in range(1, count):
        to = lax.rem(me + step, count)
        copy = remote(
            small_ref, small_all.at[me], ssend.at[step], srecv.at[step], {"shard": to}
        )
        copy.start()
        spread.append(copy)
    toks = remote(tok_ref, tok_all.at[core], tsem.at[0], tsem.at[1], other_core())
    toks.start()
    tok_all[core] = tok_ref[...]
    own = cube_index(me, nbits, ())
    local = pltpu.make_async_copy(own_ref, whole_ref.at[own], lsem)
    local.start()
    local.wait()
    up, other = orders(nbits)

    def cube_step(which, step, seq):
        held = seq[:step]
        bit = seq[step]
        part = whole_ref.at[cube_index(me, nbits, held, (which,))]
        return remote(part, part, send.at[step], recv.at[step], {"shard": flip(me, bit)})

    def forward(which, step, seq):
        held = seq[:step]
        bit = seq[step]
        part = whole_ref.at[cube_index(flip(me, bit), nbits, held, (which,))]
        return remote(part, part, psend.at[step], precv.at[step], other_core())

    for which, order in enumerate((up, other)):

        @pl.when(core == which)
        def _():
            cube_step(which, 0, order[::-1]).start()

    for copy in spread:
        copy.wait()
    cond = small_all[:, 0, :]
    silu_low = silu_of(cond).astype(BF)
    part = dot(silu_low, wmod_ref[...])
    for row in range(count):
        mod_send[row] = jnp.broadcast_to(part[row : row + 1, :], (8, width))
    mod_all[me] = mod_send[me]
    mods = []
    for step in range(1, count):
        to = lax.rem(me + step, count)
        copy = remote(mod_send.at[to], mod_all.at[me], msend.at[step], mrecv.at[step], {"shard": to})
        copy.start()
        mods.append(copy)
    for which, order in enumerate((up, other)):

        @pl.when(core == which)
        def _():
            seq = order[::-1]
            for step in range(nbits):
                now = cube_step(which, step, seq)
                if step > 0:
                    now.start()
                now.wait()
                forward(which, step, seq).start()
            for step in range(nbits):
                forward(which, step, seq).wait_send()
            back = (other if which == 0 else up)[::-1]
            for step in range(nbits):
                forward(1 - which, step, back).wait_recv()

    for copy in mods:
        copy.wait()
    toks.wait()


def gather(own, small, wmod, tok, count):
    nbits = count.bit_length() - 1
    rows = own.shape[0]
    half = rows // 2
    width = wmod.shape[1]
    sems = lambda n: pltpu.SemaphoreType.DMA((n,))
    whole, small_all, mod_all, tok_all = pl.pallas_call(
        functools.partial(gather_kernel, nbits, width),
        out_shape=[
            jax.ShapeDtypeStruct((2,) * nbits + (2, half, D), BF),
            jax.ShapeDtypeStruct((count, 8, D), F32),
            jax.ShapeDtypeStruct((count, 8, width), F32),
            jax.ShapeDtypeStruct((2,) + tok.shape, BF),
        ],
        in_specs=[VM] * 4,
        out_specs=[VM] * 4,
        scratch_shapes=[
            pltpu.VMEM((count, 8, width), F32),
            sems(nbits),
            sems(nbits),
            sems(nbits),
            sems(nbits),
            sems(count),
            sems(count),
            sems(count),
            sems(count),
            sems(2),
            pltpu.SemaphoreType.DMA,
        ],
        compiler_params=params(0),
        name="gather",
    )(own.reshape(2, half, D), small, wmod, tok)
    return whole.reshape(count, rows, D), small_all, mod_all, tok_all


def forward_kernel(
    tok_ref,
    mod_ref,
    w_ref,
    bias_ref,
    xin_ref,
    q_ref,
    k_ref,
    v_ref,
    ctx_ref,
    lse_ref,
    both_ref,
    cols,
    outgoing,
    sems,
):
    core = lax.axis_index("ctx")
    signal_core()
    half = tok_ref.shape[1]
    shift = mod_ref[0:1, :]
    scale = 1.0 + mod_ref[1:2, :]
    block = 256

    def norm_block(index, _):
        rows = pl.ds(pl.multiple_of(index * block, block), block)
        for side in range(2):
            normed, _inverse = normalize(tok_ref[side, rows, :].astype(F32))
            xin_ref[side, rows, :] = (normed * scale + shift).astype(BF)
        return 0

    lax.fori_loop(0, half // block, norm_block, 0)
    for side in range(2):
        xin = xin_ref[side]
        rows = pl.ds(side * half, half)
        query = dot_nt(w_ref[0:HALF, :], xin) + bias_ref[0:HALF, 0:1]
        value = dot_nt(w_ref[2 * HALF :, :], xin) + bias_ref[2 * HALF :, 0:1]
        query = query.astype(BF) * jnp.asarray(HEAD_DIM**-0.5, BF)
        value = value.astype(BF)
        for head in range(HALF_HEADS):
            part = slice(head * HEAD_DIM, (head + 1) * HEAD_DIM)
            q_ref[head, side] = query[part, :]
            v_ref[head, :, rows] = value[part, :]
            k_ref[head, rows, :] = dot_nt(
                xin, w_ref[HALF + head * HEAD_DIM : HALF + (head + 1) * HEAD_DIM, :]
            ).astype(BF)

    def attend(step, _):
        head = step // 2
        side = lax.rem(step, 2)
        scores = dot(k_ref[head], q_ref[head, side])
        top = jnp.max(scores, axis=0, keepdims=True)
        shifted = jnp.exp2((scores - top) * LOG2E)
        total = jnp.sum(shifted, axis=0, keepdims=True)
        probs = (shifted * (1.0 / total)).astype(BF)
        out = dot(v_ref[head], probs)
        ctx_ref[head, side] = out
        lse_ref[head, side] = jnp.broadcast_to(top * LOG2E + jnp.log2(total), (8, half))
        cols[side, pl.ds(pl.multiple_of(head * HEAD_DIM, HEAD_DIM), HEAD_DIM), :] = out
        return 0

    lax.fori_loop(0, 2 * HALF_HEADS, attend, 0)
    outgoing[...] = jnp.transpose(cols[1 - core]).astype(BF)
    copy = remote(outgoing, both_ref.at[core], sems.at[0], sems.at[1], other_core())
    copy.start()
    both_ref[core] = jnp.transpose(cols[core]).astype(BF)
    copy.wait()


def attention_forward(tok_all, mod_rows, weight, bias_cols):
    half = tok_all.shape[1]
    full = 2 * half
    shape = jax.ShapeDtypeStruct
    return pl.pallas_call(
        forward_kernel,
        out_shape=[
            shape((2, half, D), BF),
            shape((HALF_HEADS, 2, HEAD_DIM, half), BF),
            shape((HALF_HEADS, full, HEAD_DIM), BF),
            shape((HALF_HEADS, HEAD_DIM, full), BF),
            shape((HALF_HEADS, 2, HEAD_DIM, half), F32),
            shape((HALF_HEADS, 2, 8, half), F32),
            shape((2, half, HALF), BF),
        ],
        in_specs=[VM] * 4,
        out_specs=[VM] * 7,
        scratch_shapes=[
            pltpu.VMEM((2, HALF, half), F32),
            pltpu.VMEM((half, HALF), BF),
            pltpu.SemaphoreType.DMA((2,)),
        ],
        compiler_params=params(1),
        name="attend_forward",
    )(tok_all, mod_rows, weight, bias_cols)


def branch_kernel(
    ctx_ref,
    tok_ref,
    cot_ref,
    mod_ref,
    bias_ref,
    wide_ref,
    wp_ref,
    we_ref,
    wr_ref,
    out_ref,
    mid_ref,
    gp_ref,
    ge_ref,
    gr_ref,
    sums_ref,
    wides_ref,
    both_ref,
    outgoing,
    sems,
):
    core = lax.axis_index("ctx")
    signal_core()
    half = tok_ref.shape[0]
    block = 256
    gate_one = mod_ref[2:3, :]
    shift_two = mod_ref[3:4, :]
    scale_two = 1.0 + mod_ref[4:5, :]
    gate_two = mod_ref[5:6, :]
    gp_ref[...] = jnp.zeros_like(gp_ref)
    ge_ref[...] = jnp.zeros_like(ge_ref)
    gr_ref[...] = jnp.zeros_like(gr_ref)
    sums_ref[...] = jnp.zeros_like(sums_ref)
    wides_ref[...] = jnp.zeros_like(wides_ref)

    def step(index, _):
        rows = pl.ds(pl.multiple_of(index * block, block), block)
        ctx = jnp.concatenate([ctx_ref[0, rows, :], ctx_ref[1, rows, :]], axis=1)
        attended = dot_nt(ctx, wp_ref[...]) + bias_ref[0:1, :]
        middle = tok_ref[rows, :].astype(F32) + gate_one * attended
        normed, inverse = normalize(middle)
        expand_in = (normed * scale_two + shift_two).astype(BF)
        hidden = dot_nt(expand_in, we_ref[...]) + wide_ref[0:1, :]
        squared = hidden * hidden
        bend = jnp.tanh(0.7978845608028654 * (hidden + 0.044715 * squared * hidden))
        rise = 0.5 * (1.0 + bend)
        act = (hidden * rise).astype(BF)
        slope = rise + 0.5 * hidden * (1.0 - bend * bend) * (
            0.7978845608028654 * (1.0 + 3.0 * 0.044715 * squared)
        )
        mlp_out = dot(act, wr_ref[...]) + bias_ref[1:2, :]
        out_ref[rows, :] = (middle + gate_two * mlp_out).astype(BF)
        grad_out = cot_ref[rows, :].astype(F32)
        grad_mlp = (gate_two * grad_out).astype(BF)
        gr_ref[...] += dot_tn(act, grad_mlp)
        grad_hidden = (dot_nt(grad_mlp, wr_ref[...]) * slope).astype(BF)
        ge_ref[...] += dot_tn(grad_hidden, expand_in)
        grad_in = dot(grad_hidden, we_ref[...])
        grad_middle = grad_out + norm_back(grad_in * scale_two, normed, inverse)
        mid_ref[rows, :] = grad_middle
        grad_attended = (gate_one * grad_middle).astype(BF)
        gp_ref[...] += dot_tn(grad_attended, ctx)
        back = dot(grad_attended, wp_ref[...]).astype(BF)
        first, second = back[:, :HALF], back[:, HALF:]
        both_ref[core, rows, :] = jnp.where(core == 0, first, second)
        outgoing[rows, :] = jnp.where(core == 0, second, first)
        add = lambda value: jnp.sum(value, axis=0, keepdims=True)
        sums_ref[0:1, :] += add(grad_out * mlp_out)
        sums_ref[1:2, :] += add(grad_in)
        sums_ref[2:3, :] += add(grad_in * normed)
        sums_ref[3:4, :] += add(grad_middle * attended)
        sums_ref[4:5, :] += add(grad_attended.astype(F32))
        sums_ref[5:6, :] += add(grad_mlp.astype(F32))
        wides_ref[0:1, :] += add(grad_hidden.astype(F32))
        return 0

    lax.fori_loop(0, half // block, step, 0)
    copy = remote(outgoing, both_ref.at[core], sems.at[0], sems.at[1], other_core())
    copy.start()
    copy.wait()


def branch(ctx, tok, cot, mod_rows, bias_rows, wide_rows, wp, we, wr):
    half = tok.shape[0]
    shape = jax.ShapeDtypeStruct
    return pl.pallas_call(
        branch_kernel,
        out_shape=[
            shape((half, D), BF),
            shape((half, D), F32),
            shape((D, D), F32),
            shape((FF, D), F32),
            shape((FF, D), F32),
            shape((8, D), F32),
            shape((8, FF), F32),
            shape((2, half, HALF), BF),
        ],
        in_specs=[VM] * 9,
        out_specs=[VM] * 8,
        scratch_shapes=[pltpu.VMEM((half, HALF), BF), pltpu.SemaphoreType.DMA((2,))],
        compiler_params=params(2),
        name="branch",
    )(ctx, tok, cot, mod_rows, bias_rows, wide_rows, wp, we, wr)


def backward_kernel(
    dctx_ref,
    xin_ref,
    q_ref,
    k_ref,
    v_ref,
    ctx_ref,
    lse_ref,
    w_ref,
    tok_ref,
    mid_ref,
    mod_ref,
    grad_ref,
    gw_ref,
    sums_ref,
    bias_ref,
    k_turn,
    v_rows,
    dk_sum,
    dv_sum,
    dq_low,
    dk_low,
    dv_low,
    outgoing,
    incoming,
    sems,
):
    core = lax.axis_index("ctx")
    signal_core()
    half = tok_ref.shape[0]
    full = 2 * half
    turn = lambda value: jnp.transpose(value.astype(F32)).astype(BF)

    for head in range(HALF_HEADS):
        k_turn[...] = turn(k_ref[head])
        v_rows[...] = turn(v_ref[head])
        dk_sum[...] = jnp.zeros_like(dk_sum)
        dv_sum[...] = jnp.zeros_like(dv_sum)

        def step(side, _):
            query = q_ref[head, side]
            down = dctx_ref[side, :, head * HEAD_DIM : (head + 1) * HEAD_DIM]
            down_turn = jnp.transpose(down.astype(F32))
            delta = jnp.sum(down_turn * ctx_ref[head, side], axis=0, keepdims=True)
            scores = dot(k_ref[head], query)
            probs = jnp.exp2(scores * LOG2E - lse_ref[head, side, 0:1, :])
            dv_sum[...] += dot(probs.astype(BF), down)
            grad_probs = dot(v_rows[...], down_turn.astype(BF))
            grad_scores = (probs * (grad_probs - delta)).astype(BF)
            dk_sum[...] += dot(grad_scores, turn(query))
            dq_low[head, side] = (
                jnp.transpose(dot(k_turn[...], grad_scores)) * (HEAD_DIM**-0.5)
            ).astype(BF)
            return 0

        lax.fori_loop(0, 2, step, 0)
        dk_low[head] = dk_sum[...].reshape(2, half, HEAD_DIM).astype(BF)
        dv_low[head] = dv_sum[...].reshape(2, half, HEAD_DIM).astype(BF)

    gw_ref[...] = jnp.zeros_like(gw_ref)
    bias_ref[...] = jnp.zeros_like(bias_ref)

    def side_grads(side):
        pieces = [dq_low[h, side] for h in range(HALF_HEADS)]
        pieces += [dk_low[h, side] for h in range(HALF_HEADS)]
        pieces += [dv_low[h, side] for h in range(HALF_HEADS)]
        joined = jnp.concatenate(pieces, axis=1)
        gw_ref[...] += dot_tn(joined, xin_ref[side])
        bias_ref[...] += dot(jnp.ones((8, half), BF), joined)
        return dot(joined, w_ref[...])

    outgoing[...] = side_grads(1 - core)
    copy = remote(outgoing, incoming, sems.at[0], sems.at[1], other_core())
    copy.start()
    own = side_grads(core)
    copy.wait()
    grad_in = own + incoming[...]
    normed, inverse = normalize(tok_ref[...].astype(F32))
    scale = 1.0 + mod_ref[1:2, :]
    grad_ref[...] = mid_ref[...] + norm_back(grad_in * scale, normed, inverse)
    sums_ref[0:1, :] = jnp.sum(grad_in, axis=0, keepdims=True)
    sums_ref[1:2, :] = jnp.sum(grad_in * normed, axis=0, keepdims=True)


def attention_backward(dctx, xin, q, k, v, ctx, lse, weight, tok, mid, mod_rows):
    half = tok.shape[0]
    full = 2 * half
    shape = jax.ShapeDtypeStruct
    return pl.pallas_call(
        backward_kernel,
        out_shape=[
            shape((half, D), F32),
            shape((3 * HALF, D), F32),
            shape((8, D), F32),
            shape((8, 3 * HALF), F32),
        ],
        in_specs=[VM] * 11,
        out_specs=[VM] * 4,
        scratch_shapes=[
            pltpu.VMEM((HEAD_DIM, full), BF),
            pltpu.VMEM((full, HEAD_DIM), BF),
            pltpu.VMEM((full, HEAD_DIM), F32),
            pltpu.VMEM((full, HEAD_DIM), F32),
            pltpu.VMEM((HALF_HEADS, 2, half, HEAD_DIM), BF),
            pltpu.VMEM((HALF_HEADS, 2, half, HEAD_DIM), BF),
            pltpu.VMEM((HALF_HEADS, 2, half, HEAD_DIM), BF),
            pltpu.VMEM((half, D), F32),
            pltpu.VMEM((half, D), F32),
            pltpu.SemaphoreType.DMA((2,)),
        ],
        compiler_params=params(3),
        name="attend_backward",
    )(dctx, xin, q, k, v, ctx, lse, weight, tok, mid, mod_rows)


def scatter_kernel(nbits, g_ref, o_ref, first, *rest):
    stages = rest[:nbits]
    total, send, recv = rest[nbits:]
    me = lax.axis_index("shard")
    core = lax.axis_index("ctx")
    signal_cube(me, nbits)
    lead = (slice(None),) * nbits
    up, other = orders(nbits)
    for which, order in enumerate((up, other)):

        @pl.when(core == which)
        def _():
            copy = remote(
                g_ref.at[lead + (1 - which,)], first, send.at[0], recv.at[0], other_core()
            )
            copy.start()
            copy.wait()
            total[...] = g_ref[lead + (which,)] + first[...]
            for step, bit in enumerate(order):
                free = order[step + 1 :]
                there = flip(me, bit)
                copy = remote(
                    total.at[cube_index(there, nbits, free)],
                    stages[step],
                    send.at[step + 1],
                    recv.at[step + 1],
                    {"shard": there},
                )
                copy.start()
                copy.wait()
                total[cube_index(me, nbits, free)] += stages[step][...]
            o_ref[which] = total[cube_index(me, nbits, ())]
            copy = remote(
                o_ref.at[which],
                o_ref.at[which],
                send.at[nbits + 1],
                recv.at[nbits + 1],
                other_core(),
            )
            copy.start()
            copy.wait()


def reduce_scatter(grads):
    count, rows, width = grads.shape
    nbits = count.bit_length() - 1
    half = rows // 2
    out = pl.pallas_call(
        functools.partial(scatter_kernel, nbits),
        out_shape=jax.ShapeDtypeStruct((2, half, width), F32),
        in_specs=[VM],
        out_specs=VM,
        scratch_shapes=[pltpu.VMEM((2,) * nbits + (half, width), F32)]
        + [pltpu.VMEM((2,) * (nbits - 1 - k) + (half, width), F32) for k in range(nbits)]
        + [pltpu.VMEM((2,) * nbits + (half, width), F32)]
        + [pltpu.SemaphoreType.DMA((nbits + 2,))] * 2,
        compiler_params=params(4),
        name="scatter",
    )(grads.reshape((2,) * nbits + (2, half, width)))
    return out.reshape(rows, width)


def modulate_kernel(
    count,
    mine_ref,
    small_ref,
    wmod_ref,
    grad_ref,
    cond_ref,
    got,
    theirs,
    back_send,
    back,
    send,
    recv,
    bsend,
    brecv,
    csem,
):
    me = lax.axis_index("shard")
    signal_all(me, count)
    got[me] = mine_ref[me]
    copies = []
    for step in range(1, count):
        to = lax.rem(me + step, count)
        copy = remote(mine_ref.at[to], got.at[me], send.at[step], recv.at[step], {"shard": to})
        copy.start()
        copies.append(copy)
    for copy in copies:
        copy.wait()
    swap = remote(got, theirs, csem.at[0], csem.at[1], other_core())
    swap.start()
    swap.wait()
    grad_mod = got[:, 0, :] + theirs[:, 0, :]
    cond = small_ref[:, 0, :]
    silu_low = silu_of(cond).astype(BF)
    grad_ref[...] = lax.dot_general(
        silu_low.astype(F32),
        grad_mod,
        (((0,), (0,)), ((), ())),
        precision=precise,
        preferred_element_type=F32,
    )
    part = lax.dot_general(
        grad_mod,
        wmod_ref[...].astype(F32),
        (((1,), (1,)), ((), ())),
        precision=precise,
        preferred_element_type=F32,
    )
    for row in range(count):
        back_send[row] = jnp.broadcast_to(part[row : row + 1, :], (8, D))
    back[me] = back_send[me]
    copies = []
    for step in range(1, count):
        to = lax.rem(me + step, count)
        copy = remote(
            back_send.at[to], back.at[me], bsend.at[step], brecv.at[step], {"shard": to}
        )
        copy.start()
        copies.append(copy)
    for copy in copies:
        copy.wait()
    grad_silu = jnp.sum(back[...], axis=0)
    own = small_ref[me]
    gate = jax.nn.sigmoid(own)
    cond_ref[...] = grad_silu * (gate + own * gate * (1.0 - gate))


def modulate_grads(mine, small_all, wmod):
    count, _, width = mine.shape
    sems = pltpu.SemaphoreType.DMA((count,))
    return pl.pallas_call(
        functools.partial(modulate_kernel, count),
        out_shape=[
            jax.ShapeDtypeStruct((D, width), F32),
            jax.ShapeDtypeStruct((8, D), F32),
        ],
        in_specs=[VM] * 3,
        out_specs=[VM] * 2,
        scratch_shapes=[
            pltpu.VMEM((count, 8, width), F32),
            pltpu.VMEM((count, 8, width), F32),
            pltpu.VMEM((count, 8, D), F32),
            pltpu.VMEM((count, 8, D), F32),
            sems,
            sems,
            sems,
            sems,
            pltpu.SemaphoreType.DMA((2,)),
        ],
        compiler_params=params(5),
        name="modulate_grads",
    )(mine, small_all, wmod)


def newton_factors(grams, eye):
    grams = list(grams)
    factors = [None] * len(grams)
    for sweep in range(NS_ITERS):
        squares = [dot_three(gram, gram) for gram in grams]
        steps = [
            newton_a * eye + newton_b * gram + newton_c * square
            for gram, square in zip(grams, squares)
        ]
        if sweep < NS_ITERS - 1:
            lefts = [dot_three(step, gram) for step, gram in zip(steps, grams)]
            grams = [dot_three(left, step) for left, step in zip(lefts, steps)]
        factors = [
            step if factor is None else dot_three(step, factor)
            for step, factor in zip(steps, factors)
        ]
    return factors


TAKES = ((0, 1, 2), (3, 4))
SLOTS = 3


def newton_kernel(nbits, sbits, *refs):
    moments, outs = refs[:5], refs[5:10]
    total, stages = refs[10], refs[11 : 11 + nbits]
    gathered, factors, send, recv, gsend, grecv, fsem = refs[11 + nbits :]
    me = lax.axis_index("shard")
    core = lax.axis_index("ctx")
    signal_cube(me, nbits)
    rows = SLOTS * D // (1 << sbits)
    lead = (2,) * sbits

    def gram_of(matrix):
        return lax.dot_general(
            matrix,
            matrix,
            (((1,), (1,)), ((), ())),
            precision=precise,
            preferred_element_type=F32,
        )

    for which in range(2):

        @pl.when(core == which)
        def _():
            grams = [gram_of(moments[index][...]) for index in TAKES[which]]
            while len(grams) < SLOTS:
                grams.append(jnp.zeros((D, D), F32))
            stacked = jnp.concatenate(grams, axis=0)
            total[...] = stacked.reshape(lead + (rows, D))
            up, other = orders(sbits)
            order = (up, other)[which]
            for step, bit in enumerate(order):
                free = order[step + 1 :]
                there = flip(me, bit)
                copy = remote(
                    total.at[cube_index(there, sbits, free)],
                    stages[step],
                    send.at[step],
                    recv.at[step],
                    {"shard": there},
                )
                copy.start()
                copy.wait()
                total[cube_index(me, sbits, free)] += stages[step][...]
            for bit in range(sbits, nbits):
                copy = remote(
                    total.at[cube_index(me, sbits, ())],
                    stages[bit],
                    send.at[bit],
                    recv.at[bit],
                    {"shard": flip(me, bit)},
                )
                copy.start()
                copy.wait()
                total[cube_index(me, sbits, ())] += stages[bit][...]
            gathered[cube_index(me, sbits, ())] = total[cube_index(me, sbits, ())]
            seq = order[::-1]
            for step, bit in enumerate(seq):
                part = gathered.at[cube_index(me, sbits, seq[:step])]
                copy = remote(part, part, gsend.at[step], grecv.at[step], {"shard": flip(me, bit)})
                copy.start()
                copy.wait()
            whole = gathered[...].reshape(SLOTS, D, D)
            row = lax.broadcasted_iota(jnp.int32, (D, D), 0)
            column = lax.broadcasted_iota(jnp.int32, (D, D), 1)
            eye = (row == column).astype(F32)
            scaled = []
            sizes = []
            for slot in range(len(TAKES[which])):
                gram = whole[slot]
                size = jnp.sqrt(jnp.sum(jnp.sum(gram * eye, axis=0, keepdims=True), axis=1, keepdims=True))
                size = 1.0 / (size + 1e-07)
                sizes.append(size)
                scaled.append((gram * size) * size)
            for slot, result in enumerate(newton_factors(scaled, eye)):
                index = TAKES[which][slot]
                factors[index] = result * sizes[slot]
            copies = []
            for index in TAKES[which]:
                copy = remote(
                    factors.at[index],
                    factors.at[index],
                    fsem.at[0, index],
                    fsem.at[1, index],
                    other_core(),
                )
                copy.start()
                copies.append(copy)
            for copy in copies:
                copy.wait_send()
            for index in TAKES[1 - which]:
                remote(
                    factors.at[index],
                    factors.at[index],
                    fsem.at[0, index],
                    fsem.at[1, index],
                    other_core(),
                ).wait_recv()

    for index in range(5):
        outs[index][...] = dot_three(factors[index], moments[index][...])


def newton(moments, count):
    nbits = count.bit_length() - 1
    sbits = min(nbits, 4)
    rows = SLOTS * D // (1 << sbits)
    shapes = [jax.ShapeDtypeStruct(m.shape, F32) for m in moments]
    stages = [
        pltpu.VMEM((2,) * max(sbits - 1 - k, 0) + (rows, D), F32) for k in range(nbits)
    ]
    sems = pltpu.SemaphoreType.DMA
    return pl.pallas_call(
        functools.partial(newton_kernel, nbits, sbits),
        out_shape=shapes,
        in_specs=[VM] * 5,
        out_specs=[VM] * 5,
        scratch_shapes=[pltpu.VMEM((2,) * sbits + (rows, D), F32)]
        + stages
        + [
            pltpu.VMEM((2,) * sbits + (rows, D), F32),
            pltpu.VMEM((5, D, D), F32),
            sems((nbits,)),
            sems((nbits,)),
            sems((sbits,)),
            sems((sbits,)),
            sems((2, 5)),
        ],
        compiler_params=params(6),
        name="newton",
    )(*moments)


def pad_rows(array, rows):
    return jnp.pad(array, ((0, 0),) * (array.ndim - 2) + ((0, rows - array.shape[-2]), (0, 0)))


def on_device(
    tokens,
    condition,
    cotangent,
    modulate_weight,
    attend_weight,
    project_weight,
    expand_weight,
    reduce_weight,
    bias_flat,
    modulate_moment,
    attend_moment,
    project_moment,
    expand_moment,
    reduce_moment,
    bias_moment,
):
    count = lax.axis_size("shard")
    core = lax.axis_index("ctx")
    half = tokens.shape[1]
    full = half * lax.axis_size("ctx")
    local = [w.shape[1] for w in (attend_weight, project_weight, expand_weight, reduce_weight)]
    nbias = bias_flat.shape[0]
    tok = tokens[0]
    own = jnp.concatenate(
        [attend_weight, project_weight, expand_weight, reduce_weight], axis=1
    ).T.astype(BF)
    rows = -(-own.shape[0] // 32) * 32
    own = pad_rows(own, rows)
    bias_low = bias_flat.astype(BF).astype(F32)
    small = jnp.concatenate(
        [condition.astype(F32), jnp.pad(bias_low, (0, D - nbias))[None], jnp.zeros((6, D), F32)]
    )
    wmod = modulate_weight.astype(BF)
    whole, small_all, mod_all, tok_all = gather(own, small, wmod, tok, count)
    bounds = [sum(local[:k]) for k in range(5)]
    attend_turn, project_turn, expand_turn, reduce_turn = (
        whole[:, bounds[k] : bounds[k + 1]].reshape(count * local[k], D) for k in range(4)
    )
    bias_full = small_all[:, 1, :nbias].reshape(-1)
    bias_mod = bias_full[: 6 * D]
    bias_query = bias_full[6 * D : 7 * D]
    bias_value = bias_full[7 * D : 8 * D]
    bias_proj = bias_full[8 * D : 9 * D]
    bias_expand = bias_full[9 * D : 9 * D + FF]
    bias_reduce = bias_full[9 * D + FF :]
    modulation = mod_all[:, 0, :].reshape(-1) + bias_mod
    mod_rows = pad_rows(modulation.reshape(6, D), 8)
    weight_core = lax.dynamic_slice_in_dim(
        attend_turn.reshape(3, HEADS * HEAD_DIM, D), core * HALF, HALF, 1
    ).reshape(3 * HALF, D)
    bias_qkv = jnp.stack([bias_query, jnp.zeros((D,), F32), bias_value])
    bias_cols = jnp.broadcast_to(
        lax.dynamic_slice_in_dim(bias_qkv, core * HALF, HALF, 1).reshape(3 * HALF, 1),
        (3 * HALF, 128),
    )
    xin, q, k, v, ctx_turn, lse, ctx = attention_forward(tok_all, mod_rows, weight_core, bias_cols)
    bias_rows = pad_rows(jnp.stack([bias_proj, bias_reduce]), 8)
    wide_rows = pad_rows(bias_expand[None], 8)
    block_out, mid, gp, ge, gr, sums, wides, dctx = branch(
        ctx,
        tok,
        cotangent[0],
        mod_rows,
        bias_rows,
        wide_rows,
        project_turn,
        expand_turn,
        reduce_turn,
    )
    tokens_grad, gw, sums_one, sums_bias = attention_backward(
        dctx, xin, q, k, v, ctx_turn, lse, weight_core, tok, mid, mod_rows
    )
    ga = lax.dynamic_update_slice_in_dim(
        jnp.zeros((3, HEADS * HEAD_DIM, D), F32), gw.reshape(3, HALF, D), core * HALF, 1
    ).reshape(3 * D, D)
    bias_own = sums_bias[0].reshape(3, HALF)
    bias_att = lax.dynamic_update_slice_in_dim(
        jnp.zeros((3, D), F32), bias_own, core * HALF, 1
    )
    grad_mod = jnp.concatenate(
        [sums_one[0], sums_one[1], sums[3], sums[1], sums[2], sums[0]]
    )
    bias_grad = jnp.concatenate(
        [grad_mod, bias_att[0], bias_att[2], sums[4], wides[0], sums[5]]
    )
    bias_part = pad_rows(
        jnp.pad(bias_grad.reshape(count, 1, nbias), ((0, 0), (0, 0), (0, D - nbias))), 8
    )
    grads = jnp.concatenate(
        [
            g.reshape(count, n, D)
            for g, n in zip((ga, gp, ge, gr), local)
        ]
        + [bias_part],
        axis=1,
    )
    total_rows = -(-grads.shape[1] // 16) * 16
    summed = reduce_scatter(pad_rows(grads, total_rows))
    width = wmod.shape[1]
    mine = jnp.broadcast_to(grad_mod.reshape(count, 1, width), (count, 8, width))
    modulate_raw, condition_rows = modulate_grads(mine, small_all, wmod)
    scale = 1.0 / math.sqrt(tokens.shape[0] * count * full)
    turned = summed.T
    grads = [modulate_raw * scale] + [
        turned[:, bounds[k] : bounds[k + 1]] * scale for k in range(4)
    ]
    bias_out = summed[bounds[4], :nbias] * scale
    old = [modulate_moment, attend_moment, project_moment, expand_moment, reduce_moment]
    moments = [moment_decay * o + g for o, g in zip(old, grads)]
    bias_new = moment_decay * bias_moment + bias_out
    directions = newton(moments, count)
    masters = [modulate_weight, attend_weight, project_weight, expand_weight, reduce_weight]
    new_masters = [
        master - matrix_rate * 0.2 * math.sqrt(max(D, master.shape[1] * count)) * direction
        for master, direction in zip(masters, directions)
    ]
    result = [block_out[None], tokens_grad[None], condition_rows[0:1]]
    for g, w, m in zip(grads, new_masters, moments):
        result += [g, w, m]
    result += [bias_out, bias_flat - bias_rate * bias_new, bias_new]
    return tuple(result)


def solution(mesh):
    tok = P("shard", "ctx", None)
    row = P("shard", None)
    col = P(None, "shard")
    flat = P("shard")
    return jax.shard_map(
        on_device,
        mesh=mesh,
        in_specs=(tok, row, tok) + (col,) * 5 + (flat,) + (col,) * 5 + (flat,),
        out_specs=(tok, tok, row) + (col,) * 15 + (flat,) * 3,
        check_vma=False,
    )
```

```python
import functools
import math

import jax
import jax.numpy as jnp
from jax import lax
from jax.experimental import pallas as pl
from jax.experimental.pallas import tpu as pltpu
from jax.sharding import PartitionSpec as P

D = 384
FF = 1536
HEADS = 6
HEAD_DIM = 64
NS_ITERS = 5
HALF_HEADS = HEADS // 2
HALF = HALF_HEADS * HEAD_DIM

norm_eps = 1e-06
newton_a = 3.4445
newton_b = -4.775
newton_c = 2.0315
moment_decay = 0.95
matrix_rate = 0.5
bias_rate = 0.1
precise = lax.Precision.HIGHEST
LOG2E = 1.4426950408889634

MESH = pl.DeviceIdType.MESH
BF = jnp.bfloat16
F32 = jnp.float32
VMEM_BYTES = 60 * 2**20
VM = pl.BlockSpec(memory_space=pltpu.VMEM)


def params(collective=None):
    if collective is None:
        return pltpu.CompilerParams(vmem_limit_bytes=VMEM_BYTES)
    return pltpu.CompilerParams(
        collective_id=collective, has_side_effects=True, vmem_limit_bytes=VMEM_BYTES
    )


def dot(left, right):
    return jnp.dot(left, right, preferred_element_type=F32)


def dot_nt(left, right):
    return lax.dot_general(left, right, (((1,), (1,)), ((), ())), preferred_element_type=F32)


def dot_tn(left, right):
    return lax.dot_general(left, right, (((0,), (0,)), ((), ())), preferred_element_type=F32)


def split_low(values):
    high = values.astype(BF)
    return high, (values - high.astype(F32)).astype(BF)


def dot_three(left, right, op=dot):
    left_high, left_low = split_low(left)
    right_high, right_low = split_low(right)
    return op(left_high, right_high) + (op(left_high, right_low) + op(left_low, right_high))


def silu_of(values):
    return values * jax.nn.sigmoid(values)


def normalize(values):
    centered = values - jnp.mean(values, axis=-1, keepdims=True)
    inverse = lax.rsqrt(jnp.mean(centered * centered, axis=-1, keepdims=True) + norm_eps)
    return (centered * inverse, inverse)


def norm_back(grad_normed, normed, inverse):
    first = jnp.mean(grad_normed, axis=-1, keepdims=True)
    second = jnp.mean(grad_normed * normed, axis=-1, keepdims=True)
    return (grad_normed - first - normed * second) * inverse


def bit_of(value, bit):
    return lax.rem(value // (1 << bit), 2)


def flip(me, bit):
    return me + (1 - 2 * bit_of(me, bit)) * (1 << bit)


def other_core():
    return {"ctx": 1 - lax.axis_index("ctx")}


def signal_cube(me, nbits):
    sem = pltpu.get_barrier_semaphore()
    for bit in range(nbits):
        pl.semaphore_signal(
            sem, inc=1, device_id={"shard": flip(me, bit)}, device_id_type=MESH
        )
    pl.semaphore_signal(sem, inc=1, device_id=other_core(), device_id_type=MESH)
    pl.semaphore_wait(sem, nbits + 1)


def signal_all(me, count):
    sem = pltpu.get_barrier_semaphore()
    for step in range(1, count):
        pl.semaphore_signal(
            sem, inc=1, device_id={"shard": lax.rem(me + step, count)}, device_id_type=MESH
        )
    pl.semaphore_signal(sem, inc=1, device_id=other_core(), device_id_type=MESH)
    pl.semaphore_wait(sem, count)


def signal_core():
    sem = pltpu.get_barrier_semaphore()
    pl.semaphore_signal(sem, inc=1, device_id=other_core(), device_id_type=MESH)
    pl.semaphore_wait(sem, 1)


def remote(src, dst, send, recv, where):
    return pltpu.make_async_remote_copy(
        src, dst, send, recv, device_id=where, device_id_type=MESH
    )


def orders(nbits):
    up = list(range(nbits))
    return up, ([1, 0] + up[2:] if nbits >= 2 else up)


def cube_index(who, nbits, free, tail=()):
    lead = tuple(
        slice(None) if (nbits - 1 - d) in free else bit_of(who, nbits - 1 - d)
        for d in range(nbits)
    )
    return lead + tuple(tail)


def gather_kernel(
    nbits,
    width,
    own_ref,
    small_ref,
    wmod_ref,
    tok_ref,
    whole_ref,
    small_all,
    mod_all,
    tok_all,
    mod_send,
    send,
    recv,
    psend,
    precv,
    ssend,
    srecv,
    msend,
    mrecv,
    tsem,
    lsem,
):
    count = 1 << nbits
    me = lax.axis_index("shard")
    core = lax.axis_index("ctx")
    signal_all(me, count)
    small_all[me] = small_ref[...]
    spread = []
    for step in range(1, count):
        to = lax.rem(me + step, count)
        copy = remote(
            small_ref, small_all.at[me], ssend.at[step], srecv.at[step], {"shard": to}
        )
        copy.start()
        spread.append(copy)
    toks = remote(tok_ref, tok_all.at[core], tsem.at[0], tsem.at[1], other_core())
    toks.start()
    tok_all[core] = tok_ref[...]
    own = cube_index(me, nbits, ())
    local = pltpu.make_async_copy(own_ref, whole_ref.at[own], lsem)
    local.start()
    local.wait()
    up, other = orders(nbits)

    def cube_step(which, step, seq):
        held = seq[:step]
        bit = seq[step]
        part = whole_ref.at[cube_index(me, nbits, held, (which,))]
        return remote(part, part, send.at[step], recv.at[step], {"shard": flip(me, bit)})

    def forward(which, step, seq):
        held = seq[:step]
        bit = seq[step]
        part = whole_ref.at[cube_index(flip(me, bit), nbits, held, (which,))]
        return remote(part, part, psend.at[step], precv.at[step], other_core())

    for which, order in enumerate((up, other)):

        @pl.when(core == which)
        def _():
            cube_step(which, 0, order[::-1]).start()

    for copy in spread:
        copy.wait()
    cond = small_all[:, 0, :]
    silu_low = silu_of(cond).astype(BF)
    part = dot_nt(silu_low, wmod_ref[...])
    for row in range(count):
        mod_send[row] = jnp.broadcast_to(part[row : row + 1, :], (8, width))
    mod_all[me] = mod_send[me]
    mods = []
    for step in range(1, count):
        to = lax.rem(me + step, count)
        copy = remote(mod_send.at[to], mod_all.at[me], msend.at[step], mrecv.at[step], {"shard": to})
        copy.start()
        mods.append(copy)
    for which, order in enumerate((up, other)):

        @pl.when(core == which)
        def _():
            seq = order[::-1]
            for step in range(nbits):
                now = cube_step(which, step, seq)
                if step > 0:
                    now.start()
                now.wait()
                forward(which, step, seq).start()
            for step in range(nbits):
                forward(which, step, seq).wait_send()
            back = (other if which == 0 else up)[::-1]
            for step in range(nbits):
                forward(1 - which, step, back).wait_recv()

    for copy in mods:
        copy.wait()
    toks.wait()


def gather(own, small, wmod, tok, count):
    nbits = count.bit_length() - 1
    rows = own.shape[0]
    half = rows // 2
    width = wmod.shape[0]
    sems = lambda n: pltpu.SemaphoreType.DMA((n,))
    whole, small_all, mod_all, tok_all = pl.pallas_call(
        functools.partial(gather_kernel, nbits, width),
        out_shape=[
            jax.ShapeDtypeStruct((2,) * nbits + (2, half, D), BF),
            jax.ShapeDtypeStruct((count, 8, D), F32),
            jax.ShapeDtypeStruct((count, 8, width), F32),
            jax.ShapeDtypeStruct((2,) + tok.shape, BF),
        ],
        in_specs=[VM] * 4,
        out_specs=[VM] * 4,
        scratch_shapes=[
            pltpu.VMEM((count, 8, width), F32),
            sems(nbits),
            sems(nbits),
            sems(nbits),
            sems(nbits),
            sems(count),
            sems(count),
            sems(count),
            sems(count),
            sems(2),
            pltpu.SemaphoreType.DMA,
        ],
        compiler_params=params(0),
        name="gather",
    )(own.reshape(2, half, D), small, wmod, tok)
    return whole.reshape(count, rows, D), small_all, mod_all, tok_all


def forward_kernel(
    tok_ref,
    mod_ref,
    w_ref,
    bias_ref,
    xin_ref,
    q_ref,
    k_ref,
    v_ref,
    ctx_ref,
    lse_ref,
    both_ref,
    cols,
    outgoing,
    sems,
):
    core = lax.axis_index("ctx")
    signal_core()
    half = tok_ref.shape[1]
    shift = mod_ref[0:1, :]
    scale = 1.0 + mod_ref[1:2, :]
    block = 256

    def norm_block(index, _):
        rows = pl.ds(pl.multiple_of(index * block, block), block)
        for side in range(2):
            normed, _inverse = normalize(tok_ref[side, rows, :].astype(F32))
            xin_ref[side, rows, :] = (normed * scale + shift).astype(BF)
        return 0

    lax.fori_loop(0, half // block, norm_block, 0)
    for side in range(2):
        xin = xin_ref[side]
        rows = pl.ds(side * half, half)
        query = dot_nt(w_ref[0:HALF, :], xin) + bias_ref[0:HALF, 0:1]
        value = dot_nt(w_ref[2 * HALF :, :], xin) + bias_ref[2 * HALF :, 0:1]
        query = query.astype(BF) * jnp.asarray(HEAD_DIM**-0.5, BF)
        value = value.astype(BF)
        for head in range(HALF_HEADS):
            part = slice(head * HEAD_DIM, (head + 1) * HEAD_DIM)
            q_ref[head, side] = query[part, :]
            v_ref[head, :, rows] = value[part, :]
            k_ref[head, rows, :] = dot_nt(
                xin, w_ref[HALF + head * HEAD_DIM : HALF + (head + 1) * HEAD_DIM, :]
            ).astype(BF)

    def attend(step, _):
        head = step // 2
        side = lax.rem(step, 2)
        scores = dot(k_ref[head], q_ref[head, side])
        top = jnp.max(scores, axis=0, keepdims=True)
        shifted = jnp.exp2((scores - top) * LOG2E)
        total = jnp.sum(shifted, axis=0, keepdims=True)
        probs = (shifted * (1.0 / total)).astype(BF)
        out = dot(v_ref[head], probs)
        ctx_ref[head, side] = out
        lse_ref[head, side] = jnp.broadcast_to(top * LOG2E + jnp.log2(total), (8, half))
        cols[side, pl.ds(pl.multiple_of(head * HEAD_DIM, HEAD_DIM), HEAD_DIM), :] = out
        return 0

    lax.fori_loop(0, 2 * HALF_HEADS, attend, 0)
    outgoing[...] = jnp.transpose(cols[1 - core]).astype(BF)
    copy = remote(outgoing, both_ref.at[core], sems.at[0], sems.at[1], other_core())
    copy.start()
    both_ref[core] = jnp.transpose(cols[core]).astype(BF)
    copy.wait()


def attention_forward(tok_all, mod_rows, weight, bias_cols):
    half = tok_all.shape[1]
    full = 2 * half
    shape = jax.ShapeDtypeStruct
    return pl.pallas_call(
        forward_kernel,
        out_shape=[
            shape((2, half, D), BF),
            shape((HALF_HEADS, 2, HEAD_DIM, half), BF),
            shape((HALF_HEADS, full, HEAD_DIM), BF),
            shape((HALF_HEADS, HEAD_DIM, full), BF),
            shape((HALF_HEADS, 2, HEAD_DIM, half), F32),
            shape((HALF_HEADS, 2, 8, half), F32),
            shape((2, half, HALF), BF),
        ],
        in_specs=[VM] * 4,
        out_specs=[VM] * 7,
        scratch_shapes=[
            pltpu.VMEM((2, HALF, half), F32),
            pltpu.VMEM((half, HALF), BF),
            pltpu.SemaphoreType.DMA((2,)),
        ],
        compiler_params=params(1),
        name="attend_forward",
    )(tok_all, mod_rows, weight, bias_cols)


def branch_kernel(
    ctx_ref,
    tok_ref,
    cot_ref,
    mod_ref,
    bias_ref,
    wide_ref,
    wp_ref,
    we_ref,
    wr_ref,
    out_ref,
    mid_ref,
    gp_ref,
    ge_ref,
    gr_ref,
    sums_ref,
    wides_ref,
    both_ref,
    outgoing,
    sems,
):
    core = lax.axis_index("ctx")
    signal_core()
    half = tok_ref.shape[0]
    block = 256
    gate_one = mod_ref[2:3, :]
    shift_two = mod_ref[3:4, :]
    scale_two = 1.0 + mod_ref[4:5, :]
    gate_two = mod_ref[5:6, :]
    gp_ref[...] = jnp.zeros_like(gp_ref)
    ge_ref[...] = jnp.zeros_like(ge_ref)
    gr_ref[...] = jnp.zeros_like(gr_ref)
    sums_ref[...] = jnp.zeros_like(sums_ref)
    wides_ref[...] = jnp.zeros_like(wides_ref)

    def step(index, _):
        rows = pl.ds(pl.multiple_of(index * block, block), block)
        ctx = jnp.concatenate([ctx_ref[0, rows, :], ctx_ref[1, rows, :]], axis=1)
        attended = dot_nt(ctx, wp_ref[...]) + bias_ref[0:1, :]
        middle = tok_ref[rows, :].astype(F32) + gate_one * attended
        normed, inverse = normalize(middle)
        expand_in = (normed * scale_two + shift_two).astype(BF)
        hidden = dot_nt(expand_in, we_ref[...]) + wide_ref[0:1, :]
        squared = hidden * hidden
        bend = jnp.tanh(0.7978845608028654 * (hidden + 0.044715 * squared * hidden))
        rise = 0.5 * (1.0 + bend)
        act = (hidden * rise).astype(BF)
        slope = rise + 0.5 * hidden * (1.0 - bend * bend) * (
            0.7978845608028654 * (1.0 + 3.0 * 0.044715 * squared)
        )
        mlp_out = dot(act, wr_ref[...]) + bias_ref[1:2, :]
        out_ref[rows, :] = (middle + gate_two * mlp_out).astype(BF)
        grad_out = cot_ref[rows, :].astype(F32)
        grad_mlp = (gate_two * grad_out).astype(BF)
        gr_ref[...] += dot_tn(act, grad_mlp)
        grad_hidden = (dot_nt(grad_mlp, wr_ref[...]) * slope).astype(BF)
        ge_ref[...] += dot_tn(grad_hidden, expand_in)
        grad_in = dot(grad_hidden, we_ref[...])
        grad_middle = grad_out + norm_back(grad_in * scale_two, normed, inverse)
        mid_ref[rows, :] = grad_middle
        grad_attended = (gate_one * grad_middle).astype(BF)
        gp_ref[...] += dot_tn(grad_attended, ctx)
        back = dot(grad_attended, wp_ref[...]).astype(BF)
        first, second = back[:, :HALF], back[:, HALF:]
        both_ref[core, rows, :] = jnp.where(core == 0, first, second)
        outgoing[rows, :] = jnp.where(core == 0, second, first)
        add = lambda value: jnp.sum(value, axis=0, keepdims=True)
        sums_ref[0:1, :] += add(grad_out * mlp_out)
        sums_ref[1:2, :] += add(grad_in)
        sums_ref[2:3, :] += add(grad_in * normed)
        sums_ref[3:4, :] += add(grad_middle * attended)
        sums_ref[4:5, :] += add(grad_attended.astype(F32))
        sums_ref[5:6, :] += add(grad_mlp.astype(F32))
        wides_ref[0:1, :] += add(grad_hidden.astype(F32))
        return 0

    lax.fori_loop(0, half // block, step, 0)
    copy = remote(outgoing, both_ref.at[core], sems.at[0], sems.at[1], other_core())
    copy.start()
    copy.wait()


def branch(ctx, tok, cot, mod_rows, bias_rows, wide_rows, wp, we, wr):
    half = tok.shape[0]
    shape = jax.ShapeDtypeStruct
    return pl.pallas_call(
        branch_kernel,
        out_shape=[
            shape((half, D), BF),
            shape((half, D), F32),
            shape((D, D), F32),
            shape((FF, D), F32),
            shape((FF, D), F32),
            shape((8, D), F32),
            shape((8, FF), F32),
            shape((2, half, HALF), BF),
        ],
        in_specs=[VM] * 9,
        out_specs=[VM] * 8,
        scratch_shapes=[pltpu.VMEM((half, HALF), BF), pltpu.SemaphoreType.DMA((2,))],
        compiler_params=params(2),
        name="branch",
    )(ctx, tok, cot, mod_rows, bias_rows, wide_rows, wp, we, wr)


def backward_kernel(
    nbits,
    dctx_ref,
    xin_ref,
    q_ref,
    k_ref,
    v_ref,
    ctx_ref,
    lse_ref,
    w_ref,
    tok_ref,
    mid_ref,
    mod_ref,
    gp_ref,
    ge_ref,
    gr_ref,
    grad_ref,
    att_ref,
    sums_ref,
    bias_ref,
    own_ref,
    *rest,
):
    stages = rest[:nbits]
    (
        first,
        total,
        k_turn,
        v_rows,
        dk_sum,
        dv_sum,
        dq_low,
        dk_low,
        dv_low,
        gw,
        outgoing,
        incoming,
        sems,
        asems,
        send,
        recv,
    ) = rest[nbits:]
    me = lax.axis_index("shard")
    core = lax.axis_index("ctx")
    signal_cube(me, nbits)
    half = tok_ref.shape[0]
    lead = (slice(None),) * nbits
    wide = ge_ref.shape[-2]
    both = wide + gp_ref.shape[-2]
    last = nbits + 1
    main = lead + (slice(0, wide),)
    side_rows = lead + (slice(wide, both),)
    spots = {1: 0, 2: 2, 3: 3, 4: 4}

    def swap_main(which):
        return remote(
            (gr_ref, ge_ref)[which], first.at[main], send.at[0], recv.at[0], other_core()
        )

    swap_side = remote(gp_ref, first.at[side_rows], send.at[last], recv.at[last], other_core())

    def cube_step(which, step):
        order = orders(nbits)[which]
        rows = slice(0, both if which == 0 else wide)
        bit = order[step]
        free = order[step + 1 :]
        there = flip(me, bit)
        return remote(
            total.at[cube_index(there, nbits, free, (rows,))],
            stages[step].at[(slice(None),) * len(free) + (rows,)],
            send.at[step + 1],
            recv.at[step + 1],
            {"shard": there},
        )

    def last_swap(which):
        rows = slice(0, both if which == 0 else wide)
        return remote(
            own_ref.at[which, rows],
            own_ref.at[which, rows],
            send.at[nbits + 2],
            recv.at[nbits + 2],
            other_core(),
        )

    def progress(point):
        for which in range(2):

            @pl.when(core == which)
            def _():
                rows = slice(0, both if which == 0 else wide)
                order = orders(nbits)[which]
                if point == 0:
                    swap_main(which).start()
                    if which == 1:
                        swap_side.start()
                elif point == 1:
                    swap_main(which).wait()
                    if which == 0:
                        swap_side.wait_recv()
                        total[main] = ge_ref[...] + first[main]
                        total[side_rows] = gp_ref[...] + first[side_rows]
                    else:
                        swap_side.wait_send()
                        total[main] = gr_ref[...] + first[main]
                elif point <= nbits + 1:
                    step = point - 2
                    cube_step(which, step).wait()
                    free = order[step + 1 :]
                    total[cube_index(me, nbits, free, (rows,))] += stages[step][
                        (slice(None),) * len(free) + (rows,)
                    ]
                if 1 <= point <= nbits:
                    cube_step(which, point - 1).start()
                if point == nbits + 1:
                    own_ref[which, rows] = total[cube_index(me, nbits, (), (rows,))]
                    last_swap(which).start()
                if point == nbits + 2:
                    last_swap(which).wait_send()
                    last_swap(1 - which).wait_recv()

    turn = lambda value: jnp.transpose(value.astype(F32)).astype(BF)
    progress(0)
    for head in range(HALF_HEADS):
        k_turn[...] = turn(k_ref[head])
        v_rows[...] = turn(v_ref[head])
        dk_sum[...] = jnp.zeros_like(dk_sum)
        dv_sum[...] = jnp.zeros_like(dv_sum)

        def step(side, _):
            query = q_ref[head, side]
            down = dctx_ref[side, :, head * HEAD_DIM : (head + 1) * HEAD_DIM]
            down_turn = jnp.transpose(down.astype(F32))
            delta = jnp.sum(down_turn * ctx_ref[head, side], axis=0, keepdims=True)
            scores = dot(k_ref[head], query)
            probs = jnp.exp2(scores * LOG2E - lse_ref[head, side, 0:1, :])
            dv_sum[...] += dot(probs.astype(BF), down)
            grad_probs = dot(v_rows[...], down_turn.astype(BF))
            grad_scores = (probs * (grad_probs - delta)).astype(BF)
            dk_sum[...] += dot(grad_scores, turn(query))
            dq_low[head, side] = (
                jnp.transpose(dot(k_turn[...], grad_scores)) * (HEAD_DIM**-0.5)
            ).astype(BF)
            for at in range(2):
                for point in range(1, nbits + 2):
                    if spots.get(point, 5) == head * 2 + at:
                        pl.when(side == at)(functools.partial(progress, point))
            return 0

        lax.fori_loop(0, 2, step, 0)
        dk_low[head] = dk_sum[...].reshape(2, half, HEAD_DIM).astype(BF)
        dv_low[head] = dv_sum[...].reshape(2, half, HEAD_DIM).astype(BF)

    def side_grads(side, fresh):
        pieces = [dq_low[h, side] for h in range(HALF_HEADS)]
        pieces += [dk_low[h, side] for h in range(HALF_HEADS)]
        pieces += [dv_low[h, side] for h in range(HALF_HEADS)]
        joined = jnp.concatenate(pieces, axis=1)
        grad = dot_tn(joined, xin_ref[side])
        sums = dot(jnp.ones((8, half), BF), joined)
        gw[...] = grad if fresh else gw[...] + grad
        bias_ref[...] = sums if fresh else bias_ref[...] + sums
        return dot(joined, w_ref[...])

    outgoing[...] = side_grads(1 - core, True)
    copy = remote(outgoing, incoming, sems.at[0], sems.at[1], other_core())
    copy.start()
    own = side_grads(core, False)

    def share(which):
        return [
            remote(
                att_ref.at[pl.ds(block * D + which * HALF, HALF), :],
                att_ref.at[pl.ds(block * D + which * HALF, HALF), :],
                asems.at[0, block],
                asems.at[1, block],
                other_core(),
            )
            for block in range(3)
        ]

    for which in range(2):

        @pl.when(core == which)
        def _():
            for block in range(3):
                att_ref[block * D + which * HALF : block * D + (which + 1) * HALF, :] = gw[
                    block * HALF : (block + 1) * HALF, :
                ]
            for part in share(which):
                part.start()

    copy.wait()
    grad_in = own + incoming[...]
    normed, inverse = normalize(tok_ref[...].astype(F32))
    scale = 1.0 + mod_ref[1:2, :]
    grad_ref[...] = mid_ref[...] + norm_back(grad_in * scale, normed, inverse)
    sums_ref[0:1, :] = jnp.sum(grad_in, axis=0, keepdims=True)
    sums_ref[1:2, :] = jnp.sum(grad_in * normed, axis=0, keepdims=True)
    for which in range(2):

        @pl.when(core == which)
        def _():
            for part in share(which):
                part.wait_send()
            for part in share(1 - which):
                part.wait_recv()

    progress(nbits + 2)


def attention_backward(dctx, xin, q, k, v, ctx, lse, weight, tok, mid, mod_rows, gp, ge, gr):
    half = tok.shape[0]
    full = 2 * half
    count, wide, _ = ge.shape
    both = wide + gp.shape[1]
    nbits = count.bit_length() - 1
    lead = (2,) * nbits
    shape = jax.ShapeDtypeStruct
    sems = pltpu.SemaphoreType.DMA
    return pl.pallas_call(
        functools.partial(backward_kernel, nbits),
        out_shape=[
            shape((half, D), F32),
            shape((3 * D, D), F32),
            shape((8, D), F32),
            shape((8, 3 * HALF), F32),
            shape((2, both, D), F32),
        ],
        in_specs=[VM] * 14,
        out_specs=[VM] * 5,
        scratch_shapes=[pltpu.VMEM((2,) * (nbits - 1 - k) + (both, D), F32) for k in range(nbits)]
        + [
            pltpu.VMEM(lead + (both, D), F32),
            pltpu.VMEM(lead + (both, D), F32),
            pltpu.VMEM((HEAD_DIM, full), BF),
            pltpu.VMEM((full, HEAD_DIM), BF),
            pltpu.VMEM((full, HEAD_DIM), F32),
            pltpu.VMEM((full, HEAD_DIM), F32),
            pltpu.VMEM((HALF_HEADS, 2, half, HEAD_DIM), BF),
            pltpu.VMEM((HALF_HEADS, 2, half, HEAD_DIM), BF),
            pltpu.VMEM((HALF_HEADS, 2, half, HEAD_DIM), BF),
            pltpu.VMEM((3 * HALF, D), F32),
            pltpu.VMEM((half, D), F32),
            pltpu.VMEM((half, D), F32),
            sems((2,)),
            sems((2, 3)),
            sems((nbits + 3,)),
            sems((nbits + 3,)),
        ],
        compiler_params=params(3),
        name="attend_backward",
    )(
        dctx,
        xin,
        q,
        k,
        v,
        ctx,
        lse,
        weight,
        tok,
        mid,
        mod_rows,
        gp.reshape(lead + gp.shape[1:]),
        ge.reshape(lead + ge.shape[1:]),
        gr.reshape(lead + gr.shape[1:]),
    )


def newton_factor(gram, eye):
    factor = None
    for sweep in range(NS_ITERS):
        square = dot_three(gram, gram)
        step = newton_a * eye + newton_b * gram + newton_c * square
        if sweep < NS_ITERS - 1:
            gram = dot_three(dot_three(step, gram), step)
        factor = step if factor is None else dot_three(step, factor)
    return factor


def gram_of(turned):
    return lax.dot_general(
        turned,
        turned,
        (((0,), (0,)), ((), ())),
        precision=precise,
        preferred_element_type=F32,
    )


TILE = 128


def pack_gram(gram):
    tile = lambda r, c: gram[r * TILE : (r + 1) * TILE, c * TILE : (c + 1) * TILE]
    upper = jnp.concatenate([tile(0, 0), tile(1, 1), tile(2, 2)], axis=1)
    lower = jnp.concatenate([tile(1, 0), tile(2, 0), tile(2, 1)], axis=1)
    return upper, lower


def unpack_gram(upper, lower):
    tile = lambda packed, c: packed[:, c * TILE : (c + 1) * TILE]
    one, two, three = (tile(lower, c) for c in range(3))
    return jnp.concatenate(
        [
            jnp.concatenate([tile(upper, 0), one.T, two.T], axis=1),
            jnp.concatenate([one, tile(upper, 1), three.T], axis=1),
            jnp.concatenate([two, three, tile(upper, 2)], axis=1),
        ],
        axis=0,
    )


class Sum:
    def __init__(self, count, source, landed, whole, extra, send, recv, gsend, grecv, hsend, hrecv):
        self.pieces = source.shape[0]
        self.high = [b for b in range(count.bit_length() - 1) if (1 << b) >= self.pieces]
        self.source, self.landed, self.whole, self.extra = source, landed, whole, extra
        self.sems = send, recv, gsend, grecv, hsend, hrecv
        self.me = lax.axis_index("shard")
        self.low = lax.rem(self.me, self.pieces)

    def peer(self, step):
        place = lax.rem(self.low + step, self.pieces)
        return place, {"shard": self.me - self.low + place}

    def scatter(self, step):
        place, where = self.peer(step)
        send, recv = self.sems[:2]
        return remote(
            self.source.at[place], self.landed.at[self.low], send.at[step], recv.at[step], where
        )

    def spread(self, step):
        _, where = self.peer(step)
        send, recv = self.sems[2:4]
        part = self.whole.at[self.low]
        return remote(part, part, send.at[step], recv.at[step], where)

    def start(self):
        for step in range(1, self.pieces):
            self.scatter(step).start()
        self.landed[self.low] = self.source[self.low]

    def turn(self):
        for step in range(1, self.pieces):
            self.scatter(step).wait()
        self.whole[self.low] = jnp.sum(self.landed[...], axis=0)
        send, recv = self.sems[4:]
        for at, bit in enumerate(self.high):
            copy = remote(
                self.whole.at[self.low],
                self.extra.at[at],
                send.at[at],
                recv.at[at],
                {"shard": flip(self.me, bit)},
            )
            copy.start()
            copy.wait()
            self.whole[self.low] += self.extra[at]
        for step in range(1, self.pieces):
            self.spread(step).start()

    def finish(self):
        for step in range(1, self.pieces):
            self.spread(step).wait()

    @staticmethod
    def scratch(count, rows):
        pieces = min(count, 16)
        high = max(count.bit_length() - pieces.bit_length(), 1)
        sems = pltpu.SemaphoreType.DMA
        block = pltpu.VMEM((pieces, rows // pieces, D), F32)
        return [block, block, block, pltpu.VMEM((high, rows // pieces, D), F32)] + [
            sems((pieces,))
        ] * 4 + [sems((high,))] * 2


SUM_REFS = 10


def tail_kernel(
    count,
    scale,
    local,
    att_ref,
    own_ref,
    mine_ref,
    small_ref,
    wmod_ref,
    old_mod,
    old_att,
    old_pro,
    old_exp,
    old_red,
    fac_ref,
    rows_ref,
    modg_ref,
    bias_ref,
    cond_ref,
    *rest,
):
    nbits = count.bit_length() - 1
    stages = rest[:nbits]
    total, got, theirs, back_send, back, upper_half, other_half = rest[nbits : nbits + 7]
    send, recv, msend, mrecv, bsend, brecv, csem, fsem = rest[nbits + 7 : nbits + 15]
    sums = rest[nbits + 15 :]
    one = Sum(count, *sums[:SUM_REFS])
    two = Sum(count, *sums[SUM_REFS : 2 * SUM_REFS])
    late = Sum(count, *sums[2 * SUM_REFS :])
    me = lax.axis_index("shard")
    core = lax.axis_index("ctx")
    signal_all(me, count)
    wide = old_exp.shape[0]
    n_att, n_pro = local
    padded = att_ref.shape[-2]
    first_rows = total.shape[-2]

    def rows_of(which):
        return slice(0, first_rows) if which == 0 else slice(0, padded - first_rows)

    def cube_step(which, step):
        order = orders(nbits)[which]
        bit = order[step]
        free = order[step + 1 :]
        there = flip(me, bit)
        rows = rows_of(which)
        source = total.at[cube_index(there, nbits, free, (rows,))]
        return remote(
            source,
            stages[step].at[(slice(None),) * len(free) + (rows,)],
            send.at[step],
            recv.at[step],
            {"shard": there},
        )

    def swap_rows(which):
        part = rows_ref.at[which, rows_of(which)]
        return remote(part, part, csem.at[2], csem.at[3], other_core())

    def progress(point):
        for which in range(2):

            @pl.when(core == which)
            def _():
                rows = rows_of(which)
                lead = (slice(None),) * nbits
                order = orders(nbits)[which]
                if point == 0:
                    begin = 0 if which == 0 else first_rows
                    total[lead + (rows,)] = att_ref[
                        lead + (slice(begin, begin + rows.stop),)
                    ]
                else:
                    step = point - 1
                    cube_step(which, step).wait()
                    free = order[step + 1 :]
                    total[cube_index(me, nbits, free, (rows,))] += stages[step][
                        (slice(None),) * len(free) + (rows,)
                    ]
                if point < nbits:
                    cube_step(which, point).start()
                else:
                    rows_ref[which, rows] = total[cube_index(me, nbits, (), (rows,))]
                    swap_rows(which).start()

    progress(0)
    copies = []
    got[me] = mine_ref[me]
    for step in range(1, count):
        to = lax.rem(me + step, count)
        copy = remote(mine_ref.at[to], got.at[me], msend.at[step], mrecv.at[step], {"shard": to})
        copy.start()
        copies.append(copy)

    def put(target, gram):
        upper, lower = pack_gram(gram)
        packed = jnp.concatenate([upper, lower], axis=0)
        target.source[...] = packed.reshape(target.source.shape)

    old = jnp.where(core == 0, old_exp[...], old_red[...])
    put(one, gram_of(moment_decay * old + own_ref[core, 0:wide, :] * scale))
    one.start()

    for copy in copies:
        copy.wait()
    swap = remote(got, theirs, csem.at[0], csem.at[1], other_core())
    swap.start()
    cond = small_ref[:, 0, :]
    silu_low = silu_of(cond).astype(BF).astype(F32)
    swap.wait()
    width = old_mod.shape[0]
    grad_mod = got[:, 1, 0:width] + theirs[:, 1, 0:width]
    bias_ref[...] = jnp.sum(got[...] + theirs[...], axis=0)
    raw = lax.dot_general(
        grad_mod,
        silu_low,
        (((0,), (0,)), ((), ())),
        precision=precise,
        preferred_element_type=F32,
    )
    modg_ref[...] = raw
    part = jnp.dot(
        grad_mod, wmod_ref[...].astype(F32), precision=precise, preferred_element_type=F32
    )
    for row in range(count):
        back_send[row] = jnp.broadcast_to(part[row : row + 1, :], (8, D))
    back[me] = back_send[me]
    backs = []
    for step in range(1, count):
        to = lax.rem(me + step, count)
        copy = remote(
            back_send.at[to], back.at[me], bsend.at[step], brecv.at[step], {"shard": to}
        )
        copy.start()
        backs.append(copy)

    @pl.when(core == 0)
    def _():
        grad = own_ref[0, wide : wide + n_pro, :] * scale
        put(two, gram_of(moment_decay * old_pro[...] + grad))

    @pl.when(core == 1)
    def _():
        put(two, gram_of(moment_decay * old_mod[...] + modg_ref[...] * scale))

    two.start()
    points = list(range(1, nbits + 1))
    progress(points[0])
    one.turn()
    for copy in backs:
        copy.wait()
    grad_silu = jnp.sum(back[...], axis=0)
    own = small_ref[me]
    gate = jax.nn.sigmoid(own)
    cond_ref[...] = grad_silu * (gate + own * gate * (1.0 - gate))
    for point in points[1:2]:
        progress(point)
    two.turn()
    for point in points[2:]:
        progress(point)

    for which in range(2):

        @pl.when(core == which)
        def _():
            swap_rows(which).wait_send()
            swap_rows(1 - which).wait_recv()

    grad = jnp.concatenate(
        [rows_ref[0], rows_ref[1, 0 : padded - first_rows]], axis=0
    )[0:n_att] * scale
    upper, lower = pack_gram(gram_of(moment_decay * old_att[...] + grad))
    late.source[...] = jnp.where(core == 0, upper, lower).reshape(late.source.shape)
    late.start()

    row = lax.broadcasted_iota(jnp.int32, (D, D), 0)
    column = lax.broadcasted_iota(jnp.int32, (D, D), 1)
    eye = (row == column).astype(F32)

    def solve(gram):
        diagonal = jnp.sum(gram * eye, axis=0, keepdims=True)
        size = 1.0 / (jnp.sqrt(jnp.sum(diagonal, axis=1, keepdims=True)) + 1e-07)
        return newton_factor((gram * size) * size, eye) * size

    def solve_sum(item):
        packed = item.whole[...].reshape(2 * TILE, D)
        return solve(unpack_gram(packed[0:TILE], packed[TILE:]))

    def pass_factor(index, at):
        part = fac_ref.at[index]
        return remote(part, part, fsem.at[0, at], fsem.at[1, at], other_core())

    one.finish()
    place_one, place_two = 3 + core, 2 - 2 * core
    fac_ref[place_one] = solve_sum(one)
    first_pass = pass_factor(place_one, 0)
    first_pass.start()
    late.turn()
    two.finish()
    fac_ref[place_two] = solve_sum(two)
    second_pass = pass_factor(place_two, 1)
    second_pass.start()
    late.finish()
    upper_half[...] = late.whole[...].reshape(TILE, D)
    halves = remote(upper_half, other_half, csem.at[4], csem.at[5], other_core())
    halves.start()
    halves.wait()
    mine_half, their_half = upper_half[...], other_half[...]
    fac_ref[1] = solve(
        unpack_gram(
            jnp.where(core == 0, mine_half, their_half),
            jnp.where(core == 0, their_half, mine_half),
        )
    )
    first_pass.wait()
    second_pass.wait()


def tail(att, own, mine, small_all, wmod, olds, scale, local):
    count, padded, _ = att.shape
    nbits = count.bit_length() - 1
    lead = (2,) * nbits
    first_rows = -(-padded // 16) * 8
    width = wmod.shape[0]
    sems = pltpu.SemaphoreType.DMA
    shape = jax.ShapeDtypeStruct
    return pl.pallas_call(
        functools.partial(tail_kernel, count, scale, local),
        out_shape=[
            shape((5, D, D), F32),
            shape((2, first_rows, D), F32),
            shape((width, D), F32),
            shape((8, D), F32),
            shape((8, D), F32),
        ],
        in_specs=[VM] * 10,
        out_specs=[VM] * 5,
        scratch_shapes=[
            pltpu.VMEM((2,) * (nbits - 1 - k) + (first_rows, D), F32) for k in range(nbits)
        ]
        + [
            pltpu.VMEM(lead + (first_rows, D), F32),
            pltpu.VMEM((count, 8, D), F32),
            pltpu.VMEM((count, 8, D), F32),
            pltpu.VMEM((count, 8, D), F32),
            pltpu.VMEM((count, 8, D), F32),
            pltpu.VMEM((TILE, D), F32),
            pltpu.VMEM((TILE, D), F32),
            sems((nbits,)),
            sems((nbits,)),
            sems((count,)),
            sems((count,)),
            sems((count,)),
            sems((count,)),
            sems((6,)),
            sems((2, 2)),
        ]
        + Sum.scratch(count, 2 * TILE)
        + Sum.scratch(count, 2 * TILE)
        + Sum.scratch(count, TILE),
        compiler_params=params(4),
        name="tail",
    )(att.reshape(lead + (padded, D)), own, mine, small_all, wmod, *olds)


def update_kernel(scale, rates, bounds, *refs):
    fac_ref, att_ref, modg_ref, own_ref, bias_ref = refs[:5]
    olds, masters, old_bias, bias = refs[5:10], refs[10:15], refs[15], refs[16]
    outs = refs[17:]
    n_att, wide, n_pro, nbias = bounds
    first_rows = att_ref.shape[1]
    joined = jnp.concatenate([att_ref[0], att_ref[1]], axis=0)
    grads = [
        modg_ref[...],
        joined[0:n_att],
        own_ref[0, wide : wide + n_pro, :],
        own_ref[0, 0:wide, :],
        own_ref[1, 0:wide, :],
    ]
    for index in range(5):
        grad = grads[index] * scale
        moment = moment_decay * olds[index][...] + grad
        direction = dot_three(moment, fac_ref[index])
        outs[3 * index][...] = grad
        outs[3 * index + 1][...] = masters[index][...] - rates[index] * direction
        outs[3 * index + 2][...] = moment
    grad = bias_ref[0:1, 0:nbias] * scale
    moment = moment_decay * old_bias[...] + grad
    outs[15][...] = grad
    outs[16][...] = bias[...] - bias_rate * moment
    outs[17][...] = moment


def update(fac, att, modg, own, bias_sum, olds, masters, old_bias, bias, scale, count):
    shape = jax.ShapeDtypeStruct
    out = []
    for m in masters:
        out += [shape(m.shape, F32)] * 3
    out += [shape(bias.shape, F32)] * 3
    rates = [matrix_rate * 0.2 * math.sqrt(max(D, m.shape[0] * count)) for m in masters]
    bounds = (olds[1].shape[0], olds[3].shape[0], olds[2].shape[0], bias.shape[1])
    return pl.pallas_call(
        functools.partial(update_kernel, scale, rates, bounds),
        out_shape=out,
        in_specs=[VM] * 17,
        out_specs=[VM] * 18,
        compiler_params=params(),
        name="update",
    )(fac, att, modg, own, bias_sum, *olds, *masters, old_bias, bias)


def pad_rows(array, rows):
    return jnp.pad(array, ((0, 0),) * (array.ndim - 2) + ((0, rows - array.shape[-2]), (0, 0)))


def up_to(value, step):
    return -(-value // step) * step


def on_device(
    tokens,
    condition,
    cotangent,
    modulate_weight,
    attend_weight,
    project_weight,
    expand_weight,
    reduce_weight,
    bias_flat,
    modulate_moment,
    attend_moment,
    project_moment,
    expand_moment,
    reduce_moment,
    bias_moment,
):
    count = lax.axis_size("shard")
    core = lax.axis_index("ctx")
    half = tokens.shape[1]
    full = half * lax.axis_size("ctx")
    local = [w.shape[1] for w in (attend_weight, project_weight, expand_weight, reduce_weight)]
    nbias = bias_flat.shape[0]
    tok = tokens[0]
    own = jnp.concatenate(
        [attend_weight, project_weight, expand_weight, reduce_weight], axis=1
    ).T.astype(BF)
    rows = -(-own.shape[0] // 32) * 32
    own = pad_rows(own, rows)
    bias_low = bias_flat.astype(BF).astype(F32)
    small = jnp.concatenate(
        [condition.astype(F32), jnp.pad(bias_low, (0, D - nbias))[None], jnp.zeros((6, D), F32)]
    )
    wmod = modulate_weight.T.astype(BF)
    whole, small_all, mod_all, tok_all = gather(own, small, wmod, tok, count)
    bounds = [sum(local[:k]) for k in range(5)]
    attend_turn, project_turn, expand_turn, reduce_turn = (
        whole[:, bounds[k] : bounds[k + 1]].reshape(count * local[k], D) for k in range(4)
    )
    bias_full = small_all[:, 1, :nbias].reshape(-1)
    bias_mod = bias_full[: 6 * D]
    bias_query = bias_full[6 * D : 7 * D]
    bias_value = bias_full[7 * D : 8 * D]
    bias_proj = bias_full[8 * D : 9 * D]
    bias_expand = bias_full[9 * D : 9 * D + FF]
    bias_reduce = bias_full[9 * D + FF :]
    modulation = mod_all[:, 0, :].reshape(-1) + bias_mod
    mod_rows = pad_rows(modulation.reshape(6, D), 8)
    weight_core = lax.dynamic_slice_in_dim(
        attend_turn.reshape(3, HEADS * HEAD_DIM, D), core * HALF, HALF, 1
    ).reshape(3 * HALF, D)
    bias_qkv = jnp.stack([bias_query, jnp.zeros((D,), F32), bias_value])
    bias_cols = jnp.broadcast_to(
        lax.dynamic_slice_in_dim(bias_qkv, core * HALF, HALF, 1).reshape(3 * HALF, 1),
        (3 * HALF, 128),
    )
    xin, q, k, v, ctx_turn, lse, ctx = attention_forward(tok_all, mod_rows, weight_core, bias_cols)
    bias_rows = pad_rows(jnp.stack([bias_proj, bias_reduce]), 8)
    wide_rows = pad_rows(bias_expand[None], 8)
    block_out, mid, gp, ge, gr, sums, wides, dctx = branch(
        ctx,
        tok,
        cotangent[0],
        mod_rows,
        bias_rows,
        wide_rows,
        project_turn,
        expand_turn,
        reduce_turn,
    )
    n_att, n_pro, n_wide = local[:3]
    gp = pad_rows(gp.reshape(count, n_pro, D), up_to(n_pro, 8))
    tokens_grad, att, sums_one, sums_bias, mlp_rows = attention_backward(
        dctx,
        xin,
        q,
        k,
        v,
        ctx_turn,
        lse,
        weight_core,
        tok,
        mid,
        mod_rows,
        gp,
        ge.reshape(count, n_wide, D),
        gr.reshape(count, n_wide, D),
    )
    bias_att = lax.dynamic_update_slice_in_dim(
        jnp.zeros((3, D), F32), sums_bias[0].reshape(3, HALF), core * HALF, 1
    )
    grad_mod = jnp.concatenate(
        [sums_one[0], sums_one[1], sums[3], sums[1], sums[2], sums[0]]
    )
    bias_grad = jnp.concatenate(
        [grad_mod, bias_att[0], bias_att[2], sums[4], wides[0], sums[5]]
    )
    width = wmod.shape[0]
    mine = jnp.concatenate(
        [
            jnp.pad(bias_grad.reshape(count, 1, nbias), ((0, 0), (0, 0), (0, D - nbias))),
            jnp.pad(grad_mod.reshape(count, 1, width), ((0, 0), (0, 6), (0, D - width))),
        ],
        axis=1,
    )
    scale = 1.0 / math.sqrt(tokens.shape[0] * count * full)
    olds = [
        m.T
        for m in (modulate_moment, attend_moment, project_moment, expand_moment, reduce_moment)
    ]
    masters = [
        w.T
        for w in (modulate_weight, attend_weight, project_weight, expand_weight, reduce_weight)
    ]
    att = pad_rows(att.reshape(count, n_att, D), up_to(n_att, 8))
    fac, att_rows, modg, bias_sum, condition_rows = tail(
        att, mlp_rows, mine, small_all, wmod, olds, scale, (n_att, n_pro)
    )
    out = update(
        fac,
        att_rows,
        modg,
        mlp_rows,
        bias_sum,
        olds,
        masters,
        bias_moment[None],
        bias_flat[None],
        scale,
        count,
    )
    result = [block_out[None], tokens_grad[None], condition_rows[0:1]]
    result += [value.T for value in out[:15]]
    result += [value[0] for value in out[15:]]
    return tuple(result)


def solution(mesh):
    tok = P("shard", "ctx", None)
    row = P("shard", None)
    col = P(None, "shard")
    flat = P("shard")
    return jax.shard_map(
        on_device,
        mesh=mesh,
        in_specs=(tok, row, tok) + (col,) * 5 + (flat,) + (col,) * 5 + (flat,),
        out_specs=(tok, tok, row) + (col,) * 15 + (flat,) * 3,
        check_vma=False,
    )
```

```python
import functools
import math

import jax
import jax.numpy as jnp
from jax import lax
from jax.experimental import pallas as pl
from jax.experimental.pallas import tpu as pltpu
from jax.sharding import PartitionSpec as P

D = 384
FF = 1536
HEADS = 6
HEAD_DIM = 64
NS_ITERS = 5
HALF_HEADS = HEADS // 2
HALF = HALF_HEADS * HEAD_DIM

norm_eps = 1e-06
newton_a = 3.4445
newton_b = -4.775
newton_c = 2.0315
moment_decay = 0.95
matrix_rate = 0.5
bias_rate = 0.1
precise = lax.Precision.HIGHEST
LOG2E = 1.4426950408889634

MESH = pl.DeviceIdType.MESH
BF = jnp.bfloat16
F32 = jnp.float32
VMEM_BYTES = 60 * 2**20
VM = pl.BlockSpec(memory_space=pltpu.VMEM)


def params(collective=None):
    if collective is None:
        return pltpu.CompilerParams(vmem_limit_bytes=VMEM_BYTES)
    return pltpu.CompilerParams(
        collective_id=collective, has_side_effects=True, vmem_limit_bytes=VMEM_BYTES
    )


def dot(left, right):
    return jnp.dot(left, right, preferred_element_type=F32)


def dot_nt(left, right):
    return lax.dot_general(left, right, (((1,), (1,)), ((), ())), preferred_element_type=F32)


def dot_tn(left, right):
    return lax.dot_general(left, right, (((0,), (0,)), ((), ())), preferred_element_type=F32)


def split_low(values):
    high = values.astype(BF)
    return high, (values - high.astype(F32)).astype(BF)


def dot_three(left, right, op=dot):
    left_high, left_low = split_low(left)
    right_high, right_low = split_low(right)
    return op(left_high, right_high) + (op(left_high, right_low) + op(left_low, right_high))


def silu_of(values):
    return values * jax.nn.sigmoid(values)


def normalize(values):
    centered = values - jnp.mean(values, axis=-1, keepdims=True)
    inverse = lax.rsqrt(jnp.mean(centered * centered, axis=-1, keepdims=True) + norm_eps)
    return (centered * inverse, inverse)


def norm_back(grad_normed, normed, inverse):
    first = jnp.mean(grad_normed, axis=-1, keepdims=True)
    second = jnp.mean(grad_normed * normed, axis=-1, keepdims=True)
    return (grad_normed - first - normed * second) * inverse


def pad_rows(array, rows):
    return jnp.pad(array, ((0, 0),) * (array.ndim - 2) + ((0, rows - array.shape[-2]), (0, 0)))


def up_to(value, step):
    return -(-value // step) * step


def bit_of(value, bit):
    return lax.rem(value // (1 << bit), 2)


def flip(me, bit):
    return me + (1 - 2 * bit_of(me, bit)) * (1 << bit)


def other_core():
    return {"ctx": 1 - lax.axis_index("ctx")}


def signal_cube(me, nbits):
    sem = pltpu.get_barrier_semaphore()
    for bit in range(nbits):
        pl.semaphore_signal(
            sem, inc=1, device_id={"shard": flip(me, bit)}, device_id_type=MESH
        )
    pl.semaphore_signal(sem, inc=1, device_id=other_core(), device_id_type=MESH)
    pl.semaphore_wait(sem, nbits + 1)


def signal_all(me, count):
    sem = pltpu.get_barrier_semaphore()
    for step in range(1, count):
        pl.semaphore_signal(
            sem, inc=1, device_id={"shard": lax.rem(me + step, count)}, device_id_type=MESH
        )
    pl.semaphore_signal(sem, inc=1, device_id=other_core(), device_id_type=MESH)
    pl.semaphore_wait(sem, count)


def signal_core():
    sem = pltpu.get_barrier_semaphore()
    pl.semaphore_signal(sem, inc=1, device_id=other_core(), device_id_type=MESH)
    pl.semaphore_wait(sem, 1)


def remote(src, dst, send, recv, where):
    return pltpu.make_async_remote_copy(
        src, dst, send, recv, device_id=where, device_id_type=MESH
    )


def orders(nbits):
    up = list(range(nbits))
    return up, ([1, 0] + up[2:] if nbits >= 2 else up)


def scatter_orders(nbits):
    up = list(range(nbits))
    return up, (up[1:] + up[:1] if nbits >= 2 else up)


def cube_index(who, nbits, free, tail=()):
    lead = tuple(
        slice(None) if (nbits - 1 - d) in free else bit_of(who, nbits - 1 - d)
        for d in range(nbits)
    )
    return lead + tuple(tail)


class Gather:
    def __init__(self, nbits, whole, send, recv, psend, precv):
        self.nbits, self.whole = nbits, whole
        self.sems = send, recv, psend, precv
        self.me = lax.axis_index("shard")

    def step(self, which, at):
        seq = orders(self.nbits)[which][::-1]
        bit = seq[at]
        part = self.whole.at[cube_index(self.me, self.nbits, seq[:at], (which,))]
        send, recv = self.sems[:2]
        return remote(part, part, send.at[at], recv.at[at], {"shard": flip(self.me, bit)})

    def forward(self, which, at):
        seq = orders(self.nbits)[which][::-1]
        bit = seq[at]
        part = self.whole.at[
            cube_index(flip(self.me, bit), self.nbits, seq[:at], (which,))
        ]
        send, recv = self.sems[2:]
        return remote(part, part, send.at[at], recv.at[at], other_core())

    def each(self, act):
        for which in range(2):
            pl.when(lax.axis_index("ctx") == which)(functools.partial(act, which))

    def start(self):
        self.each(lambda which: self.step(which, 0).start())

    def advance(self, at):
        def act(which):
            self.step(which, at).wait()
            if at + 1 < self.nbits:
                self.step(which, at + 1).start()
            self.forward(which, at).start()

        self.each(act)

    def finish(self):
        def act(which):
            for at in range(self.nbits):
                self.forward(which, at).wait_send()
            for at in range(self.nbits):
                self.forward(1 - which, at).wait_recv()

        self.each(act)

    @staticmethod
    def scratch(nbits):
        return [pltpu.SemaphoreType.DMA((nbits,))] * 4


def front_kernel(
    nbits,
    att_own,
    pro_own,
    exp_own,
    red_own,
    mod_own,
    cond_ref,
    bias_ref,
    tok_ref,
    small_all,
    rows_ref,
    wide_ref,
    wp_ref,
    we_ref,
    wr_ref,
    w_ref,
    xin_ref,
    q_ref,
    k_ref,
    v_ref,
    ctx_ref,
    lse_ref,
    both_ref,
    whole_one,
    whole_two,
    tok_all,
    normed_all,
    small_own,
    mod_all,
    mod_send,
    cols,
    outgoing,
    ssend,
    srecv,
    msend,
    mrecv,
    sems,
    *gsems,
):
    count = 1 << nbits
    me = lax.axis_index("shard")
    core = lax.axis_index("ctx")
    signal_all(me, count)
    n_att, n_pro, n_wide = att_own.shape[0], pro_own.shape[0], exp_own.shape[0]
    width, nbias = mod_own.shape[0], bias_ref.shape[1]
    half = tok_ref.shape[0]
    own = cube_index(me, nbits, ())
    one = Gather(nbits, whole_one, *gsems[:4])
    two = Gather(nbits, whole_two, *gsems[4:])
    half_one, half_two = whole_one.shape[-2], whole_two.shape[-2]
    pad_pro, pad_wide = up_to(n_pro, 16), up_to(n_wide, 16)

    def joined(parts, total):
        pieces = []
        for part, rows in parts:
            pieces.append(part[...])
            if rows > part.shape[0]:
                pieces.append(jnp.zeros((rows - part.shape[0], D), F32))
        rows = sum(rows for _, rows in parts)
        if total > rows:
            pieces.append(jnp.zeros((total - rows, D), F32))
        return jnp.concatenate(pieces, axis=0).astype(BF)

    small_own[...] = jnp.zeros_like(small_own)
    small_own[0:1, :] = cond_ref[...].astype(F32)
    small_own[1:2, 0:nbias] = bias_ref[...].astype(BF).astype(F32)
    spread = []
    for step in range(1, count):
        to = lax.rem(me + step, count)
        copy = remote(
            small_own, small_all.at[me], ssend.at[step], srecv.at[step], {"shard": to}
        )
        copy.start()
        spread.append(copy)
    whole_one[own] = joined([(att_own, n_att)], 2 * half_one).reshape(2, half_one, D)
    one.start()
    toks = remote(tok_ref, tok_all.at[core], sems.at[0], sems.at[1], other_core())
    toks.start()
    tok_all[core] = tok_ref[...]
    small_all[me] = small_own[...]
    whole_two[own] = joined(
        [(pro_own, pad_pro), (exp_own, pad_wide), (red_own, pad_wide)], 2 * half_two
    ).reshape(2, half_two, D)
    block = 256

    def norm_side(side):
        def norm_block(index, _):
            rows = pl.ds(pl.multiple_of(index * block, block), block)
            normed, _inverse = normalize(tok_all[side, rows, :].astype(F32))
            normed_all[side, rows, :] = normed
            return 0

        lax.fori_loop(0, half // block, norm_block, 0)

    for copy in spread:
        copy.wait()
    silu_low = silu_of(small_all[:, 0, :]).astype(BF)
    part = dot_nt(silu_low, mod_own[...].astype(BF))
    for row in range(count):
        mod_send[row] = jnp.broadcast_to(part[row : row + 1, :], (8, width))
    mods = []
    for step in range(1, count):
        to = lax.rem(me + step, count)
        copy = remote(
            mod_send.at[to], mod_all.at[me], msend.at[step], mrecv.at[step], {"shard": to}
        )
        copy.start()
        mods.append(copy)
    mod_all[me] = mod_send[me]
    one.advance(0)
    norm_side(core)
    one.advance(1)
    toks.wait()
    norm_side(1 - core)
    biases = jnp.concatenate([small_all[s, 1:2, 0:nbias] for s in range(count)], axis=1)
    for at in range(2, nbits):
        one.advance(at)
    two.start()
    for copy in mods:
        copy.wait()
    mods = jnp.concatenate([mod_all[s, 0:1, :] for s in range(count)], axis=1)
    mods = mods + biases[:, 0 : 6 * D]
    rows_ref[...] = jnp.zeros_like(rows_ref)
    for row in range(6):
        rows_ref[row : row + 1, :] = mods[:, row * D : (row + 1) * D]
    rows_ref[6:7, :] = biases[:, 8 * D : 9 * D]
    rows_ref[7:8, :] = biases[:, 9 * D + FF :]
    wide_ref[...] = jnp.broadcast_to(biases[:, 9 * D : 9 * D + FF], (8, FF))
    shift = mods[:, 0:D]
    scale = 1.0 + mods[:, D : 2 * D]

    def shift_block(index, _):
        rows = pl.ds(pl.multiple_of(index * block, block), block)
        for side in range(2):
            xin_ref[side, rows, :] = (normed_all[side, rows, :] * scale + shift).astype(BF)
        return 0

    lax.fori_loop(0, half // block, shift_block, 0)

    def turned_bias(at):
        row = biases[:, at * D : (at + 1) * D]
        row = jnp.where(core == 0, row[:, 0:HALF], row[:, HALF:])
        return jnp.transpose(jnp.broadcast_to(row, (8, HALF)))[:, 0:1]

    query_bias, value_bias = turned_bias(6), turned_bias(7)

    def picked(rows, source, wanted, local, stride):
        index = lax.broadcasted_iota(jnp.int32, (rows, 1), 0)
        goal = wanted(index).astype(F32)
        block_of = jnp.floor((goal + 0.5) * (1.0 / local))
        place = goal + block_of * float(stride - local)
        column = lax.broadcasted_iota(jnp.int32, (rows, source.shape[0]), 1).astype(F32)
        return dot((column == place).astype(BF), source).astype(BF)

    one.finish()
    for part in range(3):
        w_ref[part * HALF : (part + 1) * HALF, :] = picked(
            HALF,
            whole_one[...].reshape(count * 2 * half_one, D),
            lambda index: index + (part * D + core * HALF),
            n_att,
            2 * half_one,
        )
    for side in range(2):
        xin = xin_ref[side]
        rows = pl.ds(side * half, half)
        query = dot_nt(w_ref[0:HALF, :], xin) + query_bias
        value = dot_nt(w_ref[2 * HALF :, :], xin) + value_bias
        query = query.astype(BF) * jnp.asarray(HEAD_DIM**-0.5, BF)
        value = value.astype(BF)
        for head in range(HALF_HEADS):
            part = slice(head * HEAD_DIM, (head + 1) * HEAD_DIM)
            q_ref[head, side] = query[part, :]
            v_ref[head, :, rows] = value[part, :]
            k_ref[head, rows, :] = dot_nt(
                xin, w_ref[HALF + head * HEAD_DIM : HALF + (head + 1) * HEAD_DIM, :]
            ).astype(BF)
    two.advance(0)

    def attend(step, _):
        head = step // 2
        side = lax.rem(step, 2)
        scores = dot(k_ref[head], q_ref[head, side])
        top = jnp.max(scores, axis=0, keepdims=True)
        shifted = jnp.exp2((scores - top) * LOG2E)
        total = jnp.sum(shifted, axis=0, keepdims=True)
        probs = (shifted * (1.0 / total)).astype(BF)
        out = dot(v_ref[head], probs)
        ctx_ref[head, side] = out
        lse_ref[head, side] = jnp.broadcast_to(top * LOG2E + jnp.log2(total), (8, half))
        cols[side, pl.ds(pl.multiple_of(head * HEAD_DIM, HEAD_DIM), HEAD_DIM), :] = out
        for at in range(1, nbits - 1):
            pl.when(step == min(2 * at - 1, 4))(functools.partial(two.advance, at))
        return 0

    lax.fori_loop(0, 2 * HALF_HEADS, attend, 0)
    outgoing[...] = jnp.transpose(cols[1 - core]).astype(BF)
    copy = remote(outgoing, both_ref.at[core], sems.at[2], sems.at[3], other_core())
    copy.start()
    two.advance(nbits - 1)
    both_ref[core] = jnp.transpose(cols[core]).astype(BF)
    two.finish()
    whole = whole_two[...].reshape(count, 2 * half_two, D)
    wp_ref[...] = picked(
        D,
        whole[:, 0:pad_pro].reshape(count * pad_pro, D),
        lambda index: index,
        n_pro,
        pad_pro,
    )
    we_ref[...] = whole[:, pad_pro : pad_pro + pad_wide]
    wr_ref[...] = whole[:, pad_pro + pad_wide : pad_pro + 2 * pad_wide]
    copy.wait()


def front(weights, modulate, condition, bias, tok, count):
    nbits = count.bit_length() - 1
    n_att, n_pro, n_wide = (w.shape[0] for w in weights[:3])
    half = tok.shape[0]
    full = 2 * half
    half_one = up_to(n_att, 32) // 2
    half_two = up_to(up_to(n_pro, 16) + 2 * up_to(n_wide, 16), 32) // 2
    width = modulate.shape[0]
    lead = (2,) * nbits
    shape = jax.ShapeDtypeStruct
    sems = pltpu.SemaphoreType.DMA
    return pl.pallas_call(
        functools.partial(front_kernel, nbits),
        out_shape=[
            shape((count, 8, D), F32),
            shape((8, D), F32),
            shape((8, FF), F32),
            shape((D, D), BF),
            shape((count, up_to(n_wide, 16), D), BF),
            shape((count, up_to(n_wide, 16), D), BF),
            shape((3 * HALF, D), BF),
            shape((2, half, D), BF),
            shape((HALF_HEADS, 2, HEAD_DIM, half), BF),
            shape((HALF_HEADS, full, HEAD_DIM), BF),
            shape((HALF_HEADS, HEAD_DIM, full), BF),
            shape((HALF_HEADS, 2, HEAD_DIM, half), F32),
            shape((HALF_HEADS, 2, 8, half), F32),
            shape((2, half, HALF), BF),
        ],
        in_specs=[VM] * 8,
        out_specs=[VM] * 14,
        scratch_shapes=[
            pltpu.VMEM(lead + (2, half_one, D), BF),
            pltpu.VMEM(lead + (2, half_two, D), BF),
            pltpu.VMEM((2, half, D), BF),
            pltpu.VMEM((2, half, D), F32),
            pltpu.VMEM((8, D), F32),
            pltpu.VMEM((count, 8, width), F32),
            pltpu.VMEM((count, 8, width), F32),
            pltpu.VMEM((2, HALF, half), F32),
            pltpu.VMEM((half, HALF), BF),
            sems((count,)),
            sems((count,)),
            sems((count,)),
            sems((count,)),
            sems((4,)),
        ]
        + Gather.scratch(nbits) * 2,
        compiler_params=params(0),
        name="front",
    )(*weights, modulate, condition, bias, tok)


def branch_kernel(
    ctx_ref,
    tok_ref,
    cot_ref,
    mod_ref,
    wide_ref,
    wp_ref,
    we_ref,
    wr_ref,
    out_ref,
    mid_ref,
    gp_ref,
    ge_ref,
    gr_ref,
    sums_ref,
    wides_ref,
    both_ref,
    outgoing,
    sems,
):
    core = lax.axis_index("ctx")
    signal_core()
    half = tok_ref.shape[0]
    block = 256
    gate_one = mod_ref[2:3, :]
    shift_two = mod_ref[3:4, :]
    scale_two = 1.0 + mod_ref[4:5, :]
    gate_two = mod_ref[5:6, :]
    gp_ref[...] = jnp.zeros_like(gp_ref)
    ge_ref[...] = jnp.zeros_like(ge_ref)
    gr_ref[...] = jnp.zeros_like(gr_ref)
    sums_ref[...] = jnp.zeros_like(sums_ref)
    wides_ref[...] = jnp.zeros_like(wides_ref)

    def step(index, _):
        rows = pl.ds(pl.multiple_of(index * block, block), block)
        ctx = jnp.concatenate([ctx_ref[0, rows, :], ctx_ref[1, rows, :]], axis=1)
        attended = dot_nt(ctx, wp_ref[...]) + mod_ref[6:7, :]
        middle = tok_ref[rows, :].astype(F32) + gate_one * attended
        normed, inverse = normalize(middle)
        expand_in = (normed * scale_two + shift_two).astype(BF)
        hidden = dot_nt(expand_in, we_ref[...]) + wide_ref[0:1, :]
        squared = hidden * hidden
        bend = jnp.tanh(0.7978845608028654 * (hidden + 0.044715 * squared * hidden))
        rise = 0.5 * (1.0 + bend)
        act = (hidden * rise).astype(BF)
        slope = rise + 0.5 * hidden * (1.0 - bend * bend) * (
            0.7978845608028654 * (1.0 + 3.0 * 0.044715 * squared)
        )
        mlp_out = dot(act, wr_ref[...]) + mod_ref[7:8, :]
        out_ref[rows, :] = (middle + gate_two * mlp_out).astype(BF)
        grad_out = cot_ref[rows, :].astype(F32)
        grad_mlp = (gate_two * grad_out).astype(BF)
        gr_ref[...] += dot_tn(act, grad_mlp)
        grad_hidden = (dot_nt(grad_mlp, wr_ref[...]) * slope).astype(BF)
        ge_ref[...] += dot_tn(grad_hidden, expand_in)
        grad_in = dot(grad_hidden, we_ref[...])
        grad_middle = grad_out + norm_back(grad_in * scale_two, normed, inverse)
        mid_ref[rows, :] = grad_middle
        grad_attended = (gate_one * grad_middle).astype(BF)
        gp_ref[...] += dot_tn(grad_attended, ctx)
        back = dot(grad_attended, wp_ref[...]).astype(BF)
        first, second = back[:, :HALF], back[:, HALF:]
        both_ref[core, rows, :] = jnp.where(core == 0, first, second)
        outgoing[rows, :] = jnp.where(core == 0, second, first)
        add = lambda value: jnp.sum(value, axis=0, keepdims=True)
        sums_ref[0:1, :] += add(grad_out * mlp_out)
        sums_ref[1:2, :] += add(grad_in)
        sums_ref[2:3, :] += add(grad_in * normed)
        sums_ref[3:4, :] += add(grad_middle * attended)
        sums_ref[4:5, :] += add(grad_attended.astype(F32))
        sums_ref[5:6, :] += add(grad_mlp.astype(F32))
        wides_ref[0:1, :] += add(grad_hidden.astype(F32))
        return 0

    lax.fori_loop(0, half // block, step, 0)
    copy = remote(outgoing, both_ref.at[core], sems.at[0], sems.at[1], other_core())
    copy.start()
    copy.wait()


def branch(ctx, tok, cot, mod_rows, wide_rows, wp, we, wr):
    half = tok.shape[0]
    shape = jax.ShapeDtypeStruct
    return pl.pallas_call(
        branch_kernel,
        out_shape=[
            shape((half, D), BF),
            shape((half, D), F32),
            shape((D, D), F32),
            shape((FF, D), F32),
            shape((FF, D), F32),
            shape((8, D), F32),
            shape((8, FF), F32),
            shape((2, half, HALF), BF),
        ],
        in_specs=[VM] * 8,
        out_specs=[VM] * 8,
        scratch_shapes=[pltpu.VMEM((half, HALF), BF), pltpu.SemaphoreType.DMA((2,))],
        compiler_params=params(2),
        name="branch",
    )(ctx, tok, cot, mod_rows, wide_rows, wp, we, wr)


def backward_kernel(
    nbits,
    dctx_ref,
    xin_ref,
    q_ref,
    k_ref,
    v_ref,
    ctx_ref,
    lse_ref,
    w_ref,
    tok_ref,
    mid_ref,
    mod_ref,
    gp_ref,
    ge_ref,
    gr_ref,
    grad_ref,
    att_ref,
    sums_ref,
    bias_ref,
    own_ref,
    *rest,
):
    stages = rest[:nbits]
    (
        first,
        total,
        k_turn,
        v_rows,
        dk_sum,
        dv_sum,
        dq_low,
        dk_low,
        dv_low,
        gw,
        outgoing,
        incoming,
        sems,
        asems,
        send,
        recv,
    ) = rest[nbits:]
    me = lax.axis_index("shard")
    core = lax.axis_index("ctx")
    signal_cube(me, nbits)
    half = tok_ref.shape[0]
    lead = (slice(None),) * nbits
    wide = ge_ref.shape[-2]
    both = wide + gp_ref.shape[-2]
    last = nbits + 1
    main = lead + (slice(0, wide),)
    side_rows = lead + (slice(wide, both),)
    spots = {1: 0, 2: 2, 3: 3, 4: 4}
    after = range(5, nbits + 2)

    def swap_main(which):
        return remote(
            (gr_ref, ge_ref)[which], first.at[main], send.at[0], recv.at[0], other_core()
        )

    swap_side = remote(gp_ref, first.at[side_rows], send.at[last], recv.at[last], other_core())

    def cube_step(which, step):
        order = scatter_orders(nbits)[which]
        rows = slice(0, both if which == 0 else wide)
        bit = order[step]
        free = order[step + 1 :]
        there = flip(me, bit)
        return remote(
            total.at[cube_index(there, nbits, free, (rows,))],
            stages[step].at[(slice(None),) * len(free) + (rows,)],
            send.at[step + 1],
            recv.at[step + 1],
            {"shard": there},
        )

    def last_swap(which):
        rows = slice(0, both if which == 0 else wide)
        return remote(
            own_ref.at[which, rows],
            own_ref.at[which, rows],
            send.at[nbits + 2],
            recv.at[nbits + 2],
            other_core(),
        )

    def progress(point):
        for which in range(2):

            @pl.when(core == which)
            def _():
                rows = slice(0, both if which == 0 else wide)
                order = scatter_orders(nbits)[which]
                if point == 0:
                    swap_main(which).start()
                    if which == 1:
                        swap_side.start()
                elif point == 1:
                    swap_main(which).wait()
                    if which == 0:
                        swap_side.wait_recv()
                        total[main] = ge_ref[...] + first[main]
                        total[side_rows] = gp_ref[...] + first[side_rows]
                    else:
                        swap_side.wait_send()
                        total[main] = gr_ref[...] + first[main]
                elif point <= nbits + 1:
                    step = point - 2
                    cube_step(which, step).wait()
                    free = order[step + 1 :]
                    total[cube_index(me, nbits, free, (rows,))] += stages[step][
                        (slice(None),) * len(free) + (rows,)
                    ]
                if 1 <= point <= nbits:
                    cube_step(which, point - 1).start()
                if point == nbits + 1:
                    own_ref[which, rows] = total[cube_index(me, nbits, (), (rows,))]
                    last_swap(which).start()
                if point == nbits + 2:
                    last_swap(which).wait_send()
                    last_swap(1 - which).wait_recv()

    turn = lambda value: jnp.transpose(value.astype(F32)).astype(BF)
    progress(0)
    for head in range(HALF_HEADS):
        k_turn[...] = turn(k_ref[head])
        v_rows[...] = turn(v_ref[head])
        dk_sum[...] = jnp.zeros_like(dk_sum)
        dv_sum[...] = jnp.zeros_like(dv_sum)

        def step(side, _):
            query = q_ref[head, side]
            down = dctx_ref[side, :, head * HEAD_DIM : (head + 1) * HEAD_DIM]
            down_turn = jnp.transpose(down.astype(F32))
            delta = jnp.sum(down_turn * ctx_ref[head, side], axis=0, keepdims=True)
            scores = dot(k_ref[head], query)
            probs = jnp.exp2(scores * LOG2E - lse_ref[head, side, 0:1, :])
            dv_sum[...] += dot(probs.astype(BF), down)
            grad_probs = dot(v_rows[...], down_turn.astype(BF))
            grad_scores = (probs * (grad_probs - delta)).astype(BF)
            dk_sum[...] += dot(grad_scores, turn(query))
            dq_low[head, side] = (
                jnp.transpose(dot(k_turn[...], grad_scores)) * (HEAD_DIM**-0.5)
            ).astype(BF)
            for at in range(2):
                for point in range(1, 5):
                    if spots[point] == head * 2 + at:
                        pl.when(side == at)(functools.partial(progress, point))
            return 0

        lax.fori_loop(0, 2, step, 0)
        dk_low[head] = dk_sum[...].reshape(2, half, HEAD_DIM).astype(BF)
        dv_low[head] = dv_sum[...].reshape(2, half, HEAD_DIM).astype(BF)

    def side_grads(side, fresh):
        pieces = [dq_low[h, side] for h in range(HALF_HEADS)]
        pieces += [dk_low[h, side] for h in range(HALF_HEADS)]
        pieces += [dv_low[h, side] for h in range(HALF_HEADS)]
        joined = jnp.concatenate(pieces, axis=1)
        grad = dot_tn(joined, xin_ref[side])
        sums = dot(jnp.ones((8, half), BF), joined)
        gw[...] = grad if fresh else gw[...] + grad
        bias_ref[...] = sums if fresh else bias_ref[...] + sums
        return dot(joined, w_ref[...])

    outgoing[...] = side_grads(1 - core, True)
    copy = remote(outgoing, incoming, sems.at[0], sems.at[1], other_core())
    copy.start()
    own = side_grads(core, False)
    for point in after:
        progress(point)

    def share(which):
        return [
            remote(
                att_ref.at[pl.ds(block * D + which * HALF, HALF), :],
                att_ref.at[pl.ds(block * D + which * HALF, HALF), :],
                asems.at[0, block],
                asems.at[1, block],
                other_core(),
            )
            for block in range(3)
        ]

    for which in range(2):

        @pl.when(core == which)
        def _():
            for block in range(3):
                att_ref[block * D + which * HALF : block * D + (which + 1) * HALF, :] = gw[
                    block * HALF : (block + 1) * HALF, :
                ]
            for part in share(which):
                part.start()

    copy.wait()
    grad_in = own + incoming[...]
    normed, inverse = normalize(tok_ref[...].astype(F32))
    scale = 1.0 + mod_ref[1:2, :]
    grad_ref[...] = mid_ref[...] + norm_back(grad_in * scale, normed, inverse)
    sums_ref[0:1, :] = jnp.sum(grad_in, axis=0, keepdims=True)
    sums_ref[1:2, :] = jnp.sum(grad_in * normed, axis=0, keepdims=True)
    for which in range(2):

        @pl.when(core == which)
        def _():
            for part in share(which):
                part.wait_send()
            for part in share(1 - which):
                part.wait_recv()

    progress(nbits + 2)


def attention_backward(dctx, xin, q, k, v, ctx, lse, weight, tok, mid, mod_rows, gp, ge, gr):
    half = tok.shape[0]
    full = 2 * half
    count, wide, _ = ge.shape
    both = wide + gp.shape[1]
    nbits = count.bit_length() - 1
    lead = (2,) * nbits
    shape = jax.ShapeDtypeStruct
    sems = pltpu.SemaphoreType.DMA
    return pl.pallas_call(
        functools.partial(backward_kernel, nbits),
        out_shape=[
            shape((half, D), F32),
            shape((3 * D, D), F32),
            shape((8, D), F32),
            shape((8, 3 * HALF), F32),
            shape((2, both, D), F32),
        ],
        in_specs=[VM] * 14,
        out_specs=[VM] * 5,
        scratch_shapes=[pltpu.VMEM((2,) * (nbits - 1 - k) + (both, D), F32) for k in range(nbits)]
        + [
            pltpu.VMEM(lead + (both, D), F32),
            pltpu.VMEM(lead + (both, D), F32),
            pltpu.VMEM((HEAD_DIM, full), BF),
            pltpu.VMEM((full, HEAD_DIM), BF),
            pltpu.VMEM((full, HEAD_DIM), F32),
            pltpu.VMEM((full, HEAD_DIM), F32),
            pltpu.VMEM((HALF_HEADS, 2, half, HEAD_DIM), BF),
            pltpu.VMEM((HALF_HEADS, 2, half, HEAD_DIM), BF),
            pltpu.VMEM((HALF_HEADS, 2, half, HEAD_DIM), BF),
            pltpu.VMEM((3 * HALF, D), F32),
            pltpu.VMEM((half, D), F32),
            pltpu.VMEM((half, D), F32),
            sems((2,)),
            sems((2, 3)),
            sems((nbits + 3,)),
            sems((nbits + 3,)),
        ],
        compiler_params=params(3),
        name="attend_backward",
    )(
        dctx,
        xin,
        q,
        k,
        v,
        ctx,
        lse,
        weight,
        tok,
        mid,
        mod_rows,
        gp.reshape(lead + gp.shape[1:]),
        ge.reshape(lead + ge.shape[1:]),
        gr.reshape(lead + gr.shape[1:]),
    )


def newton_factor(gram, eye):
    factor = None
    for sweep in range(NS_ITERS):
        square = dot_three(gram, gram)
        step = newton_a * eye + newton_b * gram + newton_c * square
        if sweep < NS_ITERS - 1:
            gram = dot_three(dot_three(step, gram), step)
        factor = step if factor is None else dot_three(step, factor)
    return factor


def gram_of(turned):
    return lax.dot_general(
        turned,
        turned,
        (((0,), (0,)), ((), ())),
        precision=precise,
        preferred_element_type=F32,
    )


TILE = 128


def pack_gram(gram):
    tile = lambda r, c: gram[r * TILE : (r + 1) * TILE, c * TILE : (c + 1) * TILE]
    upper = jnp.concatenate([tile(0, 0), tile(1, 1), tile(2, 2)], axis=1)
    lower = jnp.concatenate([tile(1, 0), tile(2, 0), tile(2, 1)], axis=1)
    return upper, lower


def unpack_gram(upper, lower):
    tile = lambda packed, c: packed[:, c * TILE : (c + 1) * TILE]
    one, two, three = (tile(lower, c) for c in range(3))
    return jnp.concatenate(
        [
            jnp.concatenate([tile(upper, 0), one.T, two.T], axis=1),
            jnp.concatenate([one, tile(upper, 1), three.T], axis=1),
            jnp.concatenate([two, three, tile(upper, 2)], axis=1),
        ],
        axis=0,
    )


class Sum:
    def __init__(self, count, source, landed, whole, extra, send, recv, gsend, grecv, hsend, hrecv):
        self.pieces = source.shape[0]
        self.high = [b for b in range(count.bit_length() - 1) if (1 << b) >= self.pieces]
        self.source, self.landed, self.whole, self.extra = source, landed, whole, extra
        self.sems = send, recv, gsend, grecv, hsend, hrecv
        self.me = lax.axis_index("shard")
        self.low = lax.rem(self.me, self.pieces)

    def peer(self, step):
        place = lax.rem(self.low + step, self.pieces)
        return place, {"shard": self.me - self.low + place}

    def scatter(self, step):
        place, where = self.peer(step)
        send, recv = self.sems[:2]
        return remote(
            self.source.at[place], self.landed.at[self.low], send.at[step], recv.at[step], where
        )

    def spread(self, step):
        _, where = self.peer(step)
        send, recv = self.sems[2:4]
        part = self.whole.at[self.low]
        return remote(part, part, send.at[step], recv.at[step], where)

    def start(self):
        for step in range(1, self.pieces):
            self.scatter(step).start()
        self.landed[self.low] = self.source[self.low]

    def turn(self):
        for step in range(1, self.pieces):
            self.scatter(step).wait()
        self.whole[self.low] = jnp.sum(self.landed[...], axis=0)
        send, recv = self.sems[4:]
        for at, bit in enumerate(self.high):
            copy = remote(
                self.whole.at[self.low],
                self.extra.at[at],
                send.at[at],
                recv.at[at],
                {"shard": flip(self.me, bit)},
            )
            copy.start()
            copy.wait()
            self.whole[self.low] += self.extra[at]
        for step in range(1, self.pieces):
            self.spread(step).start()

    def finish(self):
        for step in range(1, self.pieces):
            self.spread(step).wait()

    @staticmethod
    def scratch(count, rows):
        pieces = min(count, 16)
        high = max(count.bit_length() - pieces.bit_length(), 1)
        sems = pltpu.SemaphoreType.DMA
        block = pltpu.VMEM((pieces, rows // pieces, D), F32)
        return [block, block, block, pltpu.VMEM((high, rows // pieces, D), F32)] + [
            sems((pieces,))
        ] * 4 + [sems((high,))] * 2


SUM_REFS = 10


def tail_kernel(
    count,
    scale,
    local,
    att_ref,
    own_ref,
    mine_ref,
    small_ref,
    wmod_ref,
    old_mod,
    old_att,
    old_pro,
    old_exp,
    old_red,
    fac_ref,
    rows_ref,
    modg_ref,
    bias_ref,
    cond_ref,
    *rest,
):
    nbits = count.bit_length() - 1
    stages = rest[:nbits]
    total, got, theirs, back_send, back, upper_half, other_half = rest[nbits : nbits + 7]
    send, recv, msend, mrecv, bsend, brecv, csem, fsem = rest[nbits + 7 : nbits + 15]
    sums = rest[nbits + 15 :]
    one = Sum(count, *sums[:SUM_REFS])
    two = Sum(count, *sums[SUM_REFS : 2 * SUM_REFS])
    late = Sum(count, *sums[2 * SUM_REFS :])
    me = lax.axis_index("shard")
    core = lax.axis_index("ctx")
    signal_all(me, count)
    wide = old_exp.shape[0]
    n_att, n_pro = local
    padded = att_ref.shape[-2]
    first_rows = total.shape[-2]

    def rows_of(which):
        return slice(0, first_rows) if which == 0 else slice(0, padded - first_rows)

    def cube_step(which, step):
        order = scatter_orders(nbits)[which]
        bit = order[step]
        free = order[step + 1 :]
        there = flip(me, bit)
        rows = rows_of(which)
        source = total.at[cube_index(there, nbits, free, (rows,))]
        return remote(
            source,
            stages[step].at[(slice(None),) * len(free) + (rows,)],
            send.at[step],
            recv.at[step],
            {"shard": there},
        )

    def swap_rows(which):
        part = rows_ref.at[which, rows_of(which)]
        return remote(part, part, csem.at[2], csem.at[3], other_core())

    def progress(point):
        for which in range(2):

            @pl.when(core == which)
            def _():
                rows = rows_of(which)
                lead = (slice(None),) * nbits
                order = scatter_orders(nbits)[which]
                if point == 0:
                    begin = 0 if which == 0 else first_rows
                    total[lead + (rows,)] = att_ref[
                        lead + (slice(begin, begin + rows.stop),)
                    ]
                else:
                    step = point - 1
                    cube_step(which, step).wait()
                    free = order[step + 1 :]
                    total[cube_index(me, nbits, free, (rows,))] += stages[step][
                        (slice(None),) * len(free) + (rows,)
                    ]
                if point < nbits:
                    cube_step(which, point).start()
                else:
                    rows_ref[which, rows] = total[cube_index(me, nbits, (), (rows,))]
                    swap_rows(which).start()

    progress(0)
    copies = []
    got[me] = mine_ref[me]
    for step in range(1, count):
        to = lax.rem(me + step, count)
        copy = remote(mine_ref.at[to], got.at[me], msend.at[step], mrecv.at[step], {"shard": to})
        copy.start()
        copies.append(copy)

    def put(target, gram):
        upper, lower = pack_gram(gram)
        packed = jnp.concatenate([upper, lower], axis=0)
        target.source[...] = packed.reshape(target.source.shape)

    old = jnp.where(core == 0, old_exp[...], old_red[...])
    put(one, gram_of(moment_decay * old + own_ref[core, 0:wide, :] * scale))
    one.start()

    for copy in copies:
        copy.wait()
    swap = remote(got, theirs, csem.at[0], csem.at[1], other_core())
    swap.start()
    cond = small_ref[:, 0, :]
    silu_low = silu_of(cond).astype(BF).astype(F32)
    swap.wait()
    width = old_mod.shape[0]
    grad_mod = got[:, 1, 0:width] + theirs[:, 1, 0:width]
    bias_ref[...] = jnp.sum(got[...] + theirs[...], axis=0)
    raw = lax.dot_general(
        grad_mod,
        silu_low,
        (((0,), (0,)), ((), ())),
        precision=precise,
        preferred_element_type=F32,
    )
    modg_ref[...] = raw
    part = jnp.dot(
        grad_mod, wmod_ref[...].astype(BF).astype(F32), precision=precise, preferred_element_type=F32
    )
    for row in range(count):
        back_send[row] = jnp.broadcast_to(part[row : row + 1, :], (8, D))
    back[me] = back_send[me]
    backs = []
    for step in range(1, count):
        to = lax.rem(me + step, count)
        copy = remote(
            back_send.at[to], back.at[me], bsend.at[step], brecv.at[step], {"shard": to}
        )
        copy.start()
        backs.append(copy)

    @pl.when(core == 0)
    def _():
        grad = own_ref[0, wide : wide + n_pro, :] * scale
        put(two, gram_of(moment_decay * old_pro[...] + grad))

    @pl.when(core == 1)
    def _():
        put(two, gram_of(moment_decay * old_mod[...] + modg_ref[...] * scale))

    two.start()
    points = list(range(1, nbits + 1))
    progress(points[0])
    one.turn()
    for copy in backs:
        copy.wait()
    grad_silu = jnp.sum(back[...], axis=0)
    own = small_ref[me]
    gate = jax.nn.sigmoid(own)
    cond_ref[...] = grad_silu * (gate + own * gate * (1.0 - gate))
    for point in points[1:2]:
        progress(point)
    two.turn()
    for point in points[2:]:
        progress(point)

    for which in range(2):

        @pl.when(core == which)
        def _():
            swap_rows(which).wait_send()
            swap_rows(1 - which).wait_recv()

    grad = jnp.concatenate(
        [rows_ref[0], rows_ref[1, 0 : padded - first_rows]], axis=0
    )[0:n_att] * scale
    upper, lower = pack_gram(gram_of(moment_decay * old_att[...] + grad))
    late.source[...] = jnp.where(core == 0, upper, lower).reshape(late.source.shape)
    late.start()

    row = lax.broadcasted_iota(jnp.int32, (D, D), 0)
    column = lax.broadcasted_iota(jnp.int32, (D, D), 1)
    eye = (row == column).astype(F32)

    def solve(gram):
        diagonal = jnp.sum(gram * eye, axis=0, keepdims=True)
        size = 1.0 / (jnp.sqrt(jnp.sum(diagonal, axis=1, keepdims=True)) + 1e-07)
        return newton_factor((gram * size) * size, eye) * size

    def solve_sum(item):
        packed = item.whole[...].reshape(2 * TILE, D)
        return solve(unpack_gram(packed[0:TILE], packed[TILE:]))

    def pass_factor(index, at):
        part = fac_ref.at[index]
        return remote(part, part, fsem.at[0, at], fsem.at[1, at], other_core())

    one.finish()
    place_one, place_two = 3 + core, 2 - 2 * core
    fac_ref[place_one] = solve_sum(one)
    first_pass = pass_factor(place_one, 0)
    first_pass.start()
    late.turn()
    two.finish()
    fac_ref[place_two] = solve_sum(two)
    second_pass = pass_factor(place_two, 1)
    second_pass.start()
    late.finish()
    upper_half[...] = late.whole[...].reshape(TILE, D)
    halves = remote(upper_half, other_half, csem.at[4], csem.at[5], other_core())
    halves.start()
    halves.wait()
    mine_half, their_half = upper_half[...], other_half[...]
    fac_ref[1] = solve(
        unpack_gram(
            jnp.where(core == 0, mine_half, their_half),
            jnp.where(core == 0, their_half, mine_half),
        )
    )
    first_pass.wait()
    second_pass.wait()


def tail(att, own, mine, small_all, wmod, olds, scale, local):
    count, padded, _ = att.shape
    nbits = count.bit_length() - 1
    lead = (2,) * nbits
    first_rows = -(-padded // 16) * 8
    width = wmod.shape[0]
    sems = pltpu.SemaphoreType.DMA
    shape = jax.ShapeDtypeStruct
    return pl.pallas_call(
        functools.partial(tail_kernel, count, scale, local),
        out_shape=[
            shape((5, D, D), F32),
            shape((2, first_rows, D), F32),
            shape((width, D), F32),
            shape((8, D), F32),
            shape((8, D), F32),
        ],
        in_specs=[VM] * 10,
        out_specs=[VM] * 5,
        scratch_shapes=[
            pltpu.VMEM((2,) * (nbits - 1 - k) + (first_rows, D), F32) for k in range(nbits)
        ]
        + [
            pltpu.VMEM(lead + (first_rows, D), F32),
            pltpu.VMEM((count, 8, D), F32),
            pltpu.VMEM((count, 8, D), F32),
            pltpu.VMEM((count, 8, D), F32),
            pltpu.VMEM((count, 8, D), F32),
            pltpu.VMEM((TILE, D), F32),
            pltpu.VMEM((TILE, D), F32),
            sems((nbits,)),
            sems((nbits,)),
            sems((count,)),
            sems((count,)),
            sems((count,)),
            sems((count,)),
            sems((6,)),
            sems((2, 2)),
        ]
        + Sum.scratch(count, 2 * TILE)
        + Sum.scratch(count, 2 * TILE)
        + Sum.scratch(count, TILE),
        compiler_params=params(4),
        name="tail",
    )(att.reshape(lead + (padded, D)), own, mine, small_all, wmod, *olds)


def update_kernel(scale, rates, bounds, *refs):
    fac_ref, att_ref, modg_ref, own_ref, bias_ref = refs[:5]
    olds, masters, old_bias, bias = refs[5:10], refs[10:15], refs[15], refs[16]
    outs = refs[17:]
    n_att, wide, n_pro, nbias = bounds
    first_rows = att_ref.shape[1]
    joined = jnp.concatenate([att_ref[0], att_ref[1]], axis=0)
    grads = [
        modg_ref[...],
        joined[0:n_att],
        own_ref[0, wide : wide + n_pro, :],
        own_ref[0, 0:wide, :],
        own_ref[1, 0:wide, :],
    ]
    for index in range(5):
        grad = grads[index] * scale
        moment = moment_decay * olds[index][...] + grad
        direction = dot_three(moment, fac_ref[index])
        outs[3 * index][...] = grad
        outs[3 * index + 1][...] = masters[index][...] - rates[index] * direction
        outs[3 * index + 2][...] = moment
    grad = bias_ref[0:1, 0:nbias] * scale
    moment = moment_decay * old_bias[...] + grad
    outs[15][...] = grad
    outs[16][...] = bias[...] - bias_rate * moment
    outs[17][...] = moment


def update(fac, att, modg, own, bias_sum, olds, masters, old_bias, bias, scale, count):
    shape = jax.ShapeDtypeStruct
    out = []
    for m in masters:
        out += [shape(m.shape, F32)] * 3
    out += [shape(bias.shape, F32)] * 3
    rates = [matrix_rate * 0.2 * math.sqrt(max(D, m.shape[0] * count)) for m in masters]
    bounds = (olds[1].shape[0], olds[3].shape[0], olds[2].shape[0], bias.shape[1])
    return pl.pallas_call(
        functools.partial(update_kernel, scale, rates, bounds),
        out_shape=out,
        in_specs=[VM] * 17,
        out_specs=[VM] * 18,
        compiler_params=params(),
        name="update",
    )(fac, att, modg, own, bias_sum, *olds, *masters, old_bias, bias)


def on_device(
    tokens,
    condition,
    cotangent,
    modulate_weight,
    attend_weight,
    project_weight,
    expand_weight,
    reduce_weight,
    bias_flat,
    modulate_moment,
    attend_moment,
    project_moment,
    expand_moment,
    reduce_moment,
    bias_moment,
):
    count = lax.axis_size("shard")
    core = lax.axis_index("ctx")
    full = tokens.shape[1] * lax.axis_size("ctx")
    olds = [
        m.T
        for m in (modulate_moment, attend_moment, project_moment, expand_moment, reduce_moment)
    ]
    masters = [
        w.T
        for w in (modulate_weight, attend_weight, project_weight, expand_weight, reduce_weight)
    ]
    n_att, n_pro, n_wide = (w.shape[0] for w in masters[1:4])
    nbias = bias_flat.shape[0]
    width = masters[0].shape[0]
    tok = tokens[0]
    (
        small_all,
        mod_rows,
        wide_rows,
        project_turn,
        expand_turn,
        reduce_turn,
        weight_core,
        xin,
        q,
        k,
        v,
        ctx_turn,
        lse,
        ctx,
    ) = front(masters[1:], masters[0], condition, bias_flat[None], tok, count)
    block_out, mid, gp, ge, gr, sums, wides, dctx = branch(
        ctx,
        tok,
        cotangent[0],
        mod_rows,
        wide_rows,
        project_turn,
        expand_turn[:, :n_wide].reshape(FF, D),
        reduce_turn[:, :n_wide].reshape(FF, D),
    )
    gp = pad_rows(gp.reshape(count, n_pro, D), up_to(n_pro, 8))
    tokens_grad, att, sums_one, sums_bias, mlp_rows = attention_backward(
        dctx,
        xin,
        q,
        k,
        v,
        ctx_turn,
        lse,
        weight_core,
        tok,
        mid,
        mod_rows,
        gp,
        ge.reshape(count, n_wide, D),
        gr.reshape(count, n_wide, D),
    )
    bias_att = lax.dynamic_update_slice_in_dim(
        jnp.zeros((3, D), F32), sums_bias[0].reshape(3, HALF), core * HALF, 1
    )
    grad_mod = jnp.concatenate(
        [sums_one[0], sums_one[1], sums[3], sums[1], sums[2], sums[0]]
    )
    bias_grad = jnp.concatenate(
        [grad_mod, bias_att[0], bias_att[2], sums[4], wides[0], sums[5]]
    )
    mine = jnp.concatenate(
        [
            jnp.pad(bias_grad.reshape(count, 1, nbias), ((0, 0), (0, 0), (0, D - nbias))),
            jnp.pad(grad_mod.reshape(count, 1, width), ((0, 0), (0, 6), (0, D - width))),
        ],
        axis=1,
    )
    scale = 1.0 / math.sqrt(tokens.shape[0] * count * full)
    att = pad_rows(att.reshape(count, n_att, D), up_to(n_att, 8))
    fac, att_rows, modg, bias_sum, condition_rows = tail(
        att, mlp_rows, mine, small_all, masters[0], olds, scale, (n_att, n_pro)
    )
    out = update(
        fac,
        att_rows,
        modg,
        mlp_rows,
        bias_sum,
        olds,
        masters,
        bias_moment[None],
        bias_flat[None],
        scale,
        count,
    )
    result = [block_out[None], tokens_grad[None], condition_rows[0:1]]
    result += [value.T for value in out[:15]]
    result += [value[0] for value in out[15:]]
    return tuple(result)


def solution(mesh):
    tok = P("shard", "ctx", None)
    row = P("shard", None)
    col = P(None, "shard")
    flat = P("shard")
    return jax.shard_map(
        on_device,
        mesh=mesh,
        in_specs=(tok, row, tok) + (col,) * 5 + (flat,) + (col,) * 5 + (flat,),
        out_specs=(tok, tok, row) + (col,) * 15 + (flat,) * 3,
        check_vma=False,
    )
```

```python
import functools
import math

import jax
import jax.numpy as jnp
from jax import lax
from jax.experimental import pallas as pl
from jax.experimental.pallas import tpu as pltpu
from jax.sharding import PartitionSpec as P

D = 384
FF = 1536
HEADS = 6
HEAD_DIM = 64
NS_ITERS = 5
LOW_STEPS = 1
HALF_HEADS = HEADS // 2
HALF = HALF_HEADS * HEAD_DIM

norm_eps = 1e-06
newton_a = 3.4445
newton_b = -4.775
newton_c = 2.0315
moment_decay = 0.95
matrix_rate = 0.5
bias_rate = 0.1
precise = lax.Precision.HIGHEST
LOG2E = 1.4426950408889634

MESH = pl.DeviceIdType.MESH
BF = jnp.bfloat16
F32 = jnp.float32
VMEM_BYTES = 60 * 2**20
VM = pl.BlockSpec(memory_space=pltpu.VMEM)


def params(collective=None):
    if collective is None:
        return pltpu.CompilerParams(vmem_limit_bytes=VMEM_BYTES)
    return pltpu.CompilerParams(
        collective_id=collective, has_side_effects=True, vmem_limit_bytes=VMEM_BYTES
    )


def dot(left, right):
    return jnp.dot(left, right, preferred_element_type=F32)


def dot_nt(left, right):
    return lax.dot_general(left, right, (((1,), (1,)), ((), ())), preferred_element_type=F32)


def dot_tn(left, right):
    return lax.dot_general(left, right, (((0,), (0,)), ((), ())), preferred_element_type=F32)


def split_low(values):
    high = values.astype(BF)
    return high, (values - high.astype(F32)).astype(BF)


def dot_three(left, right, op=dot):
    left_high, left_low = split_low(left)
    right_high, right_low = split_low(right)
    return op(left_high, right_high) + (op(left_high, right_low) + op(left_low, right_high))


def silu_of(values):
    return values * jax.nn.sigmoid(values)


def normalize(values):
    centered = values - jnp.mean(values, axis=-1, keepdims=True)
    inverse = lax.rsqrt(jnp.mean(centered * centered, axis=-1, keepdims=True) + norm_eps)
    return (centered * inverse, inverse)


def norm_back(grad_normed, normed, inverse):
    first = jnp.mean(grad_normed, axis=-1, keepdims=True)
    second = jnp.mean(grad_normed * normed, axis=-1, keepdims=True)
    return (grad_normed - first - normed * second) * inverse


def pad_rows(array, rows):
    return jnp.pad(array, ((0, 0),) * (array.ndim - 2) + ((0, rows - array.shape[-2]), (0, 0)))


def up_to(value, step):
    return -(-value // step) * step


def bit_of(value, bit):
    return lax.rem(value // (1 << bit), 2)


def flip(me, bit):
    return me + (1 - 2 * bit_of(me, bit)) * (1 << bit)


def other_core():
    return {"ctx": 1 - lax.axis_index("ctx")}


def signal_cube(me, nbits):
    sem = pltpu.get_barrier_semaphore()
    for bit in range(nbits):
        pl.semaphore_signal(
            sem, inc=1, device_id={"shard": flip(me, bit)}, device_id_type=MESH
        )
    pl.semaphore_signal(sem, inc=1, device_id=other_core(), device_id_type=MESH)
    pl.semaphore_wait(sem, nbits + 1)


def signal_all(me, count):
    sem = pltpu.get_barrier_semaphore()
    for step in range(1, count):
        pl.semaphore_signal(
            sem, inc=1, device_id={"shard": lax.rem(me + step, count)}, device_id_type=MESH
        )
    pl.semaphore_signal(sem, inc=1, device_id=other_core(), device_id_type=MESH)
    pl.semaphore_wait(sem, count)


def signal_core():
    sem = pltpu.get_barrier_semaphore()
    pl.semaphore_signal(sem, inc=1, device_id=other_core(), device_id_type=MESH)
    pl.semaphore_wait(sem, 1)


def remote(src, dst, send, recv, where):
    return pltpu.make_async_remote_copy(
        src, dst, send, recv, device_id=where, device_id_type=MESH
    )


def orders(nbits):
    up = list(range(nbits))
    return up, ([1, 0] + up[2:] if nbits >= 2 else up)


def scatter_orders(nbits):
    up = list(range(nbits))
    return up, (up[1:] + up[:1] if nbits >= 2 else up)


def digit_of(value, digit):
    return lax.rem(value // (1 << (2 * digit)), 4)


def digit_peer(me, digit, step):
    own = digit_of(me, digit)
    place = lax.rem(own + step, 4)
    return place, {"shard": me + (place - own) * (1 << (2 * digit))}


def cube_index(who, nbits, free, tail=()):
    lead = tuple(
        slice(None) if (nbits - 1 - d) in free else bit_of(who, nbits - 1 - d)
        for d in range(nbits)
    )
    return lead + tuple(tail)


class Gather:
    def __init__(self, nbits, whole, send, recv, psend, precv):
        self.nbits, self.whole = nbits, whole
        self.sems = send, recv, psend, precv
        self.me = lax.axis_index("shard")

    def step(self, which, at):
        seq = orders(self.nbits)[which][::-1]
        bit = seq[at]
        part = self.whole.at[cube_index(self.me, self.nbits, seq[:at], (which,))]
        send, recv = self.sems[:2]
        return remote(part, part, send.at[at], recv.at[at], {"shard": flip(self.me, bit)})

    def forward(self, which, at):
        seq = orders(self.nbits)[which][::-1]
        bit = seq[at]
        part = self.whole.at[
            cube_index(flip(self.me, bit), self.nbits, seq[:at], (which,))
        ]
        send, recv = self.sems[2:]
        return remote(part, part, send.at[at], recv.at[at], other_core())

    def each(self, act):
        for which in range(2):
            pl.when(lax.axis_index("ctx") == which)(functools.partial(act, which))

    def start(self):
        self.each(lambda which: self.step(which, 0).start())

    def advance(self, at):
        def act(which):
            self.step(which, at).wait()
            if at + 1 < self.nbits:
                self.step(which, at + 1).start()
            self.forward(which, at).start()

        self.each(act)

    def finish(self):
        def act(which):
            for at in range(self.nbits):
                self.forward(which, at).wait_send()
            for at in range(self.nbits):
                self.forward(1 - which, at).wait_recv()

        self.each(act)

    @staticmethod
    def scratch(nbits):
        return [pltpu.SemaphoreType.DMA((nbits,))] * 4


class FourGather:
    def __init__(self, digits, whole, send, recv, swap):
        self.digits, self.whole = digits, whole
        self.sems, self.swap = (send, recv), swap
        self.me = lax.axis_index("shard")
        self.core = lax.axis_index("ctx")

    def round(self, at):
        digit = self.digits - 1 - at
        own = tuple(digit_of(self.me, d) for d in range(digit, -1, -1))
        part = self.whole.at[(slice(None),) * at + own + (self.core,)]
        send, recv = self.sems
        copies = []
        for step in range(1, 4):
            _, where = digit_peer(self.me, digit, step)
            copies.append(remote(part, part, send.at[at, step], recv.at[at, step], where))
        return copies

    def start(self, at):
        for copy in self.round(at):
            copy.start()

    def wait(self, at):
        for copy in self.round(at):
            copy.wait()

    def forward(self):
        part = self.whole.at[(slice(None),) * self.digits + (self.core,)]
        return remote(part, part, self.swap.at[0], self.swap.at[1], other_core())


def front_kernel(
    nbits,
    att_own,
    pro_own,
    exp_own,
    red_own,
    mod_own,
    cond_ref,
    bias_ref,
    tok_ref,
    small_all,
    rows_ref,
    wide_ref,
    wp_ref,
    we_ref,
    wr_ref,
    w_ref,
    xin_ref,
    q_ref,
    k_ref,
    v_ref,
    ctx_ref,
    lse_ref,
    both_ref,
    whole_one,
    whole_two,
    tok_all,
    normed_all,
    small_own,
    mod_all,
    mod_send,
    cols,
    outgoing,
    ssend,
    srecv,
    msend,
    mrecv,
    sems,
    *gsems,
):
    count = 1 << nbits
    me = lax.axis_index("shard")
    core = lax.axis_index("ctx")
    signal_all(me, count)
    n_att, n_pro, n_wide = att_own.shape[0], pro_own.shape[0], exp_own.shape[0]
    width, nbias = mod_own.shape[0], bias_ref.shape[1]
    half = tok_ref.shape[0]
    digits = nbits // 2
    own = cube_index(me, nbits, ())
    one = FourGather(digits, whole_one, *gsems[:3])
    two = Gather(nbits, whole_two, *gsems[3:])
    half_one, half_two = whole_one.shape[-2], whole_two.shape[-2]
    pad_pro, pad_wide = up_to(n_pro, 16), up_to(n_wide, 16)

    def joined(parts, total):
        pieces = []
        for part, rows in parts:
            pieces.append(part[...])
            if rows > part.shape[0]:
                pieces.append(jnp.zeros((rows - part.shape[0], D), F32))
        rows = sum(rows for _, rows in parts)
        if total > rows:
            pieces.append(jnp.zeros((total - rows, D), F32))
        return jnp.concatenate(pieces, axis=0).astype(BF)

    small_own[...] = jnp.zeros_like(small_own)
    small_own[:, 0:D] = cond_ref[...].astype(F32)
    small_own[:, D : D + nbias] = bias_ref[...].astype(BF).astype(F32)
    spread = []
    for step in range(1, count):
        to = lax.rem(me + step, count)
        copy = remote(
            small_own, small_all.at[me], ssend.at[step], srecv.at[step], {"shard": to}
        )
        copy.start()
        spread.append(copy)
    halves = joined([(att_own, n_att)], 2 * half_one)
    place = tuple(digit_of(me, d) for d in range(digits - 1, -1, -1))
    whole_one[place + (core,)] = jnp.where(core == 0, halves[:half_one], halves[half_one:])
    one.start(0)
    toks = remote(tok_ref, tok_all.at[core], sems.at[0], sems.at[1], other_core())
    toks.start()
    tok_all[core] = tok_ref[...]
    small_all[me] = small_own[...]
    whole_two[own] = joined(
        [(pro_own, pad_pro), (exp_own, pad_wide), (red_own, pad_wide)], 2 * half_two
    ).reshape(2, half_two, D)
    block = 256

    def norm_side(side):
        def norm_block(index, _):
            rows = pl.ds(pl.multiple_of(index * block, block), block)
            normed, _inverse = normalize(tok_all[side, rows, :].astype(F32))
            normed_all[side, rows, :] = normed
            return 0

        lax.fori_loop(0, half // block, norm_block, 0)

    one.wait(0)
    one.start(1)
    for copy in spread:
        copy.wait()
    silu_low = silu_of(small_all[:, 0, 0:D]).astype(BF)
    part = dot_nt(silu_low, mod_own[...].astype(BF))
    for row in range(count):
        mod_send[row] = part[row : row + 1, :]
    mods = []
    for step in range(1, count):
        to = lax.rem(me + step, count)
        copy = remote(
            mod_send.at[to], mod_all.at[me], msend.at[step], mrecv.at[step], {"shard": to}
        )
        copy.start()
        mods.append(copy)
    mod_all[me] = mod_send[me]
    norm_side(core)
    toks.wait()
    norm_side(1 - core)
    biases = jnp.concatenate([small_all[s, :, D : D + nbias] for s in range(count)], axis=1)
    for at in range(1, digits):
        one.wait(at)
        if at + 1 < digits:
            one.start(at + 1)
    forward = one.forward()
    forward.start()
    two.start()
    for copy in mods:
        copy.wait()
    mods = jnp.concatenate([mod_all[s] for s in range(count)], axis=1)
    mods = mods + biases[:, 0 : 6 * D]
    rows_ref[...] = jnp.zeros_like(rows_ref)
    for row in range(6):
        rows_ref[row : row + 1, :] = mods[:, row * D : (row + 1) * D]
    rows_ref[6:7, :] = biases[:, 8 * D : 9 * D]
    rows_ref[7:8, :] = biases[:, 9 * D + FF :]
    wide_ref[...] = jnp.broadcast_to(biases[:, 9 * D : 9 * D + FF], (8, FF))
    shift = mods[:, 0:D]
    scale = 1.0 + mods[:, D : 2 * D]

    def shift_block(index, _):
        rows = pl.ds(pl.multiple_of(index * block, block), block)
        for side in range(2):
            xin_ref[side, rows, :] = (normed_all[side, rows, :] * scale + shift).astype(BF)
        return 0

    lax.fori_loop(0, half // block, shift_block, 0)

    def turned_bias(at):
        row = biases[:, at * D : (at + 1) * D]
        row = jnp.where(core == 0, row[:, 0:HALF], row[:, HALF:])
        return jnp.transpose(jnp.broadcast_to(row, (8, HALF)))[:, 0:1]

    query_bias, value_bias = turned_bias(6), turned_bias(7)

    def picked(rows, source, wanted, local, stride):
        index = lax.broadcasted_iota(jnp.int32, (rows, 1), 0)
        goal = wanted(index).astype(F32)
        block_of = jnp.floor((goal + 0.5) * (1.0 / local))
        place = goal + block_of * float(stride - local)
        column = lax.broadcasted_iota(jnp.int32, (rows, source.shape[0]), 1).astype(F32)
        return dot((column == place).astype(BF), source).astype(BF)

    forward.wait()
    for part in range(3):
        w_ref[part * HALF : (part + 1) * HALF, :] = picked(
            HALF,
            whole_one[...].reshape(count * 2 * half_one, D),
            lambda index: index + (part * D + core * HALF),
            n_att,
            2 * half_one,
        )
    for side in range(2):
        xin = xin_ref[side]
        rows = pl.ds(side * half, half)
        query = dot_nt(w_ref[0:HALF, :], xin) + query_bias
        value = dot_nt(w_ref[2 * HALF :, :], xin) + value_bias
        query = query.astype(BF) * jnp.asarray(HEAD_DIM**-0.5, BF)
        value = value.astype(BF)
        for head in range(HALF_HEADS):
            part = slice(head * HEAD_DIM, (head + 1) * HEAD_DIM)
            q_ref[head, side] = query[part, :]
            v_ref[head, :, rows] = value[part, :]
            k_ref[head, rows, :] = dot_nt(
                xin, w_ref[HALF + head * HEAD_DIM : HALF + (head + 1) * HEAD_DIM, :]
            ).astype(BF)
    two.advance(0)

    def attend(step, _):
        head = step // 2
        side = lax.rem(step, 2)
        scores = dot(k_ref[head], q_ref[head, side])
        top = jnp.max(scores, axis=0, keepdims=True)
        shifted = jnp.exp2((scores - top) * LOG2E)
        total = jnp.sum(shifted, axis=0, keepdims=True)
        probs = (shifted * (1.0 / total)).astype(BF)
        out = dot(v_ref[head], probs)
        ctx_ref[head, side] = out
        lse_ref[head, side] = jnp.broadcast_to(top * LOG2E + jnp.log2(total), (8, half))
        cols[side, pl.ds(pl.multiple_of(head * HEAD_DIM, HEAD_DIM), HEAD_DIM), :] = out
        for at in range(1, nbits - 1):
            pl.when(step == min(2 * at - 1, 4))(functools.partial(two.advance, at))
        return 0

    lax.fori_loop(0, 2 * HALF_HEADS, attend, 0)
    outgoing[...] = jnp.transpose(cols[1 - core]).astype(BF)
    copy = remote(outgoing, both_ref.at[core], sems.at[2], sems.at[3], other_core())
    copy.start()
    two.advance(nbits - 1)
    both_ref[core] = jnp.transpose(cols[core]).astype(BF)
    two.finish()
    whole = whole_two[...].reshape(count, 2 * half_two, D)
    wp_ref[...] = picked(
        D,
        whole[:, 0:pad_pro].reshape(count * pad_pro, D),
        lambda index: index,
        n_pro,
        pad_pro,
    )
    we_ref[...] = whole[:, pad_pro : pad_pro + pad_wide]
    wr_ref[...] = whole[:, pad_pro + pad_wide : pad_pro + 2 * pad_wide]
    copy.wait()


def front(weights, modulate, condition, bias, tok, count):
    nbits = count.bit_length() - 1
    n_att, n_pro, n_wide = (w.shape[0] for w in weights[:3])
    half = tok.shape[0]
    full = 2 * half
    half_one = up_to(n_att, 32) // 2
    half_two = up_to(up_to(n_pro, 16) + 2 * up_to(n_wide, 16), 32) // 2
    width = modulate.shape[0]
    lead = (2,) * nbits
    shape = jax.ShapeDtypeStruct
    sems = pltpu.SemaphoreType.DMA
    return pl.pallas_call(
        functools.partial(front_kernel, nbits),
        out_shape=[
            shape((count, 1, 2 * D), F32),
            shape((8, D), F32),
            shape((8, FF), F32),
            shape((D, D), BF),
            shape((count, up_to(n_wide, 16), D), BF),
            shape((count, up_to(n_wide, 16), D), BF),
            shape((3 * HALF, D), BF),
            shape((2, half, D), BF),
            shape((HALF_HEADS, 2, HEAD_DIM, half), BF),
            shape((HALF_HEADS, full, HEAD_DIM), BF),
            shape((HALF_HEADS, HEAD_DIM, full), BF),
            shape((HALF_HEADS, 2, HEAD_DIM, half), F32),
            shape((HALF_HEADS, 2, 8, half), F32),
            shape((2, half, HALF), BF),
        ],
        in_specs=[VM] * 8,
        out_specs=[VM] * 14,
        scratch_shapes=[
            pltpu.VMEM((4,) * (nbits // 2) + (2, half_one, D), BF),
            pltpu.VMEM(lead + (2, half_two, D), BF),
            pltpu.VMEM((2, half, D), BF),
            pltpu.VMEM((2, half, D), F32),
            pltpu.VMEM((1, 2 * D), F32),
            pltpu.VMEM((count, 1, width), F32),
            pltpu.VMEM((count, 1, width), F32),
            pltpu.VMEM((2, HALF, half), F32),
            pltpu.VMEM((half, HALF), BF),
            sems((count,)),
            sems((count,)),
            sems((count,)),
            sems((count,)),
            sems((4,)),
        ]
        + [sems((nbits // 2, 4)), sems((nbits // 2, 4)), sems((2,))]
        + Gather.scratch(nbits),
        compiler_params=params(0),
        name="front",
    )(*weights, modulate, condition, bias, tok)


def branch_kernel(
    ctx_ref,
    tok_ref,
    cot_ref,
    mod_ref,
    wide_ref,
    wp_ref,
    we_ref,
    wr_ref,
    out_ref,
    mid_ref,
    gp_ref,
    ge_ref,
    gr_ref,
    sums_ref,
    wides_ref,
    both_ref,
    outgoing,
    sems,
):
    core = lax.axis_index("ctx")
    signal_core()
    half = tok_ref.shape[0]
    block = 512
    gate_one = mod_ref[2:3, :]
    shift_two = mod_ref[3:4, :]
    scale_two = 1.0 + mod_ref[4:5, :]
    gate_two = mod_ref[5:6, :]
    gp_ref[...] = jnp.zeros_like(gp_ref)
    ge_ref[...] = jnp.zeros_like(ge_ref)
    gr_ref[...] = jnp.zeros_like(gr_ref)
    sums_ref[...] = jnp.zeros_like(sums_ref)
    wides_ref[...] = jnp.zeros_like(wides_ref)

    def step(index, _):
        rows = pl.ds(pl.multiple_of(index * block, block), block)
        ctx = jnp.concatenate([ctx_ref[0, rows, :], ctx_ref[1, rows, :]], axis=1)
        attended = dot_nt(ctx, wp_ref[...]) + mod_ref[6:7, :]
        middle = tok_ref[rows, :].astype(F32) + gate_one * attended
        normed, inverse = normalize(middle)
        expand_in = (normed * scale_two + shift_two).astype(BF)
        hidden = dot_nt(expand_in, we_ref[...]) + wide_ref[0:1, :]
        squared = hidden * hidden
        bend = jnp.tanh(0.7978845608028654 * (hidden + 0.044715 * squared * hidden))
        rise = 0.5 * (1.0 + bend)
        act = (hidden * rise).astype(BF)
        slope = rise + 0.5 * hidden * (1.0 - bend * bend) * (
            0.7978845608028654 * (1.0 + 3.0 * 0.044715 * squared)
        )
        mlp_out = dot(act, wr_ref[...]) + mod_ref[7:8, :]
        out_ref[rows, :] = (middle + gate_two * mlp_out).astype(BF)
        grad_out = cot_ref[rows, :].astype(F32)
        grad_mlp = (gate_two * grad_out).astype(BF)
        gr_ref[...] += dot_tn(act, grad_mlp)
        grad_hidden = (dot_nt(grad_mlp, wr_ref[...]) * slope).astype(BF)
        ge_ref[...] += dot_tn(grad_hidden, expand_in)
        grad_in = dot(grad_hidden, we_ref[...])
        grad_middle = grad_out + norm_back(grad_in * scale_two, normed, inverse)
        mid_ref[rows, :] = grad_middle
        grad_attended = (gate_one * grad_middle).astype(BF)
        gp_ref[...] += dot_tn(grad_attended, ctx)
        back = dot(grad_attended, wp_ref[...]).astype(BF)
        first, second = back[:, :HALF], back[:, HALF:]
        both_ref[core, rows, :] = jnp.where(core == 0, first, second)
        outgoing[rows, :] = jnp.where(core == 0, second, first)
        add = lambda value: jnp.sum(value, axis=0, keepdims=True)
        sums_ref[0:1, :] += add(grad_out * mlp_out)
        sums_ref[1:2, :] += add(grad_in)
        sums_ref[2:3, :] += add(grad_in * normed)
        sums_ref[3:4, :] += add(grad_middle * attended)
        sums_ref[4:5, :] += add(grad_attended.astype(F32))
        sums_ref[5:6, :] += add(grad_mlp.astype(F32))
        wides_ref[0:1, :] += add(grad_hidden.astype(F32))
        return 0

    lax.fori_loop(0, half // block, step, 0)
    copy = remote(outgoing, both_ref.at[core], sems.at[0], sems.at[1], other_core())
    copy.start()
    copy.wait()


def branch(ctx, tok, cot, mod_rows, wide_rows, wp, we, wr):
    half = tok.shape[0]
    shape = jax.ShapeDtypeStruct
    return pl.pallas_call(
        branch_kernel,
        out_shape=[
            shape((half, D), BF),
            shape((half, D), F32),
            shape((D, D), F32),
            shape((FF, D), F32),
            shape((FF, D), F32),
            shape((8, D), F32),
            shape((8, FF), F32),
            shape((2, half, HALF), BF),
        ],
        in_specs=[VM] * 8,
        out_specs=[VM] * 8,
        scratch_shapes=[pltpu.VMEM((half, HALF), BF), pltpu.SemaphoreType.DMA((2,))],
        compiler_params=params(2),
        name="branch",
    )(ctx, tok, cot, mod_rows, wide_rows, wp, we, wr)


def newton_factor(gram, eye, between):
    factor = None
    for sweep in range(NS_ITERS):
        square = dot_three(gram, gram)
        step = newton_a * eye + newton_b * gram + newton_c * square
        if sweep < NS_ITERS - 1:
            gram = dot_three(dot_three(step, gram), step)
        factor = step if factor is None else dot_three(step, factor)
        for act in between.get(sweep, ()):
            act()
    return factor


def gram_of(turned):
    return lax.dot_general(
        turned,
        turned,
        (((0,), (0,)), ((), ())),
        precision=precise,
        preferred_element_type=F32,
    )


TILE = 128


def pack_gram(gram):
    tile = lambda r, c: gram[r * TILE : (r + 1) * TILE, c * TILE : (c + 1) * TILE]
    upper = jnp.concatenate([tile(0, 0), tile(1, 1), tile(2, 2)], axis=1)
    lower = jnp.concatenate([tile(1, 0), tile(2, 0), tile(2, 1)], axis=1)
    return upper, lower


def unpack_gram(upper, lower):
    tile = lambda packed, c: packed[:, c * TILE : (c + 1) * TILE]
    one, two, three = (tile(lower, c) for c in range(3))
    return jnp.concatenate(
        [
            jnp.concatenate([tile(upper, 0), one.T, two.T], axis=1),
            jnp.concatenate([one, tile(upper, 1), three.T], axis=1),
            jnp.concatenate([two, three, tile(upper, 2)], axis=1),
        ],
        axis=0,
    )


class Sum:
    def __init__(self, count, source, landed, whole, extra, send, recv, gsend, grecv, hsend, hrecv):
        self.pieces = source.shape[0]
        self.high = [b for b in range(count.bit_length() - 1) if (1 << b) >= self.pieces]
        self.source, self.landed, self.whole, self.extra = source, landed, whole, extra
        self.sems = send, recv, gsend, grecv, hsend, hrecv
        self.me = lax.axis_index("shard")
        self.low = lax.rem(self.me, self.pieces)

    def peer(self, step):
        place = lax.rem(self.low + step, self.pieces)
        return place, {"shard": self.me - self.low + place}

    def scatter(self, step):
        place, where = self.peer(step)
        send, recv = self.sems[:2]
        return remote(
            self.source.at[place], self.landed.at[self.low], send.at[step], recv.at[step], where
        )

    def spread(self, step):
        _, where = self.peer(step)
        send, recv = self.sems[2:4]
        part = self.whole.at[self.low]
        return remote(part, part, send.at[step], recv.at[step], where)

    def put(self, packed):
        self.source[...] = packed.reshape(self.source.shape)

    def start(self):
        for step in range(1, self.pieces):
            self.scatter(step).start()
        self.landed[self.low] = self.source[self.low]

    def land(self):
        for step in range(1, self.pieces):
            self.scatter(step).wait()
        return jnp.sum(self.landed[...], axis=0)

    def turn(self):
        self.give(self.land())

    def give(self, piece):
        self.whole[self.low] = piece
        send, recv = self.sems[4:]
        for at, bit in enumerate(self.high):
            copy = remote(
                self.whole.at[self.low],
                self.extra.at[at],
                send.at[at],
                recv.at[at],
                {"shard": flip(self.me, bit)},
            )
            copy.start()
            copy.wait()
            self.whole[self.low] += self.extra[at]
        for step in range(1, self.pieces):
            self.spread(step).start()

    def finish(self):
        for step in range(1, self.pieces):
            self.spread(step).wait()

    @staticmethod
    def scratch(count, rows):
        pieces = min(count, 16)
        high = max(count.bit_length() - pieces.bit_length(), 1)
        sems = pltpu.SemaphoreType.DMA
        block = pltpu.VMEM((pieces, rows // pieces, D), F32)
        return [block, block, block, pltpu.VMEM((high, rows // pieces, D), F32)] + [
            sems((pieces,))
        ] * 4 + [sems((high,))] * 2


SUM_REFS = 10


class FourSum:
    def __init__(self, count, source, first, between, second, whole, extra, *sems):
        self.source, self.first, self.between = source, first, between
        self.second, self.whole, self.extra = second, whole, extra
        self.sems = sems
        self.high = range(2, (count.bit_length() - 1) // 2)
        self.me = lax.axis_index("shard")
        self.plane, self.along = digit_of(self.me, 0), digit_of(self.me, 1)

    def copy(self, at, digit, step, pick):
        place, where = digit_peer(self.me, digit, step)
        src, dst = pick(place)
        return remote(src, dst, self.sems[2 * at].at[step], self.sems[2 * at + 1].at[step], where)

    def round(self, at):
        if at == 0:
            pick = lambda place: (self.source.at[:, place], self.first.at[self.plane])
        elif at == 1:
            pick = lambda place: (self.between.at[place], self.second.at[self.along])
        elif at == 2:
            part = self.whole.at[self.along, self.plane]
            pick = lambda place: (part, part)
        else:
            part = self.whole.at[:, self.plane]
            pick = lambda place: (part, part)
        return [self.copy(at, (0, 1, 1, 0)[at], step, pick) for step in range(1, 4)]

    def put(self, packed):
        self.source[...] = packed.reshape(self.source.shape)

    def start(self):
        for copy in self.round(0):
            copy.start()
        self.first[self.plane] = self.source[:, self.plane]

    def along_start(self):
        for copy in self.round(0):
            copy.wait()
        self.between[...] = jnp.sum(self.first[...], axis=0)
        for copy in self.round(1):
            copy.start()
        self.second[self.along] = self.between[self.along]

    def land(self):
        for copy in self.round(1):
            copy.wait()
        return jnp.sum(self.second[...], axis=0)

    def give(self, piece):
        self.whole[self.along, self.plane] = piece
        part = self.whole.at[self.along, self.plane]
        send, recv = self.sems[8:]
        for at, digit in enumerate(self.high):
            copies = []
            for step in range(1, 4):
                _, where = digit_peer(self.me, digit, step)
                slot = 4 * at + step
                copies.append(
                    remote(part, self.extra.at[slot], send.at[slot], recv.at[slot], where)
                )
            for copy in copies:
                copy.start()
            for copy in copies:
                copy.wait()
            for step in range(1, 4):
                self.whole[self.along, self.plane] += self.extra[4 * at + step]
        for copy in self.round(2):
            copy.start()

    def turn(self):
        self.give(self.land())

    def plane_start(self):
        for copy in self.round(2):
            copy.wait()
        for copy in self.round(3):
            copy.start()

    def finish(self):
        for copy in self.round(3):
            copy.wait()

    @staticmethod
    def scratch(count, rows):
        piece = (rows // 16, D)
        high = 4 * max((count.bit_length() - 1) // 2 - 2, 1)
        sems = pltpu.SemaphoreType.DMA
        return [
            pltpu.VMEM((4, 4) + piece, F32),
            pltpu.VMEM((4, 4) + piece, F32),
            pltpu.VMEM((4,) + piece, F32),
            pltpu.VMEM((4,) + piece, F32),
            pltpu.VMEM((4, 4) + piece, F32),
            pltpu.VMEM((high,) + piece, F32),
        ] + [sems((4,))] * 8 + [sems((high,))] * 2


FOUR_REFS = 16


def backward_kernel(
    nbits,
    scale_of,
    dctx_ref,
    xin_ref,
    q_ref,
    k_ref,
    v_ref,
    ctx_ref,
    lse_ref,
    w_ref,
    tok_ref,
    mid_ref,
    mod_ref,
    gp_ref,
    ge_ref,
    gr_ref,
    old_exp,
    old_red,
    sums_in,
    wides_in,
    grad_ref,
    att_ref,
    mine_ref,
    own_ref,
    piece_ref,
    *rest,
):
    stages = rest[:nbits]
    (
        low_out,
        first,
        total,
        k_turn,
        v_rows,
        dk_sum,
        dv_sum,
        dq_low,
        dk_low,
        dv_low,
        gw,
        bias_ref,
        outgoing,
        incoming,
        sems,
        asems,
        send,
        recv,
    ) = rest[nbits:-FOUR_REFS]
    one = FourSum(1 << nbits, *rest[-FOUR_REFS:])
    me = lax.axis_index("shard")
    core = lax.axis_index("ctx")
    signal_all(me, 1 << nbits)
    half = tok_ref.shape[0]
    lead = (slice(None),) * nbits
    wide = ge_ref.shape[-2]
    both = wide + gp_ref.shape[-2]
    last = nbits + 1
    main = lead + (slice(0, wide),)
    side_rows = lead + (slice(wide, both),)
    padded = low_out.shape[-2]
    spots = {1: 0, 2: 2, 3: 4, 4: 5}
    after = range(5, nbits + 2)

    def swap_main(which):
        return remote(
            (gr_ref, ge_ref)[which], first.at[main], send.at[0], recv.at[0], other_core()
        )

    swap_side = remote(gp_ref, first.at[side_rows], send.at[last], recv.at[last], other_core())

    def cube_step(which, step):
        order = scatter_orders(nbits)[which]
        bit = order[step]
        free = order[step + 1 :]
        there = flip(me, bit)
        if step < LOW_STEPS:
            rows = slice(0, padded if which == 0 else up_to(wide, 16))
            source = low_out
        else:
            rows = slice(0, both if which == 0 else wide)
            source = total
        return remote(
            source.at[cube_index(there, nbits, free, (rows,))],
            stages[step].at[(slice(None),) * len(free) + (rows,)],
            send.at[step + 1],
            recv.at[step + 1],
            {"shard": there},
        )

    def send_step(which, step):
        order = scatter_orders(nbits)[which]
        if step < LOW_STEPS:
            rows = slice(0, both if which == 0 else wide)
            index = cube_index(flip(me, order[step]), nbits, order[step + 1 :], (rows,))
            low_out[index] = total[index].astype(BF)
        cube_step(which, step).start()

    def last_swap(which):
        rows = slice(0, both if which == 0 else wide)
        return remote(
            own_ref.at[which, rows],
            own_ref.at[which, rows],
            send.at[nbits + 2],
            recv.at[nbits + 2],
            other_core(),
        )

    def progress(point):
        for which in range(2):

            @pl.when(core == which)
            def _():
                rows = slice(0, both if which == 0 else wide)
                order = scatter_orders(nbits)[which]
                if point == 0:
                    swap_main(which).start()
                    if which == 1:
                        swap_side.start()
                elif point == 1:
                    swap_main(which).wait()
                    if which == 0:
                        swap_side.wait_recv()
                        total[main] = ge_ref[...] + first[main]
                        total[side_rows] = gp_ref[...] + first[side_rows]
                        if padded > both:
                            low_out[lead + (slice(both, padded),)] = jnp.zeros(
                                (2,) * nbits + (padded - both, D), BF
                            )
                    else:
                        swap_side.wait_send()
                        total[main] = gr_ref[...] + first[main]
                elif point <= nbits + 1:
                    step = point - 2
                    cube_step(which, step).wait()
                    free = order[step + 1 :]
                    total[cube_index(me, nbits, free, (rows,))] += stages[step][
                        (slice(None),) * len(free) + (rows,)
                    ].astype(F32)
                if 1 <= point <= nbits:
                    send_step(which, point - 1)
                if point == nbits + 1:
                    own_ref[which, rows] = total[cube_index(me, nbits, (), (rows,))]
                    last_swap(which).start()
                if point == nbits + 2:
                    last_swap(which).wait_send()
                    last_swap(1 - which).wait_recv()

    turn = lambda value: jnp.transpose(value.astype(F32)).astype(BF)
    progress(0)
    for head in range(HALF_HEADS):
        k_turn[...] = turn(k_ref[head])
        v_rows[...] = turn(v_ref[head])
        dk_sum[...] = jnp.zeros_like(dk_sum)
        dv_sum[...] = jnp.zeros_like(dv_sum)

        def step(side, _):
            query = q_ref[head, side]
            down = dctx_ref[side, :, head * HEAD_DIM : (head + 1) * HEAD_DIM]
            down_turn = jnp.transpose(down.astype(F32))
            delta = jnp.sum(down_turn * ctx_ref[head, side], axis=0, keepdims=True)
            scores = dot(k_ref[head], query)
            probs = jnp.exp2(scores * LOG2E - lse_ref[head, side, 0:1, :])
            dv_sum[...] += dot(probs.astype(BF), down)
            grad_probs = dot(v_rows[...], down_turn.astype(BF))
            grad_scores = (probs * (grad_probs - delta)).astype(BF)
            dk_sum[...] += dot(grad_scores, turn(query))
            dq_low[head, side] = (
                jnp.transpose(dot(k_turn[...], grad_scores)) * (HEAD_DIM**-0.5)
            ).astype(BF)
            for at in range(2):
                for point in range(1, 5):
                    if spots[point] == head * 2 + at:
                        pl.when(side == at)(functools.partial(progress, point))
            return 0

        lax.fori_loop(0, 2, step, 0)
        dk_low[head] = dk_sum[...].reshape(2, half, HEAD_DIM).astype(BF)
        dv_low[head] = dv_sum[...].reshape(2, half, HEAD_DIM).astype(BF)

    def side_grads(side, fresh):
        pieces = [dq_low[h, side] for h in range(HALF_HEADS)]
        pieces += [dk_low[h, side] for h in range(HALF_HEADS)]
        pieces += [dv_low[h, side] for h in range(HALF_HEADS)]
        joined = jnp.concatenate(pieces, axis=1)
        grad = dot_tn(joined, xin_ref[side])
        sums = dot(jnp.ones((8, half), BF), joined)
        gw[...] = grad if fresh else gw[...] + grad
        bias_ref[...] = sums if fresh else bias_ref[...] + sums
        return dot(joined, w_ref[...])

    outgoing[...] = side_grads(1 - core, True)
    copy = remote(outgoing, incoming, sems.at[0], sems.at[1], other_core())
    copy.start()
    for point in after:
        progress(point)
    old = jnp.where(core == 0, old_exp[...], old_red[...])
    gram = gram_of(moment_decay * old + own_ref[core, 0:wide, :] * scale_of)
    one.put(jnp.concatenate(pack_gram(gram), axis=0))
    one.start()
    own = side_grads(core, False)

    def share(which):
        return [
            remote(
                att_ref.at[pl.ds(block * D + which * HALF, HALF), :],
                att_ref.at[pl.ds(block * D + which * HALF, HALF), :],
                asems.at[0, block],
                asems.at[1, block],
                other_core(),
            )
            for block in range(3)
        ]

    for which in range(2):

        @pl.when(core == which)
        def _():
            for block in range(3):
                att_ref[block * D + which * HALF : block * D + (which + 1) * HALF, :] = gw[
                    block * HALF : (block + 1) * HALF, :
                ]
            for part in share(which):
                part.start()

    one.along_start()
    copy.wait()
    grad_in = own + incoming[...]
    normed, inverse = normalize(tok_ref[...].astype(F32))
    scale = 1.0 + mod_ref[1:2, :]
    grad_ref[...] = mid_ref[...] + norm_back(grad_in * scale, normed, inverse)
    shift_sum = jnp.sum(grad_in, axis=0, keepdims=True)
    scale_sum = jnp.sum(grad_in * normed, axis=0, keepdims=True)
    row = lambda index: sums_in[index : index + 1, :]
    grad_mod = [shift_sum, scale_sum, row(3), row(1), row(2), row(0)]
    none = jnp.zeros((1, HALF), F32)

    def placed(part):
        return jnp.where(
            core == 0,
            jnp.concatenate([part, none], axis=1),
            jnp.concatenate([none, part], axis=1),
        )

    bias_grad = jnp.concatenate(
        grad_mod
        + [
            placed(bias_ref[0:1, 0:HALF]),
            placed(bias_ref[0:1, 2 * HALF :]),
            row(4),
            wides_in[0:1, :],
            row(5),
        ],
        axis=1,
    )
    grad_mod = jnp.concatenate(grad_mod, axis=1)
    count = 1 << nbits
    nbias, width = bias_grad.shape[1] // count, grad_mod.shape[1] // count
    mine_ref[...] = jnp.zeros_like(mine_ref)
    for to in range(count):
        mine_ref[to, :, 0:nbias] = bias_grad[:, to * nbias : (to + 1) * nbias]
        mine_ref[to, :, D : D + width] = grad_mod[:, to * width : (to + 1) * width]
    for which in range(2):

        @pl.when(core == which)
        def _():
            for part in share(which):
                part.wait_send()
            for part in share(1 - which):
                part.wait_recv()

    progress(nbits + 2)
    piece_ref[...] = one.land()


def attention_backward(
    dctx,
    xin,
    q,
    k,
    v,
    ctx,
    lse,
    weight,
    tok,
    mid,
    mod_rows,
    gp,
    ge,
    gr,
    old_exp,
    old_red,
    sums,
    wides,
    scale,
):
    half = tok.shape[0]
    full = 2 * half
    count, wide, _ = ge.shape
    both = wide + gp.shape[1]
    nbits = count.bit_length() - 1
    lead = (2,) * nbits
    shape = jax.ShapeDtypeStruct
    sems = pltpu.SemaphoreType.DMA
    return pl.pallas_call(
        functools.partial(backward_kernel, nbits, scale),
        out_shape=[
            shape((half, D), F32),
            shape((3 * D, D), F32),
            shape((count, 1, D + up_to(6 * D // count, 128)), F32),
            shape((2, both, D), F32),
            shape((2 * TILE // 16, D), F32),
        ],
        in_specs=[VM] * 18,
        out_specs=[VM] * 5,
        scratch_shapes=[
            pltpu.VMEM((2,) * (nbits - 1 - k) + ((up_to(both, 16), D) if k < LOW_STEPS else (both, D)), BF if k < LOW_STEPS else F32)
            for k in range(nbits)
        ]
        + [
            pltpu.VMEM(lead + (up_to(both, 16), D), BF),
            pltpu.VMEM(lead + (both, D), F32),
            pltpu.VMEM(lead + (both, D), F32),
            pltpu.VMEM((HEAD_DIM, full), BF),
            pltpu.VMEM((full, HEAD_DIM), BF),
            pltpu.VMEM((full, HEAD_DIM), F32),
            pltpu.VMEM((full, HEAD_DIM), F32),
            pltpu.VMEM((HALF_HEADS, 2, half, HEAD_DIM), BF),
            pltpu.VMEM((HALF_HEADS, 2, half, HEAD_DIM), BF),
            pltpu.VMEM((HALF_HEADS, 2, half, HEAD_DIM), BF),
            pltpu.VMEM((3 * HALF, D), F32),
            pltpu.VMEM((8, 3 * HALF), F32),
            pltpu.VMEM((half, D), F32),
            pltpu.VMEM((half, D), F32),
            sems((2,)),
            sems((2, 3)),
            sems((nbits + 3,)),
            sems((nbits + 3,)),
        ]
        + FourSum.scratch(count, 2 * TILE),
        compiler_params=params(3),
        name="attend_backward",
    )(
        dctx,
        xin,
        q,
        k,
        v,
        ctx,
        lse,
        weight,
        tok,
        mid,
        mod_rows,
        gp.reshape(lead + gp.shape[1:]),
        ge.reshape(lead + ge.shape[1:]),
        gr.reshape(lead + gr.shape[1:]),
        old_exp,
        old_red,
        sums,
        wides,
    )


def tail_kernel(
    count,
    scale,
    local,
    att_ref,
    own_ref,
    piece_ref,
    mine_ref,
    small_ref,
    wmod_ref,
    old_mod,
    old_att,
    old_pro,
    fac_ref,
    rows_ref,
    modg_ref,
    bias_ref,
    cond_ref,
    *rest,
):
    digits = (count.bit_length() - 1) // 2
    lands, added = rest[:digits], rest[digits : 2 * digits]
    got, theirs, back_send, back, upper_half, other_half = rest[2 * digits : 2 * digits + 6]
    send, recv, msend, mrecv, bsend, brecv, csem, fsem = rest[2 * digits + 6 : 2 * digits + 14]
    sums = rest[2 * digits + 14 :]
    one = FourSum(count, *sums[:FOUR_REFS])
    two = FourSum(count, *sums[FOUR_REFS : 2 * FOUR_REFS])
    late = Sum(count, *sums[2 * FOUR_REFS :])
    me = lax.axis_index("shard")
    core = lax.axis_index("ctx")
    signal_all(me, count)
    n_att, n_pro, wide = local
    padded = att_ref.shape[-2]
    half_rows = rows_ref.shape[1]

    begin = pl.multiple_of(core * (padded - half_rows), 8)

    def rows_source(digit, place):
        lead = (slice(None),) * (digits - digit - 1) + (place,)
        if digit == 0:
            return att_ref.at[lead + (pl.ds(begin, half_rows),)]
        return added[digit - 1].at[lead]

    def rows_copies(digit):
        copies = []
        for step in range(1, 4):
            place, where = digit_peer(me, digit, step)
            copies.append(
                remote(
                    rows_source(digit, place),
                    lands[digit].at[digit_of(me, digit)],
                    send.at[digit, step],
                    recv.at[digit, step],
                    where,
                )
            )
        return copies

    def rows_start(digit):
        for copy in rows_copies(digit):
            copy.start()
        own = digit_of(me, digit)
        lands[digit][own] = rows_source(digit, own)[...]

    def rows_add(digit):
        for copy in rows_copies(digit):
            copy.wait()
        total = jnp.sum(lands[digit][...], axis=0)
        if digit < digits - 1:
            added[digit][...] = total
            rows_start(digit + 1)
        else:
            rows_ref[core] = total
            swap_rows(core).start()

    def swap_rows(which):
        part = rows_ref.at[which]
        return remote(part, part, csem.at[2], csem.at[3], other_core())

    copies = []
    for step in range(1, count):
        to = lax.rem(me + step, count)
        copy = remote(mine_ref.at[to], got.at[me], msend.at[step], mrecv.at[step], {"shard": to})
        copy.start()
        copies.append(copy)
    got[me] = mine_ref[me]
    one.give(piece_ref[...])
    rows_start(0)
    for copy in copies:
        copy.wait()
    swap = remote(got, theirs, csem.at[0], csem.at[1], other_core())
    swap.start()
    cond = small_ref[:, 0, 0:D]
    silu_low = silu_of(cond).astype(BF).astype(F32)
    one.plane_start()
    swap.wait()
    width = old_mod.shape[0]
    both = got[:, 0, :] + theirs[:, 0, :]
    grad_mod = both[:, D : D + width]
    bias_ref[...] = jnp.sum(both[:, 0:D], axis=0, keepdims=True)
    raw = lax.dot_general(
        grad_mod,
        silu_low,
        (((0,), (0,)), ((), ())),
        precision=precise,
        preferred_element_type=F32,
    )
    modg_ref[...] = raw

    @pl.when(core == 0)
    def _():
        grad = own_ref[0, wide : wide + n_pro, :] * scale
        two.put(jnp.concatenate(pack_gram(gram_of(moment_decay * old_pro[...] + grad)), axis=0))

    @pl.when(core == 1)
    def _():
        grad = modg_ref[...] * scale
        two.put(jnp.concatenate(pack_gram(gram_of(moment_decay * old_mod[...] + grad)), axis=0))

    two.start()
    part = jnp.dot(
        grad_mod, wmod_ref[...].astype(BF).astype(F32), precision=precise, preferred_element_type=F32
    )
    for row in range(count):
        back_send[row] = part[row : row + 1, :]
    back[me] = back_send[me]
    backs = []
    for step in range(1, count):
        to = lax.rem(me + step, count)
        copy = remote(
            back_send.at[to], back.at[me], bsend.at[step], brecv.at[step], {"shard": to}
        )
        copy.start()
        backs.append(copy)

    def condition_grads():
        for copy in backs:
            copy.wait()
        grad_silu = jnp.sum(back[...], axis=0)
        own = small_ref[me][:, 0:D]
        gate = jax.nn.sigmoid(own)
        cond_ref[...] = grad_silu * (gate + own * gate * (1.0 - gate))

    def late_start():
        swap_rows(core).wait_send()
        swap_rows(1 - core).wait_recv()
        skip = 2 * half_rows - padded
        grad = jnp.concatenate([rows_ref[0], rows_ref[1, skip:]], axis=0)[0:n_att] * scale
        upper, lower = pack_gram(gram_of(moment_decay * old_att[...] + grad))
        late.put(jnp.where(core == 0, upper, lower))
        late.start()

    halves = remote(upper_half, other_half, csem.at[4], csem.at[5], other_core())

    def late_swap():
        late.finish()
        upper_half[...] = late.whole[...].reshape(TILE, D)
        halves.start()

    row = lax.broadcasted_iota(jnp.int32, (D, D), 0)
    column = lax.broadcasted_iota(jnp.int32, (D, D), 1)
    eye = (row == column).astype(F32)

    def solve(gram, between):
        diagonal = jnp.sum(gram * eye, axis=0, keepdims=True)
        size = 1.0 / (jnp.sqrt(jnp.sum(diagonal, axis=1, keepdims=True)) + 1e-07)
        return newton_factor((gram * size) * size, eye, between) * size

    def solve_sum(item, between):
        packed = item.whole[...].reshape(2 * TILE, D)
        return solve(unpack_gram(packed[0:TILE], packed[TILE:]), between)

    def pass_factor(index, at):
        part = fac_ref.at[index]
        return remote(part, part, fsem.at[0, at], fsem.at[1, at], other_core())

    place_one, place_two = 3 + core, 2 - 2 * core
    rows_add(0)
    one.finish()
    last_rows = [functools.partial(rows_add, digit) for digit in range(1, digits)]
    fac_ref[place_one] = solve_sum(
        one,
        {
            0: [two.along_start],
            1: last_rows,
            2: [late_start, two.turn],
            3: [condition_grads, two.plane_start],
            4: [late.turn],
        },
    )
    first_pass = pass_factor(place_one, 0)
    first_pass.start()
    two.finish()
    fac_ref[place_two] = solve_sum(two, {1: [late_swap]})
    second_pass = pass_factor(place_two, 1)
    second_pass.start()
    halves.wait()
    mine_half, their_half = upper_half[...], other_half[...]
    fac_ref[1] = solve(
        unpack_gram(
            jnp.where(core == 0, mine_half, their_half),
            jnp.where(core == 0, their_half, mine_half),
        ),
        {},
    )
    first_pass.wait()
    second_pass.wait()


def tail(att, own, piece, mine, small_all, wmod, olds, scale, local):
    count, padded, _ = att.shape
    digits = (count.bit_length() - 1) // 2
    half_rows = up_to(padded // 2, 8)
    width = wmod.shape[0]
    sems = pltpu.SemaphoreType.DMA
    shape = jax.ShapeDtypeStruct
    return pl.pallas_call(
        functools.partial(tail_kernel, count, scale, local),
        out_shape=[
            shape((5, D, D), F32),
            shape((2, half_rows, D), F32),
            shape((width, D), F32),
            shape((1, D), F32),
            shape((1, D), F32),
        ],
        in_specs=[VM] * 9,
        out_specs=[VM] * 5,
        scratch_shapes=[
            pltpu.VMEM((4,) * (digits - d) + (half_rows, D), F32) for d in range(digits)
        ]
        + [pltpu.VMEM((4,) * (digits - d - 1) + (half_rows, D), F32) for d in range(digits)]
        + [
            pltpu.VMEM(mine.shape, F32),
            pltpu.VMEM(mine.shape, F32),
            pltpu.VMEM((count, 1, D), F32),
            pltpu.VMEM((count, 1, D), F32),
            pltpu.VMEM((TILE, D), F32),
            pltpu.VMEM((TILE, D), F32),
            sems((digits, 4)),
            sems((digits, 4)),
            sems((count,)),
            sems((count,)),
            sems((count,)),
            sems((count,)),
            sems((6,)),
            sems((2, 2)),
        ]
        + FourSum.scratch(count, 2 * TILE)
        + FourSum.scratch(count, 2 * TILE)
        + Sum.scratch(count, TILE),
        compiler_params=params(4),
        name="tail",
    )(att.reshape((4,) * digits + (padded, D)), own, piece, mine, small_all, wmod, *olds[:3])


def update_kernel(scale, rates, bounds, *refs):
    fac_ref, att_ref, modg_ref, own_ref = refs[:4]
    olds, masters, outs = refs[4:9], refs[9:14], refs[14:]
    n_att, wide, n_pro = bounds
    first_rows = att_ref.shape[1]
    skip = 2 * first_rows - up_to(n_att, 8)
    joined = jnp.concatenate([att_ref[0], att_ref[1, skip:]], axis=0)
    grads = [
        modg_ref[...],
        joined[0:n_att],
        own_ref[0, wide : wide + n_pro, :],
        own_ref[0, 0:wide, :],
        own_ref[1, 0:wide, :],
    ]
    for index in range(5):
        grad = grads[index] * scale
        moment = moment_decay * olds[index][...] + grad
        direction = dot_three(moment, fac_ref[index])
        outs[3 * index][...] = grad
        outs[3 * index + 1][...] = masters[index][...] - rates[index] * direction
        outs[3 * index + 2][...] = moment


def update(fac, att, modg, own, olds, masters, scale, count):
    shape = jax.ShapeDtypeStruct
    out = []
    for m in masters:
        out += [shape(m.shape, F32)] * 3
    rates = [matrix_rate * 0.2 * math.sqrt(max(D, m.shape[0] * count)) for m in masters]
    bounds = (olds[1].shape[0], olds[3].shape[0], olds[2].shape[0])
    return pl.pallas_call(
        functools.partial(update_kernel, scale, rates, bounds),
        out_shape=out,
        in_specs=[VM] * 14,
        out_specs=[VM] * 15,
        compiler_params=params(),
        name="update",
    )(fac, att, modg, own, *olds, *masters)


def on_device(
    tokens,
    condition,
    cotangent,
    modulate_weight,
    attend_weight,
    project_weight,
    expand_weight,
    reduce_weight,
    bias_flat,
    modulate_moment,
    attend_moment,
    project_moment,
    expand_moment,
    reduce_moment,
    bias_moment,
):
    count = lax.axis_size("shard")
    full = tokens.shape[1] * lax.axis_size("ctx")
    olds = [
        m.T
        for m in (modulate_moment, attend_moment, project_moment, expand_moment, reduce_moment)
    ]
    masters = [
        w.T
        for w in (modulate_weight, attend_weight, project_weight, expand_weight, reduce_weight)
    ]
    n_att, n_pro, n_wide = (w.shape[0] for w in masters[1:4])
    nbias = bias_flat.shape[0]
    tok = tokens[0]
    (
        small_all,
        mod_rows,
        wide_rows,
        project_turn,
        expand_turn,
        reduce_turn,
        weight_core,
        xin,
        q,
        k,
        v,
        ctx_turn,
        lse,
        ctx,
    ) = front(masters[1:], masters[0], condition, bias_flat[None], tok, count)
    block_out, mid, gp, ge, gr, sums, wides, dctx = branch(
        ctx,
        tok,
        cotangent[0],
        mod_rows,
        wide_rows,
        project_turn,
        expand_turn[:, :n_wide].reshape(FF, D),
        reduce_turn[:, :n_wide].reshape(FF, D),
    )
    gp = pad_rows(gp.reshape(count, n_pro, D), up_to(n_pro, 8))
    scale = 1.0 / math.sqrt(tokens.shape[0] * count * full)
    tokens_grad, att, mine, mlp_rows, piece = attention_backward(
        dctx,
        xin,
        q,
        k,
        v,
        ctx_turn,
        lse,
        weight_core,
        tok,
        mid,
        mod_rows,
        gp,
        ge.reshape(count, n_wide, D),
        gr.reshape(count, n_wide, D),
        olds[3],
        olds[4],
        sums,
        wides,
        scale,
    )
    att = pad_rows(att.reshape(count, n_att, D), up_to(n_att, 8))
    fac, att_rows, modg, bias_sum, condition_rows = tail(
        att, mlp_rows, piece, mine, small_all, masters[0], olds, scale, (n_att, n_pro, n_wide)
    )
    out = update(fac, att_rows, modg, mlp_rows, olds, masters, scale, count)
    bias_grad = bias_sum[0, :nbias] * scale
    bias_new = moment_decay * bias_moment + bias_grad
    result = [block_out[None], tokens_grad[None], condition_rows]
    result += [value.T for value in out]
    result += [bias_grad, bias_flat - bias_rate * bias_new, bias_new]
    return tuple(result)


def solution(mesh):
    tok = P("shard", "ctx", None)
    row = P("shard", None)
    col = P(None, "shard")
    flat = P("shard")
    return jax.shard_map(
        on_device,
        mesh=mesh,
        in_specs=(tok, row, tok) + (col,) * 5 + (flat,) + (col,) * 5 + (flat,),
        out_specs=(tok, tok, row) + (col,) * 15 + (flat,) * 3,
        check_vma=False,
    )
```

```python
import functools
import math

import jax
import jax.numpy as jnp
from jax import lax
from jax.experimental import pallas as pl
from jax.experimental.pallas import tpu as pltpu
from jax.sharding import PartitionSpec as P

D = 384
FF = 1536
HEADS = 6
HEAD_DIM = 64
NS_ITERS = 5
LOW_STEPS = 1
HALF_HEADS = HEADS // 2
HALF = HALF_HEADS * HEAD_DIM

norm_eps = 1e-06
newton_a = 3.4445
newton_b = -4.775
newton_c = 2.0315
moment_decay = 0.95
matrix_rate = 0.5
bias_rate = 0.1
precise = lax.Precision.HIGHEST
LOG2E = 1.4426950408889634

MESH = pl.DeviceIdType.MESH
BF = jnp.bfloat16
F32 = jnp.float32
VM = pl.BlockSpec(memory_space=pltpu.VMEM)
FAR = pl.BlockSpec(memory_space=pltpu.HBM)


def params(megabytes, collective=None):
    limit = megabytes * 2**20
    if collective is None:
        return pltpu.CompilerParams(vmem_limit_bytes=limit)
    return pltpu.CompilerParams(
        collective_id=collective, has_side_effects=True, vmem_limit_bytes=limit
    )


def dot(left, right):
    return jnp.dot(left, right, preferred_element_type=F32)


def dot_nt(left, right):
    return lax.dot_general(left, right, (((1,), (1,)), ((), ())), preferred_element_type=F32)


def dot_tn(left, right):
    return lax.dot_general(left, right, (((0,), (0,)), ((), ())), preferred_element_type=F32)


def split_low(values):
    high = values.astype(BF)
    return high, (values - high.astype(F32)).astype(BF)


def dot_three(left, right, op=dot):
    left_high, left_low = split_low(left)
    right_high, right_low = split_low(right)
    return op(left_high, right_high) + (op(left_high, right_low) + op(left_low, right_high))


def silu_of(values):
    return values * jax.nn.sigmoid(values)


def normalize(values):
    centered = values - jnp.mean(values, axis=-1, keepdims=True)
    inverse = lax.rsqrt(jnp.mean(centered * centered, axis=-1, keepdims=True) + norm_eps)
    return (centered * inverse, inverse)


def norm_back(grad_normed, normed, inverse):
    first = jnp.mean(grad_normed, axis=-1, keepdims=True)
    second = jnp.mean(grad_normed * normed, axis=-1, keepdims=True)
    return (grad_normed - first - normed * second) * inverse


def pad_rows(array, rows):
    return jnp.pad(array, ((0, 0),) * (array.ndim - 2) + ((0, rows - array.shape[-2]), (0, 0)))


def up_to(value, step):
    return -(-value // step) * step


def bit_of(value, bit):
    return lax.rem(value // (1 << bit), 2)


def flip(me, bit):
    return me + (1 - 2 * bit_of(me, bit)) * (1 << bit)


def other_core():
    return {"ctx": 1 - lax.axis_index("ctx")}


def signal_cube(me, nbits):
    sem = pltpu.get_barrier_semaphore()
    for bit in range(nbits):
        pl.semaphore_signal(
            sem, inc=1, device_id={"shard": flip(me, bit)}, device_id_type=MESH
        )
    pl.semaphore_signal(sem, inc=1, device_id=other_core(), device_id_type=MESH)
    pl.semaphore_wait(sem, nbits + 1)


def signal_all(me, count):
    sem = pltpu.get_barrier_semaphore()
    for step in range(1, count):
        pl.semaphore_signal(
            sem, inc=1, device_id={"shard": lax.rem(me + step, count)}, device_id_type=MESH
        )
    pl.semaphore_signal(sem, inc=1, device_id=other_core(), device_id_type=MESH)
    pl.semaphore_wait(sem, count)


def signal_core():
    sem = pltpu.get_barrier_semaphore()
    pl.semaphore_signal(sem, inc=1, device_id=other_core(), device_id_type=MESH)
    pl.semaphore_wait(sem, 1)


def remote(src, dst, send, recv, where):
    return pltpu.make_async_remote_copy(
        src, dst, send, recv, device_id=where, device_id_type=MESH
    )


def orders(nbits):
    up = list(range(nbits))
    return up, ([1, 0] + up[2:] if nbits >= 2 else up)


def scatter_orders(nbits):
    up = list(range(nbits))
    return up, (up[1:] + up[:1] if nbits >= 2 else up)


def digit_of(value, digit):
    return lax.rem(value // (1 << (2 * digit)), 4)


def digit_peer(me, digit, step):
    own = digit_of(me, digit)
    place = lax.rem(own + step, 4)
    return place, {"shard": me + (place - own) * (1 << (2 * digit))}


def cube_index(who, nbits, free, tail=()):
    lead = tuple(
        slice(None) if (nbits - 1 - d) in free else bit_of(who, nbits - 1 - d)
        for d in range(nbits)
    )
    return lead + tuple(tail)


class Gather:
    def __init__(self, nbits, whole, send, recv, psend, precv):
        self.nbits, self.whole = nbits, whole
        self.sems = send, recv, psend, precv
        self.me = lax.axis_index("shard")

    def step(self, which, at):
        seq = orders(self.nbits)[which][::-1]
        bit = seq[at]
        part = self.whole.at[cube_index(self.me, self.nbits, seq[:at], (which,))]
        send, recv = self.sems[:2]
        return remote(part, part, send.at[at], recv.at[at], {"shard": flip(self.me, bit)})

    def forward(self, which, at):
        seq = orders(self.nbits)[which][::-1]
        bit = seq[at]
        part = self.whole.at[
            cube_index(flip(self.me, bit), self.nbits, seq[:at], (which,))
        ]
        send, recv = self.sems[2:]
        return remote(part, part, send.at[at], recv.at[at], other_core())

    def each(self, act):
        for which in range(2):
            pl.when(lax.axis_index("ctx") == which)(functools.partial(act, which))

    def start(self):
        self.each(lambda which: self.step(which, 0).start())

    def advance(self, at):
        def act(which):
            self.step(which, at).wait()
            if at + 1 < self.nbits:
                self.step(which, at + 1).start()
            self.forward(which, at).start()

        self.each(act)

    def finish(self):
        def act(which):
            for at in range(self.nbits):
                self.forward(which, at).wait_send()
            for at in range(self.nbits):
                self.forward(1 - which, at).wait_recv()

        self.each(act)

    @staticmethod
    def scratch(nbits):
        return [pltpu.SemaphoreType.DMA((nbits,))] * 4


class FourGather:
    def __init__(self, digits, whole, send, recv, swap):
        self.digits, self.whole = digits, whole
        self.sems, self.swap = (send, recv), swap
        self.me = lax.axis_index("shard")
        self.core = lax.axis_index("ctx")

    def round(self, at):
        digit = self.digits - 1 - at
        own = tuple(digit_of(self.me, d) for d in range(digit, -1, -1))
        part = self.whole.at[(slice(None),) * at + own + (self.core,)]
        send, recv = self.sems
        copies = []
        for step in range(1, 4):
            _, where = digit_peer(self.me, digit, step)
            copies.append(remote(part, part, send.at[at, step], recv.at[at, step], where))
        return copies

    def start(self, at):
        for copy in self.round(at):
            copy.start()

    def wait(self, at):
        for copy in self.round(at):
            copy.wait()

    def forward(self):
        part = self.whole.at[(slice(None),) * self.digits + (self.core,)]
        return remote(part, part, self.swap.at[0], self.swap.at[1], other_core())


def front_kernel(
    nbits,
    att_far,
    pro_far,
    exp_far,
    red_far,
    mod_far,
    cond_ref,
    bias_ref,
    tok_ref,
    small_all,
    rows_ref,
    wide_ref,
    wp_ref,
    we_ref,
    wr_ref,
    w_ref,
    xin_ref,
    q_ref,
    k_ref,
    v_ref,
    ctx_ref,
    lse_ref,
    both_ref,
    whole_one,
    whole_two,
    tok_all,
    normed_all,
    small_own,
    mod_all,
    mod_send,
    cols,
    outgoing,
    att_own,
    pro_own,
    exp_own,
    red_own,
    mod_own,
    ssend,
    srecv,
    msend,
    mrecv,
    sems,
    near,
    *gsems,
):
    count = 1 << nbits
    me = lax.axis_index("shard")
    core = lax.axis_index("ctx")
    loads = [
        pltpu.make_async_copy(far, own, near.at[at])
        for at, (far, own) in enumerate(
            [
                (att_far, att_own),
                (pro_far, pro_own),
                (exp_far, exp_own),
                (red_far, red_own),
                (mod_far, mod_own),
                (tok_ref, tok_all.at[core]),
            ]
        )
    ]
    for load in loads:
        load.start()
    signal_all(me, count)
    n_att, n_pro, n_wide = att_own.shape[0], pro_own.shape[0], exp_own.shape[0]
    width, nbias = mod_own.shape[0], bias_ref.shape[1]
    half = tok_ref.shape[0]
    digits = nbits // 2
    own = cube_index(me, nbits, ())
    one = FourGather(digits, whole_one, *gsems[:3])
    two = Gather(nbits, whole_two, *gsems[3:])
    half_one, half_two = whole_one.shape[-2], whole_two.shape[-2]
    pad_pro, pad_wide = up_to(n_pro, 16), up_to(n_wide, 16)

    def joined(parts, total):
        pieces = []
        for part, rows in parts:
            pieces.append(part[...])
            if rows > part.shape[0]:
                pieces.append(jnp.zeros((rows - part.shape[0], D), F32))
        rows = sum(rows for _, rows in parts)
        if total > rows:
            pieces.append(jnp.zeros((total - rows, D), F32))
        return jnp.concatenate(pieces, axis=0).astype(BF)

    small_own[...] = jnp.zeros_like(small_own)
    small_own[:, 0:D] = cond_ref[...].astype(F32)
    small_own[:, D : D + nbias] = bias_ref[...].astype(BF).astype(F32)
    spread = []
    for step in range(1, count):
        to = lax.rem(me + step, count)
        copy = remote(
            small_own, small_all.at[me], ssend.at[step], srecv.at[step], {"shard": to}
        )
        copy.start()
        spread.append(copy)
    for load in loads:
        load.wait()
    halves = joined([(att_own, n_att)], 2 * half_one)
    place = tuple(digit_of(me, d) for d in range(digits - 1, -1, -1))
    whole_one[place + (core,)] = jnp.where(core == 0, halves[:half_one], halves[half_one:])
    one.start(0)
    toks = remote(tok_ref, tok_all.at[core], sems.at[0], sems.at[1], other_core())
    toks.start()
    small_all[me] = small_own[...]
    whole_two[own] = joined(
        [(pro_own, pad_pro), (exp_own, pad_wide), (red_own, pad_wide)], 2 * half_two
    ).reshape(2, half_two, D)
    block = 256

    def norm_side(side):
        def norm_block(index, _):
            rows = pl.ds(pl.multiple_of(index * block, block), block)
            normed, _inverse = normalize(tok_all[side, rows, :].astype(F32))
            normed_all[side, rows, :] = normed
            return 0

        lax.fori_loop(0, half // block, norm_block, 0)

    one.wait(0)
    one.start(1)
    for copy in spread:
        copy.wait()
    silu_low = silu_of(small_all[:, 0, 0:D]).astype(BF)
    part = dot_nt(silu_low, mod_own[...].astype(BF))
    for row in range(count):
        mod_send[row] = part[row : row + 1, :]
    mods = []
    for step in range(1, count):
        to = lax.rem(me + step, count)
        copy = remote(
            mod_send.at[to], mod_all.at[me], msend.at[step], mrecv.at[step], {"shard": to}
        )
        copy.start()
        mods.append(copy)
    mod_all[me] = mod_send[me]
    norm_side(core)
    toks.wait()
    norm_side(1 - core)
    biases = jnp.concatenate([small_all[s, :, D : D + nbias] for s in range(count)], axis=1)
    for at in range(1, digits):
        one.wait(at)
        if at + 1 < digits:
            one.start(at + 1)
    forward = one.forward()
    forward.start()
    two.start()
    for copy in mods:
        copy.wait()
    mods = jnp.concatenate([mod_all[s] for s in range(count)], axis=1)
    mods = mods + biases[:, 0 : 6 * D]
    rows_ref[...] = jnp.zeros_like(rows_ref)
    for row in range(6):
        rows_ref[row : row + 1, :] = mods[:, row * D : (row + 1) * D]
    rows_ref[6:7, :] = biases[:, 8 * D : 9 * D]
    rows_ref[7:8, :] = biases[:, 9 * D + FF :]
    wide_ref[...] = jnp.broadcast_to(biases[:, 9 * D : 9 * D + FF], (8, FF))
    shift = mods[:, 0:D]
    scale = 1.0 + mods[:, D : 2 * D]

    def shift_block(index, _):
        rows = pl.ds(pl.multiple_of(index * block, block), block)
        for side in range(2):
            xin_ref[side, rows, :] = (normed_all[side, rows, :] * scale + shift).astype(BF)
        return 0

    lax.fori_loop(0, half // block, shift_block, 0)

    def turned_bias(at):
        row = biases[:, at * D : (at + 1) * D]
        row = jnp.where(core == 0, row[:, 0:HALF], row[:, HALF:])
        return jnp.transpose(jnp.broadcast_to(row, (8, HALF)))[:, 0:1]

    query_bias, value_bias = turned_bias(6), turned_bias(7)

    def picked(rows, source, wanted, local, stride):
        index = lax.broadcasted_iota(jnp.int32, (rows, 1), 0)
        goal = wanted(index).astype(F32)
        block_of = jnp.floor((goal + 0.5) * (1.0 / local))
        place = goal + block_of * float(stride - local)
        column = lax.broadcasted_iota(jnp.int32, (rows, source.shape[0]), 1).astype(F32)
        return dot((column == place).astype(BF), source).astype(BF)

    forward.wait()
    for part in range(3):
        w_ref[part * HALF : (part + 1) * HALF, :] = picked(
            HALF,
            whole_one[...].reshape(count * 2 * half_one, D),
            lambda index: index + (part * D + core * HALF),
            n_att,
            2 * half_one,
        )
    for side in range(2):
        xin = xin_ref[side]
        rows = pl.ds(side * half, half)
        query = dot_nt(w_ref[0:HALF, :], xin) + query_bias
        value = dot_nt(w_ref[2 * HALF :, :], xin) + value_bias
        query = query.astype(BF) * jnp.asarray(HEAD_DIM**-0.5, BF)
        value = value.astype(BF)
        for head in range(HALF_HEADS):
            part = slice(head * HEAD_DIM, (head + 1) * HEAD_DIM)
            q_ref[head, side] = query[part, :]
            v_ref[head, :, rows] = value[part, :]
            k_ref[head, rows, :] = dot_nt(
                xin, w_ref[HALF + head * HEAD_DIM : HALF + (head + 1) * HEAD_DIM, :]
            ).astype(BF)
    two.advance(0)

    def attend(step, _):
        head = step // 2
        side = lax.rem(step, 2)
        scores = dot(k_ref[head], q_ref[head, side])
        top = jnp.max(scores, axis=0, keepdims=True)
        shifted = jnp.exp2((scores - top) * LOG2E)
        total = jnp.sum(shifted, axis=0, keepdims=True)
        probs = (shifted * (1.0 / total)).astype(BF)
        out = dot(v_ref[head], probs)
        ctx_ref[head, side] = out
        lse_ref[head, side] = jnp.broadcast_to(top * LOG2E + jnp.log2(total), (8, half))
        cols[side, pl.ds(pl.multiple_of(head * HEAD_DIM, HEAD_DIM), HEAD_DIM), :] = out
        for at in range(1, nbits - 1):
            pl.when(step == min(2 * at - 1, 4))(functools.partial(two.advance, at))
        return 0

    lax.fori_loop(0, 2 * HALF_HEADS, attend, 0)
    outgoing[...] = jnp.transpose(cols[1 - core]).astype(BF)
    copy = remote(outgoing, both_ref.at[core], sems.at[2], sems.at[3], other_core())
    copy.start()
    two.advance(nbits - 1)
    both_ref[core] = jnp.transpose(cols[core]).astype(BF)
    two.finish()
    whole = whole_two[...].reshape(count, 2 * half_two, D)
    wp_ref[...] = picked(
        D,
        whole[:, 0:pad_pro].reshape(count * pad_pro, D),
        lambda index: index,
        n_pro,
        pad_pro,
    )
    we_ref[...] = whole[:, pad_pro : pad_pro + pad_wide]
    wr_ref[...] = whole[:, pad_pro + pad_wide : pad_pro + 2 * pad_wide]
    copy.wait()


def front(weights, modulate, condition, bias, tok, count):
    far = lambda array: pltpu.with_memory_space_constraint(array, pltpu.HBM)
    weights, modulate, tok = [far(w) for w in weights], far(modulate), far(tok)
    nbits = count.bit_length() - 1
    n_att, n_pro, n_wide = (w.shape[0] for w in weights[:3])
    half = tok.shape[0]
    full = 2 * half
    half_one = up_to(n_att, 32) // 2
    half_two = up_to(up_to(n_pro, 16) + 2 * up_to(n_wide, 16), 32) // 2
    width = modulate.shape[0]
    lead = (2,) * nbits
    shape = jax.ShapeDtypeStruct
    sems = pltpu.SemaphoreType.DMA
    return pl.pallas_call(
        functools.partial(front_kernel, nbits),
        out_shape=[
            shape((count, 1, 2 * D), F32),
            shape((8, D), F32),
            shape((8, FF), F32),
            shape((D, D), BF),
            shape((count, up_to(n_wide, 16), D), BF),
            shape((count, up_to(n_wide, 16), D), BF),
            shape((3 * HALF, D), BF),
            shape((2, half, D), BF),
            shape((HALF_HEADS, 2, HEAD_DIM, half), BF),
            shape((HALF_HEADS, full, HEAD_DIM), BF),
            shape((HALF_HEADS, HEAD_DIM, full), BF),
            shape((HALF_HEADS, 2, HEAD_DIM, half), F32),
            shape((HALF_HEADS, 2, 8, half), F32),
            shape((2, half, HALF), BF),
        ],
        in_specs=[FAR] * 5 + [VM] * 2 + [FAR],
        out_specs=[VM] * 14,
        scratch_shapes=[
            pltpu.VMEM((4,) * (nbits // 2) + (2, half_one, D), BF),
            pltpu.VMEM(lead + (2, half_two, D), BF),
            pltpu.VMEM((2, half, D), BF),
            pltpu.VMEM((2, half, D), F32),
            pltpu.VMEM((1, 2 * D), F32),
            pltpu.VMEM((count, 1, width), F32),
            pltpu.VMEM((count, 1, width), F32),
            pltpu.VMEM((2, HALF, half), F32),
            pltpu.VMEM((half, HALF), BF),
            *[pltpu.VMEM(w.shape, F32) for w in (*weights, modulate)],
            sems((count,)),
            sems((count,)),
            sems((count,)),
            sems((count,)),
            sems((4,)),
            sems((6,)),
        ]
        + [sems((nbits // 2, 4)), sems((nbits // 2, 4)), sems((2,))]
        + Gather.scratch(nbits),
        compiler_params=params(24, 0),
        name="front",
    )(*weights, modulate, condition, bias, tok)


def branch_kernel(
    ctx_ref,
    tok_ref,
    cot_ref,
    mod_ref,
    wide_ref,
    wp_ref,
    we_ref,
    wr_ref,
    out_ref,
    mid_ref,
    gp_ref,
    ge_ref,
    gr_ref,
    sums_ref,
    wides_ref,
    both_ref,
    outgoing,
    sems,
):
    core = lax.axis_index("ctx")
    signal_core()
    half = tok_ref.shape[0]
    block = 512
    gate_one = mod_ref[2:3, :]
    shift_two = mod_ref[3:4, :]
    scale_two = 1.0 + mod_ref[4:5, :]
    gate_two = mod_ref[5:6, :]
    gp_ref[...] = jnp.zeros_like(gp_ref)
    ge_ref[...] = jnp.zeros_like(ge_ref)
    gr_ref[...] = jnp.zeros_like(gr_ref)
    sums_ref[...] = jnp.zeros_like(sums_ref)
    wides_ref[...] = jnp.zeros_like(wides_ref)

    def step(index, _):
        rows = pl.ds(pl.multiple_of(index * block, block), block)
        ctx = jnp.concatenate([ctx_ref[0, rows, :], ctx_ref[1, rows, :]], axis=1)
        attended = dot_nt(ctx, wp_ref[...]) + mod_ref[6:7, :]
        middle = tok_ref[rows, :].astype(F32) + gate_one * attended
        normed, inverse = normalize(middle)
        expand_in = (normed * scale_two + shift_two).astype(BF)
        hidden = dot_nt(expand_in, we_ref[...]) + wide_ref[0:1, :]
        squared = hidden * hidden
        bend = jnp.tanh(0.7978845608028654 * (hidden + 0.044715 * squared * hidden))
        rise = 0.5 * (1.0 + bend)
        act = (hidden * rise).astype(BF)
        slope = rise + 0.5 * hidden * (1.0 - bend * bend) * (
            0.7978845608028654 * (1.0 + 3.0 * 0.044715 * squared)
        )
        mlp_out = dot(act, wr_ref[...]) + mod_ref[7:8, :]
        out_ref[rows, :] = (middle + gate_two * mlp_out).astype(BF)
        grad_out = cot_ref[rows, :].astype(F32)
        grad_mlp = (gate_two * grad_out).astype(BF)
        gr_ref[...] += dot_tn(act, grad_mlp)
        grad_hidden = (dot_nt(grad_mlp, wr_ref[...]) * slope).astype(BF)
        ge_ref[...] += dot_tn(grad_hidden, expand_in)
        grad_in = dot(grad_hidden, we_ref[...])
        grad_middle = grad_out + norm_back(grad_in * scale_two, normed, inverse)
        mid_ref[rows, :] = grad_middle
        grad_attended = (gate_one * grad_middle).astype(BF)
        gp_ref[...] += dot_tn(grad_attended, ctx)
        back = dot(grad_attended, wp_ref[...]).astype(BF)
        first, second = back[:, :HALF], back[:, HALF:]
        both_ref[core, rows, :] = jnp.where(core == 0, first, second)
        outgoing[rows, :] = jnp.where(core == 0, second, first)
        add = lambda value: jnp.sum(value, axis=0, keepdims=True)
        sums_ref[0:1, :] += add(grad_out * mlp_out)
        sums_ref[1:2, :] += add(grad_in)
        sums_ref[2:3, :] += add(grad_in * normed)
        sums_ref[3:4, :] += add(grad_middle * attended)
        sums_ref[4:5, :] += add(grad_attended.astype(F32))
        sums_ref[5:6, :] += add(grad_mlp.astype(F32))
        wides_ref[0:1, :] += add(grad_hidden.astype(F32))
        return 0

    lax.fori_loop(0, half // block, step, 0)
    copy = remote(outgoing, both_ref.at[core], sems.at[0], sems.at[1], other_core())
    copy.start()
    copy.wait()


def branch(ctx, tok, cot, mod_rows, wide_rows, wp, we, wr):
    half = tok.shape[0]
    shape = jax.ShapeDtypeStruct
    return pl.pallas_call(
        branch_kernel,
        out_shape=[
            shape((half, D), BF),
            shape((half, D), F32),
            shape((D, D), F32),
            shape((FF, D), F32),
            shape((FF, D), F32),
            shape((8, D), F32),
            shape((8, FF), F32),
            shape((2, half, HALF), BF),
        ],
        in_specs=[VM] * 8,
        out_specs=[VM] * 8,
        scratch_shapes=[pltpu.VMEM((half, HALF), BF), pltpu.SemaphoreType.DMA((2,))],
        compiler_params=params(28, 2),
        name="branch",
    )(ctx, tok, cot, mod_rows, wide_rows, wp, we, wr)


def long_left(values):
    high, low = split_low(values)
    return jnp.concatenate([high, high, low], axis=1)


def long_right(values):
    high, low = split_low(values)
    return jnp.concatenate([high, low, high], axis=0)


def newton_factor(gram, eye, between):
    factor = None
    for sweep in range(NS_ITERS):
        right = long_right(gram)
        step = newton_a * eye + newton_b * gram + newton_c * dot(long_left(gram), right)
        left = long_left(step)
        if sweep < NS_ITERS - 1:
            gram = dot(long_left(dot(left, right)), long_right(step))
        factor = step if factor is None else dot(left, long_right(factor))
        for act in between.get(sweep, ()):
            act()
    return factor


def gram_of(turned):
    return lax.dot_general(
        turned,
        turned,
        (((0,), (0,)), ((), ())),
        precision=precise,
        preferred_element_type=F32,
    )


TILE = 128


def pack_gram(gram):
    tile = lambda r, c: gram[r * TILE : (r + 1) * TILE, c * TILE : (c + 1) * TILE]
    upper = jnp.concatenate([tile(0, 0), tile(1, 1), tile(2, 2)], axis=1)
    lower = jnp.concatenate([tile(1, 0), tile(2, 0), tile(2, 1)], axis=1)
    return upper, lower


def unpack_gram(upper, lower):
    tile = lambda packed, c: packed[:, c * TILE : (c + 1) * TILE]
    one, two, three = (tile(lower, c) for c in range(3))
    return jnp.concatenate(
        [
            jnp.concatenate([tile(upper, 0), one.T, two.T], axis=1),
            jnp.concatenate([one, tile(upper, 1), three.T], axis=1),
            jnp.concatenate([two, three, tile(upper, 2)], axis=1),
        ],
        axis=0,
    )


class Sum:
    def __init__(self, count, source, landed, whole, extra, send, recv, gsend, grecv, hsend, hrecv):
        self.pieces = source.shape[0]
        self.high = [b for b in range(count.bit_length() - 1) if (1 << b) >= self.pieces]
        self.source, self.landed, self.whole, self.extra = source, landed, whole, extra
        self.sems = send, recv, gsend, grecv, hsend, hrecv
        self.me = lax.axis_index("shard")
        self.low = lax.rem(self.me, self.pieces)

    def peer(self, step):
        place = lax.rem(self.low + step, self.pieces)
        return place, {"shard": self.me - self.low + place}

    def scatter(self, step):
        place, where = self.peer(step)
        send, recv = self.sems[:2]
        return remote(
            self.source.at[place], self.landed.at[self.low], send.at[step], recv.at[step], where
        )

    def spread(self, step):
        _, where = self.peer(step)
        send, recv = self.sems[2:4]
        part = self.whole.at[self.low]
        return remote(part, part, send.at[step], recv.at[step], where)

    def put(self, packed):
        self.source[...] = packed.reshape(self.source.shape)

    def start(self):
        for step in range(1, self.pieces):
            self.scatter(step).start()
        self.landed[self.low] = self.source[self.low]

    def land(self):
        for step in range(1, self.pieces):
            self.scatter(step).wait()
        return jnp.sum(self.landed[...], axis=0)

    def turn(self):
        self.give(self.land())

    def give(self, piece):
        self.whole[self.low] = piece
        send, recv = self.sems[4:]
        for at, bit in enumerate(self.high):
            copy = remote(
                self.whole.at[self.low],
                self.extra.at[at],
                send.at[at],
                recv.at[at],
                {"shard": flip(self.me, bit)},
            )
            copy.start()
            copy.wait()
            self.whole[self.low] += self.extra[at]
        for step in range(1, self.pieces):
            self.spread(step).start()

    def finish(self):
        for step in range(1, self.pieces):
            self.spread(step).wait()

    @staticmethod
    def scratch(count, rows):
        pieces = min(count, 16)
        high = max(count.bit_length() - pieces.bit_length(), 1)
        sems = pltpu.SemaphoreType.DMA
        block = pltpu.VMEM((pieces, rows // pieces, D), F32)
        return [block, block, block, pltpu.VMEM((high, rows // pieces, D), F32)] + [
            sems((pieces,))
        ] * 4 + [sems((high,))] * 2


SUM_REFS = 10


class FourSum:
    def __init__(self, count, source, first, between, second, whole, extra, *sems):
        self.source, self.first, self.between = source, first, between
        self.second, self.whole, self.extra = second, whole, extra
        self.sems = sems
        self.high = range(2, (count.bit_length() - 1) // 2)
        self.me = lax.axis_index("shard")
        self.plane, self.along = digit_of(self.me, 0), digit_of(self.me, 1)

    def copy(self, at, digit, step, pick):
        place, where = digit_peer(self.me, digit, step)
        src, dst = pick(place)
        return remote(src, dst, self.sems[2 * at].at[step], self.sems[2 * at + 1].at[step], where)

    def round(self, at):
        if at == 0:
            pick = lambda place: (self.source.at[:, place], self.first.at[self.plane])
        elif at == 1:
            pick = lambda place: (self.between.at[place], self.second.at[self.along])
        elif at == 2:
            part = self.whole.at[self.along, self.plane]
            pick = lambda place: (part, part)
        else:
            part = self.whole.at[:, self.plane]
            pick = lambda place: (part, part)
        return [self.copy(at, (0, 1, 1, 0)[at], step, pick) for step in range(1, 4)]

    def put(self, packed):
        self.source[...] = packed.reshape(self.source.shape)

    def start(self):
        for copy in self.round(0):
            copy.start()
        self.first[self.plane] = self.source[:, self.plane]

    def along_start(self):
        for copy in self.round(0):
            copy.wait()
        self.between[...] = jnp.sum(self.first[...], axis=0)
        for copy in self.round(1):
            copy.start()
        self.second[self.along] = self.between[self.along]

    def land(self):
        for copy in self.round(1):
            copy.wait()
        return jnp.sum(self.second[...], axis=0)

    def give(self, piece):
        self.whole[self.along, self.plane] = piece
        part = self.whole.at[self.along, self.plane]
        send, recv = self.sems[8:]
        for at, digit in enumerate(self.high):
            copies = []
            for step in range(1, 4):
                _, where = digit_peer(self.me, digit, step)
                slot = 4 * at + step
                copies.append(
                    remote(part, self.extra.at[slot], send.at[slot], recv.at[slot], where)
                )
            for copy in copies:
                copy.start()
            for copy in copies:
                copy.wait()
            for step in range(1, 4):
                self.whole[self.along, self.plane] += self.extra[4 * at + step]
        for copy in self.round(2):
            copy.start()

    def turn(self):
        self.give(self.land())

    def plane_start(self):
        for copy in self.round(2):
            copy.wait()
        for copy in self.round(3):
            copy.start()

    def finish(self):
        for copy in self.round(3):
            copy.wait()

    @staticmethod
    def scratch(count, rows):
        piece = (rows // 16, D)
        high = 4 * max((count.bit_length() - 1) // 2 - 2, 1)
        sems = pltpu.SemaphoreType.DMA
        return [
            pltpu.VMEM((4, 4) + piece, F32),
            pltpu.VMEM((4, 4) + piece, F32),
            pltpu.VMEM((4,) + piece, F32),
            pltpu.VMEM((4,) + piece, F32),
            pltpu.VMEM((4, 4) + piece, F32),
            pltpu.VMEM((high,) + piece, F32),
        ] + [sems((4,))] * 8 + [sems((high,))] * 2


FOUR_REFS = 16


def backward_kernel(
    nbits,
    scale_of,
    dctx_ref,
    xin_ref,
    q_ref,
    k_ref,
    v_ref,
    ctx_ref,
    lse_ref,
    w_ref,
    tok_ref,
    mid_ref,
    mod_ref,
    gp_ref,
    ge_ref,
    gr_ref,
    old_exp,
    old_red,
    sums_in,
    wides_in,
    grad_ref,
    att_ref,
    mine_ref,
    own_ref,
    piece_ref,
    *rest,
):
    stages = rest[:nbits]
    (
        low_out,
        first,
        total,
        k_turn,
        v_rows,
        dk_sum,
        dv_sum,
        dq_low,
        dk_low,
        dv_low,
        gw,
        bias_ref,
        outgoing,
        incoming,
        sems,
        asems,
        send,
        recv,
    ) = rest[nbits:-FOUR_REFS]
    one = FourSum(1 << nbits, *rest[-FOUR_REFS:])
    me = lax.axis_index("shard")
    core = lax.axis_index("ctx")
    signal_all(me, 1 << nbits)
    half = tok_ref.shape[0]
    lead = (slice(None),) * nbits
    wide = ge_ref.shape[-2]
    both = wide + gp_ref.shape[-2]
    last = nbits + 1
    main = lead + (slice(0, wide),)
    side_rows = lead + (slice(wide, both),)
    padded = low_out.shape[-2]
    spots = {1: 0, 2: 2, 3: 4, 4: 5}
    after = range(5, nbits + 2)

    def swap_main(which):
        return remote(
            (gr_ref, ge_ref)[which], first.at[main], send.at[0], recv.at[0], other_core()
        )

    swap_side = remote(gp_ref, first.at[side_rows], send.at[last], recv.at[last], other_core())

    def cube_step(which, step):
        order = scatter_orders(nbits)[which]
        bit = order[step]
        free = order[step + 1 :]
        there = flip(me, bit)
        if step < LOW_STEPS:
            rows = slice(0, padded if which == 0 else up_to(wide, 16))
            source = low_out
        else:
            rows = slice(0, both if which == 0 else wide)
            source = total
        return remote(
            source.at[cube_index(there, nbits, free, (rows,))],
            stages[step].at[(slice(None),) * len(free) + (rows,)],
            send.at[step + 1],
            recv.at[step + 1],
            {"shard": there},
        )

    def send_step(which, step):
        order = scatter_orders(nbits)[which]
        if step < LOW_STEPS:
            rows = slice(0, both if which == 0 else wide)
            index = cube_index(flip(me, order[step]), nbits, order[step + 1 :], (rows,))
            low_out[index] = total[index].astype(BF)
        cube_step(which, step).start()

    def last_swap(which):
        rows = slice(0, both if which == 0 else wide)
        return remote(
            own_ref.at[which, rows],
            own_ref.at[which, rows],
            send.at[nbits + 2],
            recv.at[nbits + 2],
            other_core(),
        )

    def progress(point):
        for which in range(2):

            @pl.when(core == which)
            def _():
                rows = slice(0, both if which == 0 else wide)
                order = scatter_orders(nbits)[which]
                if point == 0:
                    swap_main(which).start()
                    if which == 1:
                        swap_side.start()
                elif point == 1:
                    swap_main(which).wait()
                    if which == 0:
                        swap_side.wait_recv()
                        total[main] = ge_ref[...] + first[main]
                        total[side_rows] = gp_ref[...] + first[side_rows]
                        if padded > both:
                            low_out[lead + (slice(both, padded),)] = jnp.zeros(
                                (2,) * nbits + (padded - both, D), BF
                            )
                    else:
                        swap_side.wait_send()
                        total[main] = gr_ref[...] + first[main]
                elif point <= nbits + 1:
                    step = point - 2
                    cube_step(which, step).wait()
                    free = order[step + 1 :]
                    total[cube_index(me, nbits, free, (rows,))] += stages[step][
                        (slice(None),) * len(free) + (rows,)
                    ].astype(F32)
                if 1 <= point <= nbits:
                    send_step(which, point - 1)
                if point == nbits + 1:
                    own_ref[which, rows] = total[cube_index(me, nbits, (), (rows,))]
                    last_swap(which).start()
                if point == nbits + 2:
                    last_swap(which).wait_send()
                    last_swap(1 - which).wait_recv()

    turn = lambda value: jnp.transpose(value.astype(F32)).astype(BF)
    progress(0)
    for head in range(HALF_HEADS):
        k_turn[...] = turn(k_ref[head])
        v_rows[...] = turn(v_ref[head])
        dk_sum[...] = jnp.zeros_like(dk_sum)
        dv_sum[...] = jnp.zeros_like(dv_sum)

        def step(side, _):
            query = q_ref[head, side]
            down = dctx_ref[side, :, head * HEAD_DIM : (head + 1) * HEAD_DIM]
            down_turn = jnp.transpose(down.astype(F32))
            delta = jnp.sum(down_turn * ctx_ref[head, side], axis=0, keepdims=True)
            scores = dot(k_ref[head], query)
            probs = jnp.exp2(scores * LOG2E - lse_ref[head, side, 0:1, :])
            dv_sum[...] += dot(probs.astype(BF), down)
            grad_probs = dot(v_rows[...], down_turn.astype(BF))
            grad_scores = (probs * (grad_probs - delta)).astype(BF)
            dk_sum[...] += dot(grad_scores, turn(query))
            dq_low[head, side] = (
                jnp.transpose(dot(k_turn[...], grad_scores)) * (HEAD_DIM**-0.5)
            ).astype(BF)
            for at in range(2):
                for point in range(1, 5):
                    if spots[point] == head * 2 + at:
                        pl.when(side == at)(functools.partial(progress, point))
            return 0

        lax.fori_loop(0, 2, step, 0)
        dk_low[head] = dk_sum[...].reshape(2, half, HEAD_DIM).astype(BF)
        dv_low[head] = dv_sum[...].reshape(2, half, HEAD_DIM).astype(BF)

    def side_grads(side, fresh):
        pieces = [dq_low[h, side] for h in range(HALF_HEADS)]
        pieces += [dk_low[h, side] for h in range(HALF_HEADS)]
        pieces += [dv_low[h, side] for h in range(HALF_HEADS)]
        joined = jnp.concatenate(pieces, axis=1)
        grad = dot_tn(joined, xin_ref[side])
        sums = dot(jnp.ones((8, half), BF), joined)
        gw[...] = grad if fresh else gw[...] + grad
        bias_ref[...] = sums if fresh else bias_ref[...] + sums
        return dot(joined, w_ref[...])

    outgoing[...] = side_grads(1 - core, True)
    copy = remote(outgoing, incoming, sems.at[0], sems.at[1], other_core())
    copy.start()
    for point in after:
        progress(point)
    old = jnp.where(core == 0, old_exp[...], old_red[...])
    gram = gram_of(moment_decay * old + own_ref[core, 0:wide, :] * scale_of)
    one.put(jnp.concatenate(pack_gram(gram), axis=0))
    one.start()
    own = side_grads(core, False)

    def share(which):
        return [
            remote(
                att_ref.at[pl.ds(block * D + which * HALF, HALF), :],
                att_ref.at[pl.ds(block * D + which * HALF, HALF), :],
                asems.at[0, block],
                asems.at[1, block],
                other_core(),
            )
            for block in range(3)
        ]

    for which in range(2):

        @pl.when(core == which)
        def _():
            for block in range(3):
                att_ref[block * D + which * HALF : block * D + (which + 1) * HALF, :] = gw[
                    block * HALF : (block + 1) * HALF, :
                ]
            for part in share(which):
                part.start()

    one.along_start()
    copy.wait()
    grad_in = own + incoming[...]
    normed, inverse = normalize(tok_ref[...].astype(F32))
    scale = 1.0 + mod_ref[1:2, :]
    grad_ref[...] = mid_ref[...] + norm_back(grad_in * scale, normed, inverse)
    shift_sum = jnp.sum(grad_in, axis=0, keepdims=True)
    scale_sum = jnp.sum(grad_in * normed, axis=0, keepdims=True)
    row = lambda index: sums_in[index : index + 1, :]
    grad_mod = [shift_sum, scale_sum, row(3), row(1), row(2), row(0)]
    none = jnp.zeros((1, HALF), F32)

    def placed(part):
        return jnp.where(
            core == 0,
            jnp.concatenate([part, none], axis=1),
            jnp.concatenate([none, part], axis=1),
        )

    bias_grad = jnp.concatenate(
        grad_mod
        + [
            placed(bias_ref[0:1, 0:HALF]),
            placed(bias_ref[0:1, 2 * HALF :]),
            row(4),
            wides_in[0:1, :],
            row(5),
        ],
        axis=1,
    )
    grad_mod = jnp.concatenate(grad_mod, axis=1)
    count = 1 << nbits
    nbias, width = bias_grad.shape[1] // count, grad_mod.shape[1] // count
    mine_ref[...] = jnp.zeros_like(mine_ref)
    for to in range(count):
        mine_ref[to, :, 0:nbias] = bias_grad[:, to * nbias : (to + 1) * nbias]
        mine_ref[to, :, D : D + width] = grad_mod[:, to * width : (to + 1) * width]
    for which in range(2):

        @pl.when(core == which)
        def _():
            for part in share(which):
                part.wait_send()
            for part in share(1 - which):
                part.wait_recv()

    progress(nbits + 2)
    piece_ref[...] = one.land()


def attention_backward(
    dctx,
    xin,
    q,
    k,
    v,
    ctx,
    lse,
    weight,
    tok,
    mid,
    mod_rows,
    gp,
    ge,
    gr,
    old_exp,
    old_red,
    sums,
    wides,
    scale,
):
    half = tok.shape[0]
    full = 2 * half
    count, wide, _ = ge.shape
    both = wide + gp.shape[1]
    nbits = count.bit_length() - 1
    lead = (2,) * nbits
    shape = jax.ShapeDtypeStruct
    sems = pltpu.SemaphoreType.DMA
    return pl.pallas_call(
        functools.partial(backward_kernel, nbits, scale),
        out_shape=[
            shape((half, D), F32),
            shape((3 * D, D), F32),
            shape((count, 1, D + up_to(6 * D // count, 128)), F32),
            shape((2, both, D), F32),
            shape((2 * TILE // 16, D), F32),
        ],
        in_specs=[VM] * 18,
        out_specs=[VM] * 5,
        scratch_shapes=[
            pltpu.VMEM((2,) * (nbits - 1 - k) + ((up_to(both, 16), D) if k < LOW_STEPS else (both, D)), BF if k < LOW_STEPS else F32)
            for k in range(nbits)
        ]
        + [
            pltpu.VMEM(lead + (up_to(both, 16), D), BF),
            pltpu.VMEM(lead + (both, D), F32),
            pltpu.VMEM(lead + (both, D), F32),
            pltpu.VMEM((HEAD_DIM, full), BF),
            pltpu.VMEM((full, HEAD_DIM), BF),
            pltpu.VMEM((full, HEAD_DIM), F32),
            pltpu.VMEM((full, HEAD_DIM), F32),
            pltpu.VMEM((HALF_HEADS, 2, half, HEAD_DIM), BF),
            pltpu.VMEM((HALF_HEADS, 2, half, HEAD_DIM), BF),
            pltpu.VMEM((HALF_HEADS, 2, half, HEAD_DIM), BF),
            pltpu.VMEM((3 * HALF, D), F32),
            pltpu.VMEM((8, 3 * HALF), F32),
            pltpu.VMEM((half, D), F32),
            pltpu.VMEM((half, D), F32),
            sems((2,)),
            sems((2, 3)),
            sems((nbits + 3,)),
            sems((nbits + 3,)),
        ]
        + FourSum.scratch(count, 2 * TILE),
        compiler_params=params(35, 3),
        name="attend_backward",
    )(
        dctx,
        xin,
        q,
        k,
        v,
        ctx,
        lse,
        weight,
        tok,
        mid,
        mod_rows,
        gp.reshape(lead + gp.shape[1:]),
        ge.reshape(lead + ge.shape[1:]),
        gr.reshape(lead + gr.shape[1:]),
        old_exp,
        old_red,
        sums,
        wides,
    )


def tail_kernel(
    count,
    scale,
    local,
    att_ref,
    own_ref,
    piece_ref,
    mine_ref,
    small_ref,
    wmod_ref,
    old_mod,
    old_att,
    old_pro,
    fac_ref,
    rows_ref,
    modg_ref,
    bias_ref,
    cond_ref,
    *rest,
):
    digits = (count.bit_length() - 1) // 2
    lands, added = rest[:digits], rest[digits : 2 * digits]
    got, theirs, back_send, back, upper_half, other_half = rest[2 * digits : 2 * digits + 6]
    send, recv, msend, mrecv, bsend, brecv, csem, fsem = rest[2 * digits + 6 : 2 * digits + 14]
    sums = rest[2 * digits + 14 :]
    one = FourSum(count, *sums[:FOUR_REFS])
    two = Sum(count, *sums[FOUR_REFS : FOUR_REFS + SUM_REFS])
    late = Sum(count, *sums[FOUR_REFS + SUM_REFS :])
    me = lax.axis_index("shard")
    core = lax.axis_index("ctx")
    signal_all(me, count)
    n_att, n_pro, wide = local
    padded = att_ref.shape[-2]
    half_rows = rows_ref.shape[1]

    begin = pl.multiple_of(core * (padded - half_rows), 8)

    def rows_source(digit, place):
        lead = (slice(None),) * (digits - digit - 1) + (place,)
        if digit == 0:
            return att_ref.at[lead + (pl.ds(begin, half_rows),)]
        return added[digit - 1].at[lead]

    def rows_copies(digit):
        copies = []
        for step in range(1, 4):
            place, where = digit_peer(me, digit, step)
            copies.append(
                remote(
                    rows_source(digit, place),
                    lands[digit].at[digit_of(me, digit)],
                    send.at[digit, step],
                    recv.at[digit, step],
                    where,
                )
            )
        return copies

    def rows_start(digit):
        for copy in rows_copies(digit):
            copy.start()
        own = digit_of(me, digit)
        lands[digit][own] = rows_source(digit, own)[...]

    def rows_add(digit):
        for copy in rows_copies(digit):
            copy.wait()
        total = jnp.sum(lands[digit][...], axis=0)
        if digit < digits - 1:
            added[digit][...] = total
            rows_start(digit + 1)
        else:
            rows_ref[core] = total
            swap_rows(core).start()

    def swap_rows(which):
        part = rows_ref.at[which]
        return remote(part, part, csem.at[2], csem.at[3], other_core())

    copies = []
    for step in range(1, count):
        to = lax.rem(me + step, count)
        copy = remote(mine_ref.at[to], got.at[me], msend.at[step], mrecv.at[step], {"shard": to})
        copy.start()
        copies.append(copy)
    got[me] = mine_ref[me]
    one.give(piece_ref[...])
    rows_start(0)
    for copy in copies:
        copy.wait()
    swap = remote(got, theirs, csem.at[0], csem.at[1], other_core())
    swap.start()
    cond = small_ref[:, 0, 0:D]
    silu_low = silu_of(cond).astype(BF).astype(F32)
    one.plane_start()
    swap.wait()
    width = old_mod.shape[0]
    both = got[:, 0, :] + theirs[:, 0, :]
    grad_mod = both[:, D : D + width]
    bias_ref[...] = jnp.sum(both[:, 0:D], axis=0, keepdims=True)
    raw = lax.dot_general(
        grad_mod,
        silu_low,
        (((0,), (0,)), ((), ())),
        precision=precise,
        preferred_element_type=F32,
    )
    modg_ref[...] = raw

    @pl.when(core == 0)
    def _():
        grad = own_ref[0, wide : wide + n_pro, :] * scale
        two.put(jnp.concatenate(pack_gram(gram_of(moment_decay * old_pro[...] + grad)), axis=0))

    @pl.when(core == 1)
    def _():
        grad = modg_ref[...] * scale
        two.put(jnp.concatenate(pack_gram(gram_of(moment_decay * old_mod[...] + grad)), axis=0))

    two.start()
    part = jnp.dot(
        grad_mod, wmod_ref[...].astype(BF).astype(F32), precision=precise, preferred_element_type=F32
    )
    for row in range(count):
        back_send[row] = part[row : row + 1, :]
    back[me] = back_send[me]
    backs = []
    for step in range(1, count):
        to = lax.rem(me + step, count)
        copy = remote(
            back_send.at[to], back.at[me], bsend.at[step], brecv.at[step], {"shard": to}
        )
        copy.start()
        backs.append(copy)

    def condition_grads():
        for copy in backs:
            copy.wait()
        grad_silu = jnp.sum(back[...], axis=0)
        own = small_ref[me][:, 0:D]
        gate = jax.nn.sigmoid(own)
        cond_ref[...] = grad_silu * (gate + own * gate * (1.0 - gate))

    def late_start():
        swap_rows(core).wait_send()
        swap_rows(1 - core).wait_recv()
        skip = 2 * half_rows - padded
        grad = jnp.concatenate([rows_ref[0], rows_ref[1, skip:]], axis=0)[0:n_att] * scale
        upper, lower = pack_gram(gram_of(moment_decay * old_att[...] + grad))
        late.put(jnp.where(core == 0, upper, lower))
        late.start()

    halves = remote(upper_half, other_half, csem.at[4], csem.at[5], other_core())

    def late_swap():
        late.finish()
        upper_half[...] = late.whole[...].reshape(TILE, D)
        halves.start()

    row = lax.broadcasted_iota(jnp.int32, (D, D), 0)
    column = lax.broadcasted_iota(jnp.int32, (D, D), 1)
    eye = (row == column).astype(F32)

    def solve(gram, between):
        diagonal = jnp.sum(gram * eye, axis=0, keepdims=True)
        size = 1.0 / (jnp.sqrt(jnp.sum(diagonal, axis=1, keepdims=True)) + 1e-07)
        return newton_factor((gram * size) * size, eye, between) * size

    def solve_sum(item, between):
        packed = item.whole[...].reshape(2 * TILE, D)
        return solve(unpack_gram(packed[0:TILE], packed[TILE:]), between)

    def pass_factor(index, at):
        part = fac_ref.at[index]
        return remote(part, part, fsem.at[0, at], fsem.at[1, at], other_core())

    place_one, place_two = 3 + core, 2 - 2 * core
    rows_add(0)
    one.finish()
    last_rows = [functools.partial(rows_add, digit) for digit in range(1, digits)]
    fac_ref[place_one] = solve_sum(
        one,
        {
            1: last_rows + [two.turn],
            2: [late_start],
            3: [condition_grads],
        },
    )
    first_pass = pass_factor(place_one, 0)
    first_pass.start()
    two.finish()
    fac_ref[place_two] = solve_sum(two, {0: [late.turn], 3: [late_swap]})
    second_pass = pass_factor(place_two, 1)
    second_pass.start()
    halves.wait()
    mine_half, their_half = upper_half[...], other_half[...]
    fac_ref[1] = solve(
        unpack_gram(
            jnp.where(core == 0, mine_half, their_half),
            jnp.where(core == 0, their_half, mine_half),
        ),
        {},
    )
    first_pass.wait()
    second_pass.wait()


def tail(att, own, piece, mine, small_all, wmod, olds, scale, local):
    count, padded, _ = att.shape
    digits = (count.bit_length() - 1) // 2
    half_rows = up_to(padded // 2, 8)
    width = wmod.shape[0]
    sems = pltpu.SemaphoreType.DMA
    shape = jax.ShapeDtypeStruct
    return pl.pallas_call(
        functools.partial(tail_kernel, count, scale, local),
        out_shape=[
            shape((5, D, D), F32),
            shape((2, half_rows, D), F32),
            shape((width, D), F32),
            shape((1, D), F32),
            shape((1, D), F32),
        ],
        in_specs=[VM] * 9,
        out_specs=[VM] * 5,
        scratch_shapes=[
            pltpu.VMEM((4,) * (digits - d) + (half_rows, D), F32) for d in range(digits)
        ]
        + [pltpu.VMEM((4,) * (digits - d - 1) + (half_rows, D), F32) for d in range(digits)]
        + [
            pltpu.VMEM(mine.shape, F32),
            pltpu.VMEM(mine.shape, F32),
            pltpu.VMEM((count, 1, D), F32),
            pltpu.VMEM((count, 1, D), F32),
            pltpu.VMEM((TILE, D), F32),
            pltpu.VMEM((TILE, D), F32),
            sems((digits, 4)),
            sems((digits, 4)),
            sems((count,)),
            sems((count,)),
            sems((count,)),
            sems((count,)),
            sems((6,)),
            sems((2, 2)),
        ]
        + FourSum.scratch(count, 2 * TILE)
        + Sum.scratch(count, 2 * TILE)
        + Sum.scratch(count, TILE),
        compiler_params=params(14, 4),
        name="tail",
    )(att.reshape((4,) * digits + (padded, D)), own, piece, mine, small_all, wmod, *olds[:3])


def update_kernel(scale, rates, bounds, *refs):
    fac_ref, att_ref, modg_ref, own_ref = refs[:4]
    olds, masters, done = refs[4:9], refs[9:14], refs[14:16]
    outs, final, sem = refs[16:31], refs[31:33], refs[33]
    copies = [
        pltpu.make_async_copy(source, target, sem.at[at])
        for at, (source, target) in enumerate(zip(done, final))
    ]
    for copy in copies:
        copy.start()
    n_att, wide, n_pro = bounds
    first_rows = att_ref.shape[1]
    skip = 2 * first_rows - up_to(n_att, 8)
    joined = jnp.concatenate([att_ref[0], att_ref[1, skip:]], axis=0)
    grads = [
        modg_ref[...],
        joined[0:n_att],
        own_ref[0, wide : wide + n_pro, :],
        own_ref[0, 0:wide, :],
        own_ref[1, 0:wide, :],
    ]
    for index in range(5):
        grad = grads[index] * scale
        moment = moment_decay * olds[index][...] + grad
        direction = dot_three(moment, fac_ref[index])
        outs[3 * index][...] = grad
        outs[3 * index + 1][...] = masters[index][...] - rates[index] * direction
        outs[3 * index + 2][...] = moment
    for copy in copies:
        copy.wait()


def update(fac, att, modg, own, olds, masters, done, scale, count):
    shape = jax.ShapeDtypeStruct
    out = []
    for m in masters:
        out += [shape(m.shape, F32)] * 3
    out += [shape(value.shape, value.dtype) for value in done]
    anywhere = pl.BlockSpec(memory_space=pl.ANY)
    rates = [matrix_rate * 0.2 * math.sqrt(max(D, m.shape[0] * count)) for m in masters]
    bounds = (olds[1].shape[0], olds[3].shape[0], olds[2].shape[0])
    return pl.pallas_call(
        functools.partial(update_kernel, scale, rates, bounds),
        out_shape=out,
        in_specs=[VM] * 14 + [anywhere] * 2,
        out_specs=[VM] * 15 + [anywhere] * 2,
        scratch_shapes=[pltpu.SemaphoreType.DMA((2,))],
        compiler_params=params(8),
        name="update",
    )(fac, att, modg, own, *olds, *masters, *done)


def on_device(
    tokens,
    condition,
    cotangent,
    modulate_weight,
    attend_weight,
    project_weight,
    expand_weight,
    reduce_weight,
    bias_flat,
    modulate_moment,
    attend_moment,
    project_moment,
    expand_moment,
    reduce_moment,
    bias_moment,
):
    count = lax.axis_size("shard")
    full = tokens.shape[1] * lax.axis_size("ctx")
    olds = [
        m.T
        for m in (modulate_moment, attend_moment, project_moment, expand_moment, reduce_moment)
    ]
    masters = [
        w.T
        for w in (modulate_weight, attend_weight, project_weight, expand_weight, reduce_weight)
    ]
    n_att, n_pro, n_wide = (w.shape[0] for w in masters[1:4])
    nbias = bias_flat.shape[0]
    tok = tokens[0]
    (
        small_all,
        mod_rows,
        wide_rows,
        project_turn,
        expand_turn,
        reduce_turn,
        weight_core,
        xin,
        q,
        k,
        v,
        ctx_turn,
        lse,
        ctx,
    ) = front(masters[1:], masters[0], condition, bias_flat[None], tok, count)
    block_out, mid, gp, ge, gr, sums, wides, dctx = branch(
        ctx,
        tok,
        cotangent[0],
        mod_rows,
        wide_rows,
        project_turn,
        expand_turn[:, :n_wide].reshape(FF, D),
        reduce_turn[:, :n_wide].reshape(FF, D),
    )
    gp = pad_rows(gp.reshape(count, n_pro, D), up_to(n_pro, 8))
    scale = 1.0 / math.sqrt(tokens.shape[0] * count * full)
    tokens_grad, att, mine, mlp_rows, piece = attention_backward(
        dctx,
        xin,
        q,
        k,
        v,
        ctx_turn,
        lse,
        weight_core,
        tok,
        mid,
        mod_rows,
        gp,
        ge.reshape(count, n_wide, D),
        gr.reshape(count, n_wide, D),
        olds[3],
        olds[4],
        sums,
        wides,
        scale,
    )
    att = pad_rows(att.reshape(count, n_att, D), up_to(n_att, 8))
    fac, att_rows, modg, bias_sum, condition_rows = tail(
        att, mlp_rows, piece, mine, small_all, masters[0], olds, scale, (n_att, n_pro, n_wide)
    )
    done = (block_out[None], tokens_grad[None])
    out = update(fac, att_rows, modg, mlp_rows, olds, masters, done, scale, count)
    bias_grad = bias_sum[0, :nbias] * scale
    bias_new = moment_decay * bias_moment + bias_grad
    result = [*out[15:], condition_rows]
    result += [value.T for value in out[:15]]
    result += [bias_grad, bias_flat - bias_rate * bias_new, bias_new]
    return tuple(result)


def solution(mesh):
    tok = P("shard", "ctx", None)
    row = P("shard", None)
    col = P(None, "shard")
    flat = P("shard")
    return jax.shard_map(
        on_device,
        mesh=mesh,
        in_specs=(tok, row, tok) + (col,) * 5 + (flat,) + (col,) * 5 + (flat,),
        out_specs=(tok, tok, row) + (col,) * 15 + (flat,) * 3,
        check_vma=False,
    )
```

```python
import functools
import math

import jax
import jax.numpy as jnp
from jax import lax
from jax.experimental import pallas as pl
from jax.experimental.pallas import tpu as pltpu
from jax.sharding import PartitionSpec as P

D = 384
FF = 1536
HEADS = 6
HEAD_DIM = 64
NS_ITERS = 5
LOW_STEPS = 1
HALF_HEADS = HEADS // 2
HALF = HALF_HEADS * HEAD_DIM

norm_eps = 1e-06
newton_a = 3.4445
newton_b = -4.775
newton_c = 2.0315
moment_decay = 0.95
matrix_rate = 0.5
bias_rate = 0.1
precise = lax.Precision.HIGHEST
LOG2E = 1.4426950408889634

MESH = pl.DeviceIdType.MESH
BF = jnp.bfloat16
F32 = jnp.float32
VM = pl.BlockSpec(memory_space=pltpu.VMEM)
FAR = pl.BlockSpec(memory_space=pltpu.HBM)


def params(megabytes, collective=None):
    limit = megabytes * 2**20
    if collective is None:
        return pltpu.CompilerParams(vmem_limit_bytes=limit)
    return pltpu.CompilerParams(
        collective_id=collective, has_side_effects=True, vmem_limit_bytes=limit
    )


def dot(left, right):
    return jnp.dot(left, right, preferred_element_type=F32)


def dot_nt(left, right):
    return lax.dot_general(left, right, (((1,), (1,)), ((), ())), preferred_element_type=F32)


def dot_tn(left, right):
    return lax.dot_general(left, right, (((0,), (0,)), ((), ())), preferred_element_type=F32)


def split_low(values):
    high = values.astype(BF)
    return high, (values - high.astype(F32)).astype(BF)


def dot_three(left, right, op=dot):
    left_high, left_low = split_low(left)
    right_high, right_low = split_low(right)
    return op(left_high, right_high) + (op(left_high, right_low) + op(left_low, right_high))


def silu_of(values):
    return values * jax.nn.sigmoid(values)


def normalize(values):
    centered = values - jnp.mean(values, axis=-1, keepdims=True)
    inverse = lax.rsqrt(jnp.mean(centered * centered, axis=-1, keepdims=True) + norm_eps)
    return (centered * inverse, inverse)


def norm_back(grad_normed, normed, inverse):
    first = jnp.mean(grad_normed, axis=-1, keepdims=True)
    second = jnp.mean(grad_normed * normed, axis=-1, keepdims=True)
    return (grad_normed - first - normed * second) * inverse


def pad_rows(array, rows):
    return jnp.pad(array, ((0, 0),) * (array.ndim - 2) + ((0, rows - array.shape[-2]), (0, 0)))


def up_to(value, step):
    return -(-value // step) * step


def bit_of(value, bit):
    return lax.rem(value // (1 << bit), 2)


def flip(me, bit):
    return me + (1 - 2 * bit_of(me, bit)) * (1 << bit)


def other_core():
    return {"ctx": 1 - lax.axis_index("ctx")}


def signal_cube(me, nbits):
    sem = pltpu.get_barrier_semaphore()
    for bit in range(nbits):
        pl.semaphore_signal(
            sem, inc=1, device_id={"shard": flip(me, bit)}, device_id_type=MESH
        )
    pl.semaphore_signal(sem, inc=1, device_id=other_core(), device_id_type=MESH)
    pl.semaphore_wait(sem, nbits + 1)


def signal_all(me, count):
    sem = pltpu.get_barrier_semaphore()
    for step in range(1, count):
        pl.semaphore_signal(
            sem, inc=1, device_id={"shard": lax.rem(me + step, count)}, device_id_type=MESH
        )
    pl.semaphore_signal(sem, inc=1, device_id=other_core(), device_id_type=MESH)
    pl.semaphore_wait(sem, count)


def signal_core():
    sem = pltpu.get_barrier_semaphore()
    pl.semaphore_signal(sem, inc=1, device_id=other_core(), device_id_type=MESH)
    pl.semaphore_wait(sem, 1)


def remote(src, dst, send, recv, where):
    return pltpu.make_async_remote_copy(
        src, dst, send, recv, device_id=where, device_id_type=MESH
    )


def orders(nbits):
    up = list(range(nbits))
    return up, ([1, 0] + up[2:] if nbits >= 2 else up)


def scatter_orders(nbits):
    up = list(range(nbits))
    return up, (up[1:] + up[:1] if nbits >= 2 else up)


def digit_of(value, digit):
    return lax.rem(value // (1 << (2 * digit)), 4)


def digit_peer(me, digit, step):
    own = digit_of(me, digit)
    place = lax.rem(own + step, 4)
    return place, {"shard": me + (place - own) * (1 << (2 * digit))}


def cube_index(who, nbits, free, tail=()):
    lead = tuple(
        slice(None) if (nbits - 1 - d) in free else bit_of(who, nbits - 1 - d)
        for d in range(nbits)
    )
    return lead + tuple(tail)


class Gather:
    def __init__(self, nbits, whole, send, recv, psend, precv):
        self.nbits, self.whole = nbits, whole
        self.sems = send, recv, psend, precv
        self.me = lax.axis_index("shard")

    def step(self, which, at):
        seq = orders(self.nbits)[which][::-1]
        bit = seq[at]
        part = self.whole.at[cube_index(self.me, self.nbits, seq[:at], (which,))]
        send, recv = self.sems[:2]
        return remote(part, part, send.at[at], recv.at[at], {"shard": flip(self.me, bit)})

    def forward(self, which, at):
        seq = orders(self.nbits)[which][::-1]
        bit = seq[at]
        part = self.whole.at[
            cube_index(flip(self.me, bit), self.nbits, seq[:at], (which,))
        ]
        send, recv = self.sems[2:]
        return remote(part, part, send.at[at], recv.at[at], other_core())

    def each(self, act):
        for which in range(2):
            pl.when(lax.axis_index("ctx") == which)(functools.partial(act, which))

    def start(self):
        self.each(lambda which: self.step(which, 0).start())

    def advance(self, at):
        def act(which):
            self.step(which, at).wait()
            if at + 1 < self.nbits:
                self.step(which, at + 1).start()
            self.forward(which, at).start()

        self.each(act)

    def finish(self):
        def act(which):
            for at in range(self.nbits):
                self.forward(which, at).wait_send()
            for at in range(self.nbits):
                self.forward(1 - which, at).wait_recv()

        self.each(act)

    @staticmethod
    def scratch(nbits):
        return [pltpu.SemaphoreType.DMA((nbits,))] * 4


class FourGather:
    def __init__(self, digits, whole, send, recv, swap):
        self.digits, self.whole = digits, whole
        self.sems, self.swap = (send, recv), swap
        self.me = lax.axis_index("shard")
        self.core = lax.axis_index("ctx")

    def round(self, at):
        digit = self.digits - 1 - at
        own = tuple(digit_of(self.me, d) for d in range(digit, -1, -1))
        part = self.whole.at[(slice(None),) * at + own + (self.core,)]
        send, recv = self.sems
        copies = []
        for step in range(1, 4):
            _, where = digit_peer(self.me, digit, step)
            copies.append(remote(part, part, send.at[at, step], recv.at[at, step], where))
        return copies

    def start(self, at):
        for copy in self.round(at):
            copy.start()

    def wait(self, at):
        for copy in self.round(at):
            copy.wait()

    def forward(self):
        part = self.whole.at[(slice(None),) * self.digits + (self.core,)]
        return remote(part, part, self.swap.at[0], self.swap.at[1], other_core())


def front_kernel(
    nbits,
    att_far,
    pro_far,
    exp_far,
    red_far,
    mod_far,
    cond_ref,
    bias_ref,
    tok_ref,
    small_all,
    rows_ref,
    wide_ref,
    wp_ref,
    we_ref,
    wr_ref,
    w_ref,
    xin_ref,
    q_ref,
    k_ref,
    v_ref,
    ctx_ref,
    lse_ref,
    both_ref,
    whole_one,
    whole_two,
    tok_all,
    normed_all,
    small_own,
    mod_all,
    mod_send,
    cols,
    outgoing,
    att_own,
    pro_own,
    exp_own,
    red_own,
    mod_own,
    ssend,
    srecv,
    msend,
    mrecv,
    sems,
    near,
    *gsems,
):
    count = 1 << nbits
    me = lax.axis_index("shard")
    core = lax.axis_index("ctx")
    loads = [
        pltpu.make_async_copy(far, own, near.at[at])
        for at, (far, own) in enumerate(
            [
                (att_far, att_own),
                (pro_far, pro_own),
                (exp_far, exp_own),
                (red_far, red_own),
                (mod_far, mod_own),
                (tok_ref, tok_all.at[core]),
            ]
        )
    ]
    for load in loads:
        load.start()
    signal_all(me, count)
    n_att, n_pro, n_wide = att_own.shape[0], pro_own.shape[0], exp_own.shape[0]
    width, nbias = mod_own.shape[0], bias_ref.shape[1]
    half = tok_ref.shape[0]
    digits = nbits // 2
    own = cube_index(me, nbits, ())
    one = FourGather(digits, whole_one, *gsems[:3])
    two = Gather(nbits, whole_two, *gsems[3:])
    half_one, half_two = whole_one.shape[-2], whole_two.shape[-2]
    pad_pro, pad_wide = up_to(n_pro, 16), up_to(n_wide, 16)

    def joined(parts, total):
        pieces = []
        for part, rows in parts:
            pieces.append(part[...])
            if rows > part.shape[0]:
                pieces.append(jnp.zeros((rows - part.shape[0], D), F32))
        rows = sum(rows for _, rows in parts)
        if total > rows:
            pieces.append(jnp.zeros((total - rows, D), F32))
        return jnp.concatenate(pieces, axis=0).astype(BF)

    small_own[...] = jnp.zeros_like(small_own)
    small_own[:, 0:D] = cond_ref[...].astype(F32)
    small_own[:, D : D + nbias] = bias_ref[...].astype(BF).astype(F32)
    spread = []
    for step in range(1, count):
        to = lax.rem(me + step, count)
        copy = remote(
            small_own, small_all.at[me], ssend.at[step], srecv.at[step], {"shard": to}
        )
        copy.start()
        spread.append(copy)
    for load in loads:
        load.wait()
    halves = joined([(att_own, n_att)], 2 * half_one)
    place = tuple(digit_of(me, d) for d in range(digits - 1, -1, -1))
    whole_one[place + (core,)] = jnp.where(core == 0, halves[:half_one], halves[half_one:])
    one.start(0)
    toks = remote(tok_ref, tok_all.at[core], sems.at[0], sems.at[1], other_core())
    toks.start()
    small_all[me] = small_own[...]
    whole_two[own] = joined(
        [(pro_own, pad_pro), (exp_own, pad_wide), (red_own, pad_wide)], 2 * half_two
    ).reshape(2, half_two, D)
    block = 256

    def norm_side(side):
        def norm_block(index, _):
            rows = pl.ds(pl.multiple_of(index * block, block), block)
            normed, _inverse = normalize(tok_all[side, rows, :].astype(F32))
            normed_all[side, rows, :] = normed
            return 0

        lax.fori_loop(0, half // block, norm_block, 0)

    one.wait(0)
    one.start(1)
    for copy in spread:
        copy.wait()
    silu_low = silu_of(small_all[:, 0, 0:D]).astype(BF)
    part = dot_nt(silu_low, mod_own[...].astype(BF))
    for row in range(count):
        mod_send[row] = part[row : row + 1, :]
    mods = []
    for step in range(1, count):
        to = lax.rem(me + step, count)
        copy = remote(
            mod_send.at[to], mod_all.at[me], msend.at[step], mrecv.at[step], {"shard": to}
        )
        copy.start()
        mods.append(copy)
    mod_all[me] = mod_send[me]
    norm_side(core)
    toks.wait()
    norm_side(1 - core)
    biases = jnp.concatenate([small_all[s, :, D : D + nbias] for s in range(count)], axis=1)
    for at in range(1, digits):
        one.wait(at)
        if at + 1 < digits:
            one.start(at + 1)
    forward = one.forward()
    forward.start()
    two.start()
    for copy in mods:
        copy.wait()
    mods = jnp.concatenate([mod_all[s] for s in range(count)], axis=1)
    mods = mods + biases[:, 0 : 6 * D]
    rows_ref[...] = jnp.zeros_like(rows_ref)
    for row in range(6):
        rows_ref[row : row + 1, :] = mods[:, row * D : (row + 1) * D]
    rows_ref[6:7, :] = biases[:, 8 * D : 9 * D]
    rows_ref[7:8, :] = biases[:, 9 * D + FF :]
    wide_ref[...] = jnp.broadcast_to(biases[:, 9 * D : 9 * D + FF], (8, FF))
    shift = mods[:, 0:D]
    scale = 1.0 + mods[:, D : 2 * D]

    def shift_block(index, _):
        rows = pl.ds(pl.multiple_of(index * block, block), block)
        for side in range(2):
            xin_ref[side, rows, :] = (normed_all[side, rows, :] * scale + shift).astype(BF)
        return 0

    lax.fori_loop(0, half // block, shift_block, 0)

    def turned_bias(at):
        row = biases[:, at * D : (at + 1) * D]
        row = jnp.where(core == 0, row[:, 0:HALF], row[:, HALF:])
        return jnp.transpose(jnp.broadcast_to(row, (8, HALF)))[:, 0:1]

    query_bias, value_bias = turned_bias(6), turned_bias(7)

    def picked(rows, source, wanted, local, stride):
        index = lax.broadcasted_iota(jnp.int32, (rows, 1), 0)
        goal = wanted(index).astype(F32)
        block_of = jnp.floor((goal + 0.5) * (1.0 / local))
        place = goal + block_of * float(stride - local)
        column = lax.broadcasted_iota(jnp.int32, (rows, source.shape[0]), 1).astype(F32)
        return dot((column == place).astype(BF), source).astype(BF)

    forward.wait()
    for part in range(3):
        w_ref[part * HALF : (part + 1) * HALF, :] = picked(
            HALF,
            whole_one[...].reshape(count * 2 * half_one, D),
            lambda index: index + (part * D + core * HALF),
            n_att,
            2 * half_one,
        )
    for side in range(2):
        xin = xin_ref[side]
        rows = pl.ds(side * half, half)
        query = dot_nt(w_ref[0:HALF, :], xin) + query_bias
        value = dot_nt(w_ref[2 * HALF :, :], xin) + value_bias
        query = query.astype(BF) * jnp.asarray(HEAD_DIM**-0.5, BF)
        value = value.astype(BF)
        for head in range(HALF_HEADS):
            part = slice(head * HEAD_DIM, (head + 1) * HEAD_DIM)
            q_ref[head, side] = query[part, :]
            v_ref[head, :, rows] = value[part, :]
            k_ref[head, rows, :] = dot_nt(
                xin, w_ref[HALF + head * HEAD_DIM : HALF + (head + 1) * HEAD_DIM, :]
            ).astype(BF)
    two.advance(0)

    def attend(step, _):
        head = step // 2
        side = lax.rem(step, 2)
        scores = dot(k_ref[head], q_ref[head, side])
        top = jnp.max(scores, axis=0, keepdims=True)
        shifted = jnp.exp2((scores - top) * LOG2E)
        total = jnp.sum(shifted, axis=0, keepdims=True)
        probs = (shifted * (1.0 / total)).astype(BF)
        out = dot(v_ref[head], probs)
        ctx_ref[head, side] = out
        lse_ref[head, side] = jnp.broadcast_to(top * LOG2E + jnp.log2(total), (8, half))
        cols[side, pl.ds(pl.multiple_of(head * HEAD_DIM, HEAD_DIM), HEAD_DIM), :] = out
        for at in range(1, nbits - 1):
            pl.when(step == min(2 * at - 1, 4))(functools.partial(two.advance, at))
        return 0

    lax.fori_loop(0, 2 * HALF_HEADS, attend, 0)
    outgoing[...] = jnp.transpose(cols[1 - core]).astype(BF)
    copy = remote(outgoing, both_ref.at[core], sems.at[2], sems.at[3], other_core())
    copy.start()
    two.advance(nbits - 1)
    both_ref[core] = jnp.transpose(cols[core]).astype(BF)
    two.finish()
    whole = whole_two[...].reshape(count, 2 * half_two, D)
    wp_ref[...] = picked(
        D,
        whole[:, 0:pad_pro].reshape(count * pad_pro, D),
        lambda index: index,
        n_pro,
        pad_pro,
    )
    we_ref[...] = whole[:, pad_pro : pad_pro + pad_wide]
    wr_ref[...] = whole[:, pad_pro + pad_wide : pad_pro + 2 * pad_wide]
    copy.wait()


def front(weights, modulate, condition, bias, tok, count):
    far = lambda array: pltpu.with_memory_space_constraint(array, pltpu.HBM)
    weights, modulate, tok = [far(w) for w in weights], far(modulate), far(tok)
    nbits = count.bit_length() - 1
    n_att, n_pro, n_wide = (w.shape[0] for w in weights[:3])
    half = tok.shape[0]
    full = 2 * half
    half_one = up_to(n_att, 32) // 2
    half_two = up_to(up_to(n_pro, 16) + 2 * up_to(n_wide, 16), 32) // 2
    width = modulate.shape[0]
    lead = (2,) * nbits
    shape = jax.ShapeDtypeStruct
    sems = pltpu.SemaphoreType.DMA
    return pl.pallas_call(
        functools.partial(front_kernel, nbits),
        out_shape=[
            shape((count, 1, 2 * D), F32),
            shape((8, D), F32),
            shape((8, FF), F32),
            shape((D, D), BF),
            shape((count, up_to(n_wide, 16), D), BF),
            shape((count, up_to(n_wide, 16), D), BF),
            shape((3 * HALF, D), BF),
            shape((2, half, D), BF),
            shape((HALF_HEADS, 2, HEAD_DIM, half), BF),
            shape((HALF_HEADS, full, HEAD_DIM), BF),
            shape((HALF_HEADS, HEAD_DIM, full), BF),
            shape((HALF_HEADS, 2, HEAD_DIM, half), F32),
            shape((HALF_HEADS, 2, 8, half), F32),
            shape((2, half, HALF), BF),
        ],
        in_specs=[FAR] * 5 + [VM] * 2 + [FAR],
        out_specs=[VM] * 14,
        scratch_shapes=[
            pltpu.VMEM((4,) * (nbits // 2) + (2, half_one, D), BF),
            pltpu.VMEM(lead + (2, half_two, D), BF),
            pltpu.VMEM((2, half, D), BF),
            pltpu.VMEM((2, half, D), F32),
            pltpu.VMEM((1, 2 * D), F32),
            pltpu.VMEM((count, 1, width), F32),
            pltpu.VMEM((count, 1, width), F32),
            pltpu.VMEM((2, HALF, half), F32),
            pltpu.VMEM((half, HALF), BF),
            *[pltpu.VMEM(w.shape, F32) for w in (*weights, modulate)],
            sems((count,)),
            sems((count,)),
            sems((count,)),
            sems((count,)),
            sems((4,)),
            sems((6,)),
        ]
        + [sems((nbits // 2, 4)), sems((nbits // 2, 4)), sems((2,))]
        + Gather.scratch(nbits),
        compiler_params=params(24, 0),
        name="front",
    )(*weights, modulate, condition, bias, tok)


def branch_kernel(
    ctx_ref,
    tok_ref,
    cot_ref,
    mod_ref,
    wide_ref,
    wp_ref,
    we_ref,
    wr_ref,
    out_ref,
    mid_ref,
    gp_ref,
    ge_ref,
    gr_ref,
    sums_ref,
    wides_ref,
    both_ref,
    outgoing,
    sems,
):
    core = lax.axis_index("ctx")
    signal_core()
    half = tok_ref.shape[0]
    block = 512
    gate_one = mod_ref[2:3, :]
    shift_two = mod_ref[3:4, :]
    scale_two = 1.0 + mod_ref[4:5, :]
    gate_two = mod_ref[5:6, :]
    gp_ref[...] = jnp.zeros_like(gp_ref)
    ge_ref[...] = jnp.zeros_like(ge_ref)
    gr_ref[...] = jnp.zeros_like(gr_ref)
    sums_ref[...] = jnp.zeros_like(sums_ref)
    wides_ref[...] = jnp.zeros_like(wides_ref)

    def step(index, _):
        rows = pl.ds(pl.multiple_of(index * block, block), block)
        ctx = jnp.concatenate([ctx_ref[0, rows, :], ctx_ref[1, rows, :]], axis=1)
        attended = dot_nt(ctx, wp_ref[...]) + mod_ref[6:7, :]
        middle = tok_ref[rows, :].astype(F32) + gate_one * attended
        normed, inverse = normalize(middle)
        expand_in = (normed * scale_two + shift_two).astype(BF)
        hidden = dot_nt(expand_in, we_ref[...]) + wide_ref[0:1, :]
        squared = hidden * hidden
        bend = jnp.tanh(0.7978845608028654 * (hidden + 0.044715 * squared * hidden))
        rise = 0.5 * (1.0 + bend)
        act = (hidden * rise).astype(BF)
        slope = rise + 0.5 * hidden * (1.0 - bend * bend) * (
            0.7978845608028654 * (1.0 + 3.0 * 0.044715 * squared)
        )
        mlp_out = dot(act, wr_ref[...]) + mod_ref[7:8, :]
        out_ref[rows, :] = (middle + gate_two * mlp_out).astype(BF)
        grad_out = cot_ref[rows, :].astype(F32)
        grad_mlp = (gate_two * grad_out).astype(BF)
        gr_ref[...] += dot_tn(act, grad_mlp)
        grad_hidden = (dot_nt(grad_mlp, wr_ref[...]) * slope).astype(BF)
        ge_ref[...] += dot_tn(grad_hidden, expand_in)
        grad_in = dot(grad_hidden, we_ref[...])
        grad_middle = grad_out + norm_back(grad_in * scale_two, normed, inverse)
        mid_ref[rows, :] = grad_middle
        grad_attended = (gate_one * grad_middle).astype(BF)
        gp_ref[...] += dot_tn(grad_attended, ctx)
        back = dot(grad_attended, wp_ref[...]).astype(BF)
        first, second = back[:, :HALF], back[:, HALF:]
        both_ref[core, rows, :] = jnp.where(core == 0, first, second)
        outgoing[rows, :] = jnp.where(core == 0, second, first)
        add = lambda value: jnp.sum(value, axis=0, keepdims=True)
        sums_ref[0:1, :] += add(grad_out * mlp_out)
        sums_ref[1:2, :] += add(grad_in)
        sums_ref[2:3, :] += add(grad_in * normed)
        sums_ref[3:4, :] += add(grad_middle * attended)
        sums_ref[4:5, :] += add(grad_attended.astype(F32))
        sums_ref[5:6, :] += add(grad_mlp.astype(F32))
        wides_ref[0:1, :] += add(grad_hidden.astype(F32))
        return 0

    lax.fori_loop(0, half // block, step, 0)
    copy = remote(outgoing, both_ref.at[core], sems.at[0], sems.at[1], other_core())
    copy.start()
    copy.wait()


def branch(ctx, tok, cot, mod_rows, wide_rows, wp, we, wr):
    half = tok.shape[0]
    shape = jax.ShapeDtypeStruct
    return pl.pallas_call(
        branch_kernel,
        out_shape=[
            shape((half, D), BF),
            shape((half, D), F32),
            shape((D, D), F32),
            shape((FF, D), F32),
            shape((FF, D), F32),
            shape((8, D), F32),
            shape((8, FF), F32),
            shape((2, half, HALF), BF),
        ],
        in_specs=[VM] * 8,
        out_specs=[VM] * 8,
        scratch_shapes=[pltpu.VMEM((half, HALF), BF), pltpu.SemaphoreType.DMA((2,))],
        compiler_params=params(28, 2),
        name="branch",
    )(ctx, tok, cot, mod_rows, wide_rows, wp, we, wr)


def long_left(values):
    high, low = split_low(values)
    return jnp.concatenate([high, high, low], axis=1)


def long_right(values):
    high, low = split_low(values)
    return jnp.concatenate([high, low, high], axis=0)


def newton_factor(gram, eye, between):
    factor = None
    for sweep in range(NS_ITERS):
        right = long_right(gram)
        step = newton_a * eye + newton_b * gram + newton_c * dot(long_left(gram), right)
        left = long_left(step)
        if sweep < NS_ITERS - 1:
            gram = dot(long_left(dot(left, right)), long_right(step))
        factor = step if factor is None else dot(left, long_right(factor))
        for act in between.get(sweep, ()):
            act()
    return factor


def gram_of(turned):
    return lax.dot_general(
        turned,
        turned,
        (((0,), (0,)), ((), ())),
        precision=precise,
        preferred_element_type=F32,
    )


TILE = 128


def pack_gram(gram):
    tile = lambda r, c: gram[r * TILE : (r + 1) * TILE, c * TILE : (c + 1) * TILE]
    upper = jnp.concatenate([tile(0, 0), tile(1, 1), tile(2, 2)], axis=1)
    lower = jnp.concatenate([tile(1, 0), tile(2, 0), tile(2, 1)], axis=1)
    return upper, lower


def unpack_gram(upper, lower):
    tile = lambda packed, c: packed[:, c * TILE : (c + 1) * TILE]
    one, two, three = (tile(lower, c) for c in range(3))
    return jnp.concatenate(
        [
            jnp.concatenate([tile(upper, 0), one.T, two.T], axis=1),
            jnp.concatenate([one, tile(upper, 1), three.T], axis=1),
            jnp.concatenate([two, three, tile(upper, 2)], axis=1),
        ],
        axis=0,
    )


class Sum:
    def __init__(self, count, source, landed, whole, extra, send, recv, gsend, grecv, hsend, hrecv):
        self.pieces = source.shape[0]
        self.high = [b for b in range(count.bit_length() - 1) if (1 << b) >= self.pieces]
        self.source, self.landed, self.whole, self.extra = source, landed, whole, extra
        self.sems = send, recv, gsend, grecv, hsend, hrecv
        self.me = lax.axis_index("shard")
        self.low = lax.rem(self.me, self.pieces)

    def peer(self, step):
        place = lax.rem(self.low + step, self.pieces)
        return place, {"shard": self.me - self.low + place}

    def scatter(self, step):
        place, where = self.peer(step)
        send, recv = self.sems[:2]
        return remote(
            self.source.at[place], self.landed.at[self.low], send.at[step], recv.at[step], where
        )

    def spread(self, step):
        _, where = self.peer(step)
        send, recv = self.sems[2:4]
        part = self.whole.at[self.low]
        return remote(part, part, send.at[step], recv.at[step], where)

    def put(self, packed):
        self.source[...] = packed.reshape(self.source.shape)

    def start(self):
        for step in range(1, self.pieces):
            self.scatter(step).start()
        self.landed[self.low] = self.source[self.low]

    def land(self):
        for step in range(1, self.pieces):
            self.scatter(step).wait()
        return jnp.sum(self.landed[...], axis=0)

    def turn(self):
        self.give(self.land())

    def give(self, piece):
        self.whole[self.low] = piece
        send, recv = self.sems[4:]
        for at, bit in enumerate(self.high):
            copy = remote(
                self.whole.at[self.low],
                self.extra.at[at],
                send.at[at],
                recv.at[at],
                {"shard": flip(self.me, bit)},
            )
            copy.start()
            copy.wait()
            self.whole[self.low] += self.extra[at]
        for step in range(1, self.pieces):
            self.spread(step).start()

    def finish(self):
        for step in range(1, self.pieces):
            self.spread(step).wait()

    @staticmethod
    def scratch(count, rows):
        pieces = min(count, 16)
        high = max(count.bit_length() - pieces.bit_length(), 1)
        sems = pltpu.SemaphoreType.DMA
        block = pltpu.VMEM((pieces, rows // pieces, D), F32)
        return [block, block, block, pltpu.VMEM((high, rows // pieces, D), F32)] + [
            sems((pieces,))
        ] * 4 + [sems((high,))] * 2


SUM_REFS = 10


class FourSum:
    def __init__(self, count, source, first, between, second, whole, extra, *sems):
        self.source, self.first, self.between = source, first, between
        self.second, self.whole, self.extra = second, whole, extra
        self.sems = sems
        self.high = range(2, (count.bit_length() - 1) // 2)
        self.me = lax.axis_index("shard")
        self.plane, self.along = digit_of(self.me, 0), digit_of(self.me, 1)

    def copy(self, at, digit, step, pick):
        place, where = digit_peer(self.me, digit, step)
        src, dst = pick(place)
        return remote(src, dst, self.sems[2 * at].at[step], self.sems[2 * at + 1].at[step], where)

    def round(self, at):
        if at == 0:
            pick = lambda place: (self.source.at[:, place], self.first.at[self.plane])
        elif at == 1:
            pick = lambda place: (self.between.at[place], self.second.at[self.along])
        elif at == 2:
            part = self.whole.at[self.along, self.plane]
            pick = lambda place: (part, part)
        else:
            part = self.whole.at[:, self.plane]
            pick = lambda place: (part, part)
        return [self.copy(at, (0, 1, 1, 0)[at], step, pick) for step in range(1, 4)]

    def put(self, packed):
        self.source[...] = packed.reshape(self.source.shape)

    def start(self):
        for copy in self.round(0):
            copy.start()
        self.first[self.plane] = self.source[:, self.plane]

    def along_start(self):
        for copy in self.round(0):
            copy.wait()
        self.between[...] = jnp.sum(self.first[...], axis=0)
        for copy in self.round(1):
            copy.start()
        self.second[self.along] = self.between[self.along]

    def land(self):
        for copy in self.round(1):
            copy.wait()
        return jnp.sum(self.second[...], axis=0)

    def give(self, piece):
        self.whole[self.along, self.plane] = piece
        part = self.whole.at[self.along, self.plane]
        send, recv = self.sems[8:]
        for at, digit in enumerate(self.high):
            copies = []
            for step in range(1, 4):
                _, where = digit_peer(self.me, digit, step)
                slot = 4 * at + step
                copies.append(
                    remote(part, self.extra.at[slot], send.at[slot], recv.at[slot], where)
                )
            for copy in copies:
                copy.start()
            for copy in copies:
                copy.wait()
            for step in range(1, 4):
                self.whole[self.along, self.plane] += self.extra[4 * at + step]
        for copy in self.round(2):
            copy.start()

    def turn(self):
        self.give(self.land())

    def plane_start(self):
        for copy in self.round(2):
            copy.wait()
        for copy in self.round(3):
            copy.start()

    def finish(self):
        for copy in self.round(3):
            copy.wait()

    @staticmethod
    def scratch(count, rows):
        piece = (rows // 16, D)
        high = 4 * max((count.bit_length() - 1) // 2 - 2, 1)
        sems = pltpu.SemaphoreType.DMA
        return [
            pltpu.VMEM((4, 4) + piece, F32),
            pltpu.VMEM((4, 4) + piece, F32),
            pltpu.VMEM((4,) + piece, F32),
            pltpu.VMEM((4,) + piece, F32),
            pltpu.VMEM((4, 4) + piece, F32),
            pltpu.VMEM((high,) + piece, F32),
        ] + [sems((4,))] * 8 + [sems((high,))] * 2


FOUR_REFS = 16


def backward_kernel(
    nbits,
    scale_of,
    dctx_ref,
    xin_ref,
    q_ref,
    k_ref,
    v_ref,
    ctx_ref,
    lse_ref,
    w_ref,
    tok_ref,
    mid_ref,
    mod_ref,
    gp_ref,
    ge_ref,
    gr_ref,
    old_exp,
    old_red,
    sums_in,
    wides_in,
    grad_ref,
    att_ref,
    mine_ref,
    own_ref,
    piece_ref,
    *rest,
):
    stages = rest[:nbits]
    (
        low_out,
        first,
        total,
        k_turn,
        v_rows,
        dk_sum,
        dv_sum,
        dq_low,
        dk_low,
        dv_low,
        gw,
        bias_ref,
        outgoing,
        incoming,
        sems,
        asems,
        send,
        recv,
    ) = rest[nbits:-FOUR_REFS]
    one = FourSum(1 << nbits, *rest[-FOUR_REFS:])
    me = lax.axis_index("shard")
    core = lax.axis_index("ctx")
    signal_all(me, 1 << nbits)
    half = tok_ref.shape[0]
    lead = (slice(None),) * nbits
    wide = ge_ref.shape[-2]
    both = wide + gp_ref.shape[-2]
    last = nbits + 1
    main = lead + (slice(0, wide),)
    side_rows = lead + (slice(wide, both),)
    padded = low_out.shape[-2]
    spots = {1: 0, 2: 2, 3: 4, 4: 5}
    after = range(5, nbits + 2)

    def swap_main(which):
        return remote(
            (gr_ref, ge_ref)[which], first.at[main], send.at[0], recv.at[0], other_core()
        )

    swap_side = remote(gp_ref, first.at[side_rows], send.at[last], recv.at[last], other_core())

    def cube_step(which, step):
        order = scatter_orders(nbits)[which]
        bit = order[step]
        free = order[step + 1 :]
        there = flip(me, bit)
        if step < LOW_STEPS:
            rows = slice(0, padded if which == 0 else up_to(wide, 16))
            source = low_out
        else:
            rows = slice(0, both if which == 0 else wide)
            source = total
        return remote(
            source.at[cube_index(there, nbits, free, (rows,))],
            stages[step].at[(slice(None),) * len(free) + (rows,)],
            send.at[step + 1],
            recv.at[step + 1],
            {"shard": there},
        )

    def send_step(which, step):
        order = scatter_orders(nbits)[which]
        if step < LOW_STEPS:
            rows = slice(0, both if which == 0 else wide)
            index = cube_index(flip(me, order[step]), nbits, order[step + 1 :], (rows,))
            low_out[index] = total[index].astype(BF)
        cube_step(which, step).start()

    def last_swap(which):
        rows = slice(0, both if which == 0 else wide)
        return remote(
            own_ref.at[which, rows],
            own_ref.at[which, rows],
            send.at[nbits + 2],
            recv.at[nbits + 2],
            other_core(),
        )

    def progress(point):
        for which in range(2):

            @pl.when(core == which)
            def _():
                rows = slice(0, both if which == 0 else wide)
                order = scatter_orders(nbits)[which]
                if point == 0:
                    swap_main(which).start()
                    if which == 1:
                        swap_side.start()
                elif point == 1:
                    swap_main(which).wait()
                    if which == 0:
                        swap_side.wait_recv()
                        total[main] = ge_ref[...] + first[main]
                        total[side_rows] = gp_ref[...] + first[side_rows]
                        if padded > both:
                            low_out[lead + (slice(both, padded),)] = jnp.zeros(
                                (2,) * nbits + (padded - both, D), BF
                            )
                    else:
                        swap_side.wait_send()
                        total[main] = gr_ref[...] + first[main]
                elif point <= nbits + 1:
                    step = point - 2
                    cube_step(which, step).wait()
                    free = order[step + 1 :]
                    total[cube_index(me, nbits, free, (rows,))] += stages[step][
                        (slice(None),) * len(free) + (rows,)
                    ].astype(F32)
                if 1 <= point <= nbits:
                    send_step(which, point - 1)
                if point == nbits + 1:
                    own_ref[which, rows] = total[cube_index(me, nbits, (), (rows,))]
                    last_swap(which).start()
                if point == nbits + 2:
                    last_swap(which).wait_send()
                    last_swap(1 - which).wait_recv()

    turn = lambda value: jnp.transpose(value.astype(F32)).astype(BF)
    progress(0)
    for head in range(HALF_HEADS):
        k_turn[...] = turn(k_ref[head])
        v_rows[...] = turn(v_ref[head])
        dk_sum[...] = jnp.zeros_like(dk_sum)
        dv_sum[...] = jnp.zeros_like(dv_sum)

        def step(side, _):
            query = q_ref[head, side]
            down = dctx_ref[side, :, head * HEAD_DIM : (head + 1) * HEAD_DIM]
            down_turn = jnp.transpose(down.astype(F32))
            delta = jnp.sum(down_turn * ctx_ref[head, side], axis=0, keepdims=True)
            scores = dot(k_ref[head], query)
            probs = jnp.exp2(scores * LOG2E - lse_ref[head, side, 0:1, :])
            dv_sum[...] += dot(probs.astype(BF), down)
            grad_probs = dot(v_rows[...], down_turn.astype(BF))
            grad_scores = (probs * (grad_probs - delta)).astype(BF)
            dk_sum[...] += dot(grad_scores, turn(query))
            dq_low[head, side] = (
                jnp.transpose(dot(k_turn[...], grad_scores)) * (HEAD_DIM**-0.5)
            ).astype(BF)
            for at in range(2):
                for point in range(1, 5):
                    if spots[point] == head * 2 + at:
                        pl.when(side == at)(functools.partial(progress, point))
            return 0

        lax.fori_loop(0, 2, step, 0)
        dk_low[head] = dk_sum[...].reshape(2, half, HEAD_DIM).astype(BF)
        dv_low[head] = dv_sum[...].reshape(2, half, HEAD_DIM).astype(BF)

    def side_grads(side, fresh):
        pieces = [dq_low[h, side] for h in range(HALF_HEADS)]
        pieces += [dk_low[h, side] for h in range(HALF_HEADS)]
        pieces += [dv_low[h, side] for h in range(HALF_HEADS)]
        joined = jnp.concatenate(pieces, axis=1)
        grad = dot_tn(joined, xin_ref[side])
        sums = dot(jnp.ones((8, half), BF), joined)
        gw[...] = grad if fresh else gw[...] + grad
        bias_ref[...] = sums if fresh else bias_ref[...] + sums
        return dot(joined, w_ref[...])

    outgoing[...] = side_grads(1 - core, True)
    copy = remote(outgoing, incoming, sems.at[0], sems.at[1], other_core())
    copy.start()
    for point in after:
        progress(point)
    old = jnp.where(core == 0, old_exp[...], old_red[...])
    gram = gram_of(moment_decay * old + own_ref[core, 0:wide, :] * scale_of)
    one.put(jnp.concatenate(pack_gram(gram), axis=0))
    one.start()
    own = side_grads(core, False)

    def share(which):
        return [
            remote(
                att_ref.at[pl.ds(block * D + which * HALF, HALF), :],
                att_ref.at[pl.ds(block * D + which * HALF, HALF), :],
                asems.at[0, block],
                asems.at[1, block],
                other_core(),
            )
            for block in range(3)
        ]

    for which in range(2):

        @pl.when(core == which)
        def _():
            for block in range(3):
                att_ref[block * D + which * HALF : block * D + (which + 1) * HALF, :] = gw[
                    block * HALF : (block + 1) * HALF, :
                ]
            for part in share(which):
                part.start()

    one.along_start()
    copy.wait()
    grad_in = own + incoming[...]
    normed, inverse = normalize(tok_ref[...].astype(F32))
    scale = 1.0 + mod_ref[1:2, :]
    grad_ref[...] = mid_ref[...] + norm_back(grad_in * scale, normed, inverse)
    shift_sum = jnp.sum(grad_in, axis=0, keepdims=True)
    scale_sum = jnp.sum(grad_in * normed, axis=0, keepdims=True)
    row = lambda index: sums_in[index : index + 1, :]
    grad_mod = [shift_sum, scale_sum, row(3), row(1), row(2), row(0)]
    none = jnp.zeros((1, HALF), F32)

    def placed(part):
        return jnp.where(
            core == 0,
            jnp.concatenate([part, none], axis=1),
            jnp.concatenate([none, part], axis=1),
        )

    bias_grad = jnp.concatenate(
        grad_mod
        + [
            placed(bias_ref[0:1, 0:HALF]),
            placed(bias_ref[0:1, 2 * HALF :]),
            row(4),
            wides_in[0:1, :],
            row(5),
        ],
        axis=1,
    )
    grad_mod = jnp.concatenate(grad_mod, axis=1)
    count = 1 << nbits
    nbias, width = bias_grad.shape[1] // count, grad_mod.shape[1] // count
    mine_ref[...] = jnp.zeros_like(mine_ref)
    for to in range(count):
        mine_ref[to, :, 0:nbias] = bias_grad[:, to * nbias : (to + 1) * nbias]
        mine_ref[to, :, D : D + width] = grad_mod[:, to * width : (to + 1) * width]
    for which in range(2):

        @pl.when(core == which)
        def _():
            for part in share(which):
                part.wait_send()
            for part in share(1 - which):
                part.wait_recv()

    progress(nbits + 2)
    piece_ref[...] = one.land()


def attention_backward(
    dctx,
    xin,
    q,
    k,
    v,
    ctx,
    lse,
    weight,
    tok,
    mid,
    mod_rows,
    gp,
    ge,
    gr,
    old_exp,
    old_red,
    sums,
    wides,
    scale,
):
    half = tok.shape[0]
    full = 2 * half
    count, wide, _ = ge.shape
    both = wide + gp.shape[1]
    nbits = count.bit_length() - 1
    lead = (2,) * nbits
    shape = jax.ShapeDtypeStruct
    sems = pltpu.SemaphoreType.DMA
    return pl.pallas_call(
        functools.partial(backward_kernel, nbits, scale),
        out_shape=[
            shape((half, D), F32),
            shape((3 * D, D), F32),
            shape((count, 1, D + up_to(6 * D // count, 128)), F32),
            shape((2, both, D), F32),
            shape((2 * TILE // 16, D), F32),
        ],
        in_specs=[VM] * 18,
        out_specs=[VM] * 5,
        scratch_shapes=[
            pltpu.VMEM((2,) * (nbits - 1 - k) + ((up_to(both, 16), D) if k < LOW_STEPS else (both, D)), BF if k < LOW_STEPS else F32)
            for k in range(nbits)
        ]
        + [
            pltpu.VMEM(lead + (up_to(both, 16), D), BF),
            pltpu.VMEM(lead + (both, D), F32),
            pltpu.VMEM(lead + (both, D), F32),
            pltpu.VMEM((HEAD_DIM, full), BF),
            pltpu.VMEM((full, HEAD_DIM), BF),
            pltpu.VMEM((full, HEAD_DIM), F32),
            pltpu.VMEM((full, HEAD_DIM), F32),
            pltpu.VMEM((HALF_HEADS, 2, half, HEAD_DIM), BF),
            pltpu.VMEM((HALF_HEADS, 2, half, HEAD_DIM), BF),
            pltpu.VMEM((HALF_HEADS, 2, half, HEAD_DIM), BF),
            pltpu.VMEM((3 * HALF, D), F32),
            pltpu.VMEM((8, 3 * HALF), F32),
            pltpu.VMEM((half, D), F32),
            pltpu.VMEM((half, D), F32),
            sems((2,)),
            sems((2, 3)),
            sems((nbits + 3,)),
            sems((nbits + 3,)),
        ]
        + FourSum.scratch(count, 2 * TILE),
        compiler_params=params(35, 3),
        name="attend_backward",
    )(
        dctx,
        xin,
        q,
        k,
        v,
        ctx,
        lse,
        weight,
        tok,
        mid,
        mod_rows,
        gp.reshape(lead + gp.shape[1:]),
        ge.reshape(lead + ge.shape[1:]),
        gr.reshape(lead + gr.shape[1:]),
        old_exp,
        old_red,
        sums,
        wides,
    )


def tail_kernel(
    count,
    scale,
    local,
    att_ref,
    own_ref,
    piece_ref,
    mine_ref,
    small_ref,
    wmod_ref,
    old_mod,
    old_att,
    old_pro,
    fac_ref,
    rows_ref,
    modg_ref,
    bias_ref,
    cond_ref,
    *rest,
):
    digits = (count.bit_length() - 1) // 2
    lands, added = rest[:digits], rest[digits : 2 * digits]
    got, theirs, back_send, back, upper_half, other_half = rest[2 * digits : 2 * digits + 6]
    send, recv, msend, mrecv, bsend, brecv, csem, fsem = rest[2 * digits + 6 : 2 * digits + 14]
    sums = rest[2 * digits + 14 :]
    one = FourSum(count, *sums[:FOUR_REFS])
    two = Sum(count, *sums[FOUR_REFS : FOUR_REFS + SUM_REFS])
    late = Sum(count, *sums[FOUR_REFS + SUM_REFS :])
    me = lax.axis_index("shard")
    core = lax.axis_index("ctx")
    signal_all(me, count)
    n_att, n_pro, wide = local
    padded = att_ref.shape[-2]
    half_rows = rows_ref.shape[1]

    begin = pl.multiple_of(core * (padded - half_rows), 8)

    def rows_source(digit, place):
        lead = (slice(None),) * (digits - digit - 1) + (place,)
        if digit == 0:
            return att_ref.at[lead + (pl.ds(begin, half_rows),)]
        return added[digit - 1].at[lead]

    def rows_copies(digit):
        copies = []
        for step in range(1, 4):
            place, where = digit_peer(me, digit, step)
            copies.append(
                remote(
                    rows_source(digit, place),
                    lands[digit].at[digit_of(me, digit)],
                    send.at[digit, step],
                    recv.at[digit, step],
                    where,
                )
            )
        return copies

    def rows_start(digit):
        for copy in rows_copies(digit):
            copy.start()
        own = digit_of(me, digit)
        lands[digit][own] = rows_source(digit, own)[...]

    def rows_add(digit):
        for copy in rows_copies(digit):
            copy.wait()
        total = jnp.sum(lands[digit][...], axis=0)
        if digit < digits - 1:
            added[digit][...] = total
            rows_start(digit + 1)
        else:
            rows_ref[core] = total
            swap_rows(core).start()

    def swap_rows(which):
        part = rows_ref.at[which]
        return remote(part, part, csem.at[2], csem.at[3], other_core())

    copies = []
    for step in range(1, count):
        to = lax.rem(me + step, count)
        copy = remote(mine_ref.at[to], got.at[me], msend.at[step], mrecv.at[step], {"shard": to})
        copy.start()
        copies.append(copy)
    got[me] = mine_ref[me]
    one.give(piece_ref[...])
    rows_start(0)
    for copy in copies:
        copy.wait()
    swap = remote(got, theirs, csem.at[0], csem.at[1], other_core())
    swap.start()
    cond = small_ref[:, 0, 0:D]
    silu_low = silu_of(cond).astype(BF).astype(F32)
    one.plane_start()
    swap.wait()
    width = old_mod.shape[0]
    both = got[:, 0, :] + theirs[:, 0, :]
    grad_mod = both[:, D : D + width]
    bias_ref[...] = jnp.sum(both[:, 0:D], axis=0, keepdims=True)
    raw = lax.dot_general(
        grad_mod,
        silu_low,
        (((0,), (0,)), ((), ())),
        precision=precise,
        preferred_element_type=F32,
    )
    modg_ref[...] = raw

    @pl.when(core == 0)
    def _():
        grad = own_ref[0, wide : wide + n_pro, :] * scale
        two.put(jnp.concatenate(pack_gram(gram_of(moment_decay * old_pro[...] + grad)), axis=0))

    @pl.when(core == 1)
    def _():
        grad = modg_ref[...] * scale
        two.put(jnp.concatenate(pack_gram(gram_of(moment_decay * old_mod[...] + grad)), axis=0))

    two.start()
    part = jnp.dot(
        grad_mod, wmod_ref[...].astype(BF).astype(F32), precision=precise, preferred_element_type=F32
    )
    for row in range(count):
        back_send[row] = part[row : row + 1, :]
    back[me] = back_send[me]
    backs = []
    for step in range(1, count):
        to = lax.rem(me + step, count)
        copy = remote(
            back_send.at[to], back.at[me], bsend.at[step], brecv.at[step], {"shard": to}
        )
        copy.start()
        backs.append(copy)

    def condition_grads():
        for copy in backs:
            copy.wait()
        grad_silu = jnp.sum(back[...], axis=0)
        own = small_ref[me][:, 0:D]
        gate = jax.nn.sigmoid(own)
        cond_ref[...] = grad_silu * (gate + own * gate * (1.0 - gate))

    def late_start():
        swap_rows(core).wait_send()
        swap_rows(1 - core).wait_recv()
        skip = 2 * half_rows - padded
        grad = jnp.concatenate([rows_ref[0], rows_ref[1, skip:]], axis=0)[0:n_att] * scale
        upper, lower = pack_gram(gram_of(moment_decay * old_att[...] + grad))
        late.put(jnp.where(core == 0, upper, lower))
        late.start()

    halves = remote(upper_half, other_half, csem.at[4], csem.at[5], other_core())

    def late_swap():
        late.finish()
        upper_half[...] = late.whole[...].reshape(TILE, D)
        halves.start()

    row = lax.broadcasted_iota(jnp.int32, (D, D), 0)
    column = lax.broadcasted_iota(jnp.int32, (D, D), 1)
    eye = (row == column).astype(F32)

    def solve(gram, between):
        diagonal = jnp.sum(gram * eye, axis=0, keepdims=True)
        size = 1.0 / (jnp.sqrt(jnp.sum(diagonal, axis=1, keepdims=True)) + 1e-07)
        return newton_factor((gram * size) * size, eye, between) * size

    def solve_sum(item, between):
        packed = item.whole[...].reshape(2 * TILE, D)
        return solve(unpack_gram(packed[0:TILE], packed[TILE:]), between)

    def pass_factor(index, at):
        part = fac_ref.at[index]
        return remote(part, part, fsem.at[0, at], fsem.at[1, at], other_core())

    place_one, place_two = 3 + core, 2 - 2 * core
    rows_add(0)
    one.finish()
    last_rows = [functools.partial(rows_add, digit) for digit in range(1, digits)]
    fac_ref[place_one] = solve_sum(
        one,
        {
            0: [two.turn],
            1: last_rows,
            2: [late_start],
            4: [late.turn, condition_grads],
        },
    )
    first_pass = pass_factor(place_one, 0)
    first_pass.start()
    two.finish()
    fac_ref[place_two] = solve_sum(two, {2: [late_swap]})
    second_pass = pass_factor(place_two, 1)
    second_pass.start()
    halves.wait()
    mine_half, their_half = upper_half[...], other_half[...]
    fac_ref[1] = solve(
        unpack_gram(
            jnp.where(core == 0, mine_half, their_half),
            jnp.where(core == 0, their_half, mine_half),
        ),
        {},
    )
    first_pass.wait()
    second_pass.wait()


def tail(att, own, piece, mine, small_all, wmod, olds, scale, local):
    count, padded, _ = att.shape
    digits = (count.bit_length() - 1) // 2
    half_rows = up_to(padded // 2, 8)
    width = wmod.shape[0]
    sems = pltpu.SemaphoreType.DMA
    shape = jax.ShapeDtypeStruct
    return pl.pallas_call(
        functools.partial(tail_kernel, count, scale, local),
        out_shape=[
            shape((5, D, D), F32),
            shape((2, half_rows, D), F32),
            shape((width, D), F32),
            shape((1, D), F32),
            shape((1, D), F32),
        ],
        in_specs=[VM] * 9,
        out_specs=[VM] * 5,
        scratch_shapes=[
            pltpu.VMEM((4,) * (digits - d) + (half_rows, D), F32) for d in range(digits)
        ]
        + [pltpu.VMEM((4,) * (digits - d - 1) + (half_rows, D), F32) for d in range(digits)]
        + [
            pltpu.VMEM(mine.shape, F32),
            pltpu.VMEM(mine.shape, F32),
            pltpu.VMEM((count, 1, D), F32),
            pltpu.VMEM((count, 1, D), F32),
            pltpu.VMEM((TILE, D), F32),
            pltpu.VMEM((TILE, D), F32),
            sems((digits, 4)),
            sems((digits, 4)),
            sems((count,)),
            sems((count,)),
            sems((count,)),
            sems((count,)),
            sems((6,)),
            sems((2, 2)),
        ]
        + FourSum.scratch(count, 2 * TILE)
        + Sum.scratch(count, 2 * TILE)
        + Sum.scratch(count, TILE),
        compiler_params=params(14, 4),
        name="tail",
    )(att.reshape((4,) * digits + (padded, D)), own, piece, mine, small_all, wmod, *olds[:3])


def update_kernel(scale, rates, bounds, *refs):
    fac_ref, att_ref, modg_ref, own_ref = refs[:4]
    olds, masters, done = refs[4:9], refs[9:14], refs[14:16]
    outs, final, sem = refs[16:31], refs[31:33], refs[33]
    copies = [
        pltpu.make_async_copy(source, target, sem.at[at])
        for at, (source, target) in enumerate(zip(done, final))
    ]
    for copy in copies:
        copy.start()
    n_att, wide, n_pro = bounds
    first_rows = att_ref.shape[1]
    skip = 2 * first_rows - up_to(n_att, 8)
    joined = jnp.concatenate([att_ref[0], att_ref[1, skip:]], axis=0)
    grads = [
        modg_ref[...],
        joined[0:n_att],
        own_ref[0, wide : wide + n_pro, :],
        own_ref[0, 0:wide, :],
        own_ref[1, 0:wide, :],
    ]
    for index in range(5):
        grad = grads[index] * scale
        moment = moment_decay * olds[index][...] + grad
        direction = dot_three(moment, fac_ref[index])
        outs[3 * index][...] = grad
        outs[3 * index + 1][...] = masters[index][...] - rates[index] * direction
        outs[3 * index + 2][...] = moment
    for copy in copies:
        copy.wait()


def update(fac, att, modg, own, olds, masters, done, scale, count):
    shape = jax.ShapeDtypeStruct
    out = []
    for m in masters:
        out += [shape(m.shape, F32)] * 3
    out += [shape(value.shape, value.dtype) for value in done]
    anywhere = pl.BlockSpec(memory_space=pl.ANY)
    rates = [matrix_rate * 0.2 * math.sqrt(max(D, m.shape[0] * count)) for m in masters]
    bounds = (olds[1].shape[0], olds[3].shape[0], olds[2].shape[0])
    return pl.pallas_call(
        functools.partial(update_kernel, scale, rates, bounds),
        out_shape=out,
        in_specs=[VM] * 14 + [anywhere] * 2,
        out_specs=[VM] * 15 + [anywhere] * 2,
        scratch_shapes=[pltpu.SemaphoreType.DMA((2,))],
        compiler_params=params(8),
        name="update",
    )(fac, att, modg, own, *olds, *masters, *done)


def on_device(
    tokens,
    condition,
    cotangent,
    modulate_weight,
    attend_weight,
    project_weight,
    expand_weight,
    reduce_weight,
    bias_flat,
    modulate_moment,
    attend_moment,
    project_moment,
    expand_moment,
    reduce_moment,
    bias_moment,
):
    count = lax.axis_size("shard")
    full = tokens.shape[1] * lax.axis_size("ctx")
    olds = [
        m.T
        for m in (modulate_moment, attend_moment, project_moment, expand_moment, reduce_moment)
    ]
    masters = [
        w.T
        for w in (modulate_weight, attend_weight, project_weight, expand_weight, reduce_weight)
    ]
    n_att, n_pro, n_wide = (w.shape[0] for w in masters[1:4])
    nbias = bias_flat.shape[0]
    tok = tokens[0]
    (
        small_all,
        mod_rows,
        wide_rows,
        project_turn,
        expand_turn,
        reduce_turn,
        weight_core,
        xin,
        q,
        k,
        v,
        ctx_turn,
        lse,
        ctx,
    ) = front(masters[1:], masters[0], condition, bias_flat[None], tok, count)
    block_out, mid, gp, ge, gr, sums, wides, dctx = branch(
        ctx,
        tok,
        cotangent[0],
        mod_rows,
        wide_rows,
        project_turn,
        expand_turn[:, :n_wide].reshape(FF, D),
        reduce_turn[:, :n_wide].reshape(FF, D),
    )
    gp = pad_rows(gp.reshape(count, n_pro, D), up_to(n_pro, 8))
    scale = 1.0 / math.sqrt(tokens.shape[0] * count * full)
    tokens_grad, att, mine, mlp_rows, piece = attention_backward(
        dctx,
        xin,
        q,
        k,
        v,
        ctx_turn,
        lse,
        weight_core,
        tok,
        mid,
        mod_rows,
        gp,
        ge.reshape(count, n_wide, D),
        gr.reshape(count, n_wide, D),
        olds[3],
        olds[4],
        sums,
        wides,
        scale,
    )
    att = pad_rows(att.reshape(count, n_att, D), up_to(n_att, 8))
    fac, att_rows, modg, bias_sum, condition_rows = tail(
        att, mlp_rows, piece, mine, small_all, masters[0], olds, scale, (n_att, n_pro, n_wide)
    )
    done = (block_out[None], tokens_grad[None])
    out = update(fac, att_rows, modg, mlp_rows, olds, masters, done, scale, count)
    bias_grad = bias_sum[0, :nbias] * scale
    bias_new = moment_decay * bias_moment + bias_grad
    result = [*out[15:], condition_rows]
    result += [value.T for value in out[:15]]
    result += [bias_grad, bias_flat - bias_rate * bias_new, bias_new]
    return tuple(result)


def solution(mesh):
    tok = P("shard", "ctx", None)
    row = P("shard", None)
    col = P(None, "shard")
    flat = P("shard")
    return jax.shard_map(
        on_device,
        mesh=mesh,
        in_specs=(tok, row, tok) + (col,) * 5 + (flat,) + (col,) * 5 + (flat,),
        out_specs=(tok, tok, row) + (col,) * 15 + (flat,) * 3,
        check_vma=False,
    )
```

```python
import functools
import math

import jax
import jax.numpy as jnp
from jax import lax
from jax.experimental import pallas as pl
from jax.experimental.pallas import tpu as pltpu
from jax.sharding import PartitionSpec as P

D = 384
FF = 1536
HEADS = 6
HEAD_DIM = 64
NS_ITERS = 5
LOW_STEPS = 1
HALF_HEADS = HEADS // 2
HALF = HALF_HEADS * HEAD_DIM

norm_eps = 1e-06
newton_a = 3.4445
newton_b = -4.775
newton_c = 2.0315
moment_decay = 0.95
matrix_rate = 0.5
bias_rate = 0.1
precise = lax.Precision.HIGHEST
LOG2E = 1.4426950408889634

MESH = pl.DeviceIdType.MESH
BF = jnp.bfloat16
F32 = jnp.float32
VM = pl.BlockSpec(memory_space=pltpu.VMEM)
FAR = pl.BlockSpec(memory_space=pltpu.HBM)


def params(megabytes, collective=None):
    limit = megabytes * 2**20
    if collective is None:
        return pltpu.CompilerParams(vmem_limit_bytes=limit)
    return pltpu.CompilerParams(
        collective_id=collective, has_side_effects=True, vmem_limit_bytes=limit
    )


def dot(left, right):
    return jnp.dot(left, right, preferred_element_type=F32)


def dot_nt(left, right):
    return lax.dot_general(left, right, (((1,), (1,)), ((), ())), preferred_element_type=F32)


def dot_tn(left, right):
    return lax.dot_general(left, right, (((0,), (0,)), ((), ())), preferred_element_type=F32)


def split_low(values):
    high = values.astype(BF)
    return high, (values - high.astype(F32)).astype(BF)


def dot_three(left, right, op=dot):
    left_high, left_low = split_low(left)
    right_high, right_low = split_low(right)
    return op(left_high, right_high) + (op(left_high, right_low) + op(left_low, right_high))


def silu_of(values):
    return values * jax.nn.sigmoid(values)


def normalize(values):
    centered = values - jnp.mean(values, axis=-1, keepdims=True)
    inverse = lax.rsqrt(jnp.mean(centered * centered, axis=-1, keepdims=True) + norm_eps)
    return (centered * inverse, inverse)


def norm_back(grad_normed, normed, inverse):
    first = jnp.mean(grad_normed, axis=-1, keepdims=True)
    second = jnp.mean(grad_normed * normed, axis=-1, keepdims=True)
    return (grad_normed - first - normed * second) * inverse


def pad_rows(array, rows):
    return jnp.pad(array, ((0, 0),) * (array.ndim - 2) + ((0, rows - array.shape[-2]), (0, 0)))


def up_to(value, step):
    return -(-value // step) * step


def bit_of(value, bit):
    return lax.rem(value // (1 << bit), 2)


def flip(me, bit):
    return me + (1 - 2 * bit_of(me, bit)) * (1 << bit)


def other_core():
    return {"ctx": 1 - lax.axis_index("ctx")}


def signal_cube(me, nbits):
    sem = pltpu.get_barrier_semaphore()
    for bit in range(nbits):
        pl.semaphore_signal(
            sem, inc=1, device_id={"shard": flip(me, bit)}, device_id_type=MESH
        )
    pl.semaphore_signal(sem, inc=1, device_id=other_core(), device_id_type=MESH)
    pl.semaphore_wait(sem, nbits + 1)


def signal_all(me, count):
    sem = pltpu.get_barrier_semaphore()
    for step in range(1, count):
        pl.semaphore_signal(
            sem, inc=1, device_id={"shard": lax.rem(me + step, count)}, device_id_type=MESH
        )
    pl.semaphore_signal(sem, inc=1, device_id=other_core(), device_id_type=MESH)
    pl.semaphore_wait(sem, count)


def signal_core():
    sem = pltpu.get_barrier_semaphore()
    pl.semaphore_signal(sem, inc=1, device_id=other_core(), device_id_type=MESH)
    pl.semaphore_wait(sem, 1)


def remote(src, dst, send, recv, where):
    return pltpu.make_async_remote_copy(
        src, dst, send, recv, device_id=where, device_id_type=MESH
    )


def orders(nbits):
    up = list(range(nbits))
    return up, ([1, 0] + up[2:] if nbits >= 2 else up)


def scatter_orders(nbits):
    up = list(range(nbits))
    return up, (up[1:] + up[:1] if nbits >= 2 else up)


def digit_of(value, digit):
    return lax.rem(value // (1 << (2 * digit)), 4)


def digit_peer(me, digit, step):
    own = digit_of(me, digit)
    place = lax.rem(own + step, 4)
    return place, {"shard": me + (place - own) * (1 << (2 * digit))}


def cube_index(who, nbits, free, tail=()):
    lead = tuple(
        slice(None) if (nbits - 1 - d) in free else bit_of(who, nbits - 1 - d)
        for d in range(nbits)
    )
    return lead + tuple(tail)


class Gather:
    def __init__(self, nbits, whole, send, recv, psend, precv):
        self.nbits, self.whole = nbits, whole
        self.sems = send, recv, psend, precv
        self.me = lax.axis_index("shard")

    def step(self, which, at):
        seq = orders(self.nbits)[which][::-1]
        bit = seq[at]
        part = self.whole.at[cube_index(self.me, self.nbits, seq[:at], (which,))]
        send, recv = self.sems[:2]
        return remote(part, part, send.at[at], recv.at[at], {"shard": flip(self.me, bit)})

    def forward(self, which, at):
        seq = orders(self.nbits)[which][::-1]
        bit = seq[at]
        part = self.whole.at[
            cube_index(flip(self.me, bit), self.nbits, seq[:at], (which,))
        ]
        send, recv = self.sems[2:]
        return remote(part, part, send.at[at], recv.at[at], other_core())

    def each(self, act):
        for which in range(2):
            pl.when(lax.axis_index("ctx") == which)(functools.partial(act, which))

    def start(self):
        self.each(lambda which: self.step(which, 0).start())

    def advance(self, at):
        def act(which):
            self.step(which, at).wait()
            if at + 1 < self.nbits:
                self.step(which, at + 1).start()
            self.forward(which, at).start()

        self.each(act)

    def finish(self):
        def act(which):
            for at in range(self.nbits):
                self.forward(which, at).wait_send()
            for at in range(self.nbits):
                self.forward(1 - which, at).wait_recv()

        self.each(act)

    @staticmethod
    def scratch(nbits):
        return [pltpu.SemaphoreType.DMA((nbits,))] * 4


class FourGather:
    def __init__(self, digits, whole, send, recv, swap):
        self.digits, self.whole = digits, whole
        self.sems, self.swap = (send, recv), swap
        self.me = lax.axis_index("shard")
        self.core = lax.axis_index("ctx")

    def round(self, at):
        digit = self.digits - 1 - at
        own = tuple(digit_of(self.me, d) for d in range(digit, -1, -1))
        part = self.whole.at[(slice(None),) * at + own + (self.core,)]
        send, recv = self.sems
        copies = []
        for step in range(1, 4):
            _, where = digit_peer(self.me, digit, step)
            copies.append(remote(part, part, send.at[at, step], recv.at[at, step], where))
        return copies

    def start(self, at):
        for copy in self.round(at):
            copy.start()

    def wait(self, at):
        for copy in self.round(at):
            copy.wait()

    def forward(self):
        part = self.whole.at[(slice(None),) * self.digits + (self.core,)]
        return remote(part, part, self.swap.at[0], self.swap.at[1], other_core())


def front_kernel(
    nbits,
    att_far,
    pro_far,
    exp_far,
    red_far,
    mod_far,
    cond_ref,
    bias_ref,
    tok_ref,
    small_all,
    rows_ref,
    wide_ref,
    wp_ref,
    we_ref,
    wr_ref,
    w_ref,
    xin_ref,
    q_ref,
    k_ref,
    v_ref,
    ctx_ref,
    lse_ref,
    both_ref,
    whole_one,
    whole_two,
    tok_all,
    normed_all,
    small_own,
    mod_all,
    mod_send,
    cols,
    outgoing,
    att_own,
    pro_own,
    exp_own,
    red_own,
    mod_own,
    ssend,
    srecv,
    msend,
    mrecv,
    sems,
    near,
    *gsems,
):
    count = 1 << nbits
    me = lax.axis_index("shard")
    core = lax.axis_index("ctx")
    loads = [
        pltpu.make_async_copy(far, own, near.at[at])
        for at, (far, own) in enumerate(
            [
                (att_far, att_own),
                (pro_far, pro_own),
                (exp_far, exp_own),
                (red_far, red_own),
                (mod_far, mod_own),
                (tok_ref, tok_all.at[core]),
            ]
        )
    ]
    for load in loads:
        load.start()
    signal_all(me, count)
    n_att, n_pro, n_wide = att_own.shape[0], pro_own.shape[0], exp_own.shape[0]
    width, nbias = mod_own.shape[0], bias_ref.shape[1]
    half = tok_ref.shape[0]
    digits = nbits // 2
    own = cube_index(me, nbits, ())
    one = FourGather(digits, whole_one, *gsems[:3])
    two = Gather(nbits, whole_two, *gsems[3:])
    half_one, half_two = whole_one.shape[-2], whole_two.shape[-2]
    pad_pro, pad_wide = up_to(n_pro, 16), up_to(n_wide, 16)

    def joined(parts, total):
        pieces = []
        for part, rows in parts:
            pieces.append(part[...])
            if rows > part.shape[0]:
                pieces.append(jnp.zeros((rows - part.shape[0], D), F32))
        rows = sum(rows for _, rows in parts)
        if total > rows:
            pieces.append(jnp.zeros((total - rows, D), F32))
        return jnp.concatenate(pieces, axis=0).astype(BF)

    small_own[...] = jnp.zeros_like(small_own)
    small_own[:, 0:D] = cond_ref[...].astype(F32)
    small_own[:, D : D + nbias] = bias_ref[...].astype(BF).astype(F32)
    spread = []
    for step in range(1, count):
        to = lax.rem(me + step, count)
        copy = remote(
            small_own, small_all.at[me], ssend.at[step], srecv.at[step], {"shard": to}
        )
        copy.start()
        spread.append(copy)
    for load in loads:
        load.wait()
    halves = joined([(att_own, n_att)], 2 * half_one)
    place = tuple(digit_of(me, d) for d in range(digits - 1, -1, -1))
    whole_one[place + (core,)] = jnp.where(core == 0, halves[:half_one], halves[half_one:])
    one.start(0)
    toks = remote(tok_ref, tok_all.at[core], sems.at[0], sems.at[1], other_core())
    toks.start()
    small_all[me] = small_own[...]
    whole_two[own] = joined(
        [(pro_own, pad_pro), (exp_own, pad_wide), (red_own, pad_wide)], 2 * half_two
    ).reshape(2, half_two, D)
    block = 256

    def norm_side(side):
        def norm_block(index, _):
            rows = pl.ds(pl.multiple_of(index * block, block), block)
            normed, _inverse = normalize(tok_all[side, rows, :].astype(F32))
            normed_all[side, rows, :] = normed
            return 0

        lax.fori_loop(0, half // block, norm_block, 0)

    one.wait(0)
    one.start(1)
    for copy in spread:
        copy.wait()
    silu_low = silu_of(small_all[:, 0, 0:D]).astype(BF)
    part = dot_nt(silu_low, mod_own[...].astype(BF))
    for row in range(count):
        mod_send[row] = part[row : row + 1, :]
    mods = []
    for step in range(1, count):
        to = lax.rem(me + step, count)
        copy = remote(
            mod_send.at[to], mod_all.at[me], msend.at[step], mrecv.at[step], {"shard": to}
        )
        copy.start()
        mods.append(copy)
    mod_all[me] = mod_send[me]
    norm_side(core)
    toks.wait()
    norm_side(1 - core)
    biases = jnp.concatenate([small_all[s, :, D : D + nbias] for s in range(count)], axis=1)
    for at in range(1, digits):
        one.wait(at)
        if at + 1 < digits:
            one.start(at + 1)
    forward = one.forward()
    forward.start()
    two.start()
    for copy in mods:
        copy.wait()
    mods = jnp.concatenate([mod_all[s] for s in range(count)], axis=1)
    mods = mods + biases[:, 0 : 6 * D]
    rows_ref[...] = jnp.zeros_like(rows_ref)
    for row in range(6):
        rows_ref[row : row + 1, :] = mods[:, row * D : (row + 1) * D]
    rows_ref[6:7, :] = biases[:, 8 * D : 9 * D]
    rows_ref[7:8, :] = biases[:, 9 * D + FF :]
    wide_ref[...] = jnp.broadcast_to(biases[:, 9 * D : 9 * D + FF], (8, FF))
    shift = mods[:, 0:D]
    scale = 1.0 + mods[:, D : 2 * D]

    def shift_block(index, _):
        rows = pl.ds(pl.multiple_of(index * block, block), block)
        for side in range(2):
            xin_ref[side, rows, :] = (normed_all[side, rows, :] * scale + shift).astype(BF)
        return 0

    lax.fori_loop(0, half // block, shift_block, 0)

    def turned_bias(at):
        row = biases[:, at * D : (at + 1) * D]
        row = jnp.where(core == 0, row[:, 0:HALF], row[:, HALF:])
        return jnp.transpose(jnp.broadcast_to(row, (8, HALF)))[:, 0:1]

    query_bias, value_bias = turned_bias(6), turned_bias(7)

    def picked(rows, source, wanted, local, stride):
        index = lax.broadcasted_iota(jnp.int32, (rows, 1), 0)
        goal = wanted(index).astype(F32)
        block_of = jnp.floor((goal + 0.5) * (1.0 / local))
        place = goal + block_of * float(stride - local)
        column = lax.broadcasted_iota(jnp.int32, (rows, source.shape[0]), 1).astype(F32)
        return dot((column == place).astype(BF), source).astype(BF)

    forward.wait()
    for part in range(3):
        w_ref[part * HALF : (part + 1) * HALF, :] = picked(
            HALF,
            whole_one[...].reshape(count * 2 * half_one, D),
            lambda index: index + (part * D + core * HALF),
            n_att,
            2 * half_one,
        )
    for side in range(2):
        xin = xin_ref[side]
        rows = pl.ds(side * half, half)
        query = dot_nt(w_ref[0:HALF, :], xin) + query_bias
        value = dot_nt(w_ref[2 * HALF :, :], xin) + value_bias
        query = query.astype(BF) * jnp.asarray(HEAD_DIM**-0.5, BF)
        value = value.astype(BF)
        for head in range(HALF_HEADS):
            part = slice(head * HEAD_DIM, (head + 1) * HEAD_DIM)
            q_ref[head, side] = query[part, :]
            v_ref[head, :, rows] = value[part, :]
            k_ref[head, rows, :] = dot_nt(
                xin, w_ref[HALF + head * HEAD_DIM : HALF + (head + 1) * HEAD_DIM, :]
            ).astype(BF)
    two.advance(0)

    def attend(step, _):
        head = step // 2
        side = lax.rem(step, 2)
        scores = dot(k_ref[head], q_ref[head, side])
        top = jnp.max(scores, axis=0, keepdims=True)
        shifted = jnp.exp2((scores - top) * LOG2E)
        total = jnp.sum(shifted, axis=0, keepdims=True)
        probs = (shifted * (1.0 / total)).astype(BF)
        out = dot(v_ref[head], probs)
        ctx_ref[head, side] = out
        lse_ref[head, side] = jnp.broadcast_to(top * LOG2E + jnp.log2(total), (8, half))
        cols[side, pl.ds(pl.multiple_of(head * HEAD_DIM, HEAD_DIM), HEAD_DIM), :] = out
        for at in range(1, nbits - 1):
            pl.when(step == min(2 * at - 1, 4))(functools.partial(two.advance, at))
        return 0

    lax.fori_loop(0, 2 * HALF_HEADS, attend, 0)
    outgoing[...] = jnp.transpose(cols[1 - core]).astype(BF)
    copy = remote(outgoing, both_ref.at[core], sems.at[2], sems.at[3], other_core())
    copy.start()
    two.advance(nbits - 1)
    both_ref[core] = jnp.transpose(cols[core]).astype(BF)
    two.finish()
    whole = whole_two[...].reshape(count, 2 * half_two, D)
    wp_ref[...] = picked(
        D,
        whole[:, 0:pad_pro].reshape(count * pad_pro, D),
        lambda index: index,
        n_pro,
        pad_pro,
    )
    we_ref[...] = whole[:, pad_pro : pad_pro + pad_wide]
    wr_ref[...] = whole[:, pad_pro + pad_wide : pad_pro + 2 * pad_wide]
    copy.wait()


def front(weights, modulate, condition, bias, tok, count):
    far = lambda array: pltpu.with_memory_space_constraint(array, pltpu.HBM)
    weights, modulate, tok = [far(w) for w in weights], far(modulate), far(tok)
    nbits = count.bit_length() - 1
    n_att, n_pro, n_wide = (w.shape[0] for w in weights[:3])
    half = tok.shape[0]
    full = 2 * half
    half_one = up_to(n_att, 32) // 2
    half_two = up_to(up_to(n_pro, 16) + 2 * up_to(n_wide, 16), 32) // 2
    width = modulate.shape[0]
    lead = (2,) * nbits
    shape = jax.ShapeDtypeStruct
    sems = pltpu.SemaphoreType.DMA
    return pl.pallas_call(
        functools.partial(front_kernel, nbits),
        out_shape=[
            shape((count, 1, 2 * D), F32),
            shape((8, D), F32),
            shape((8, FF), F32),
            shape((D, D), BF),
            shape((count, up_to(n_wide, 16), D), BF),
            shape((count, up_to(n_wide, 16), D), BF),
            shape((3 * HALF, D), BF),
            shape((2, half, D), BF),
            shape((HALF_HEADS, 2, HEAD_DIM, half), BF),
            shape((HALF_HEADS, full, HEAD_DIM), BF),
            shape((HALF_HEADS, HEAD_DIM, full), BF),
            shape((HALF_HEADS, 2, HEAD_DIM, half), F32),
            shape((HALF_HEADS, 2, 8, half), F32),
            shape((2, half, HALF), BF),
        ],
        in_specs=[FAR] * 5 + [VM] * 2 + [FAR],
        out_specs=[VM] * 14,
        scratch_shapes=[
            pltpu.VMEM((4,) * (nbits // 2) + (2, half_one, D), BF),
            pltpu.VMEM(lead + (2, half_two, D), BF),
            pltpu.VMEM((2, half, D), BF),
            pltpu.VMEM((2, half, D), F32),
            pltpu.VMEM((1, 2 * D), F32),
            pltpu.VMEM((count, 1, width), F32),
            pltpu.VMEM((count, 1, width), F32),
            pltpu.VMEM((2, HALF, half), F32),
            pltpu.VMEM((half, HALF), BF),
            *[pltpu.VMEM(w.shape, F32) for w in (*weights, modulate)],
            sems((count,)),
            sems((count,)),
            sems((count,)),
            sems((count,)),
            sems((4,)),
            sems((6,)),
        ]
        + [sems((nbits // 2, 4)), sems((nbits // 2, 4)), sems((2,))]
        + Gather.scratch(nbits),
        compiler_params=params(24, 0),
        name="front",
    )(*weights, modulate, condition, bias, tok)


def branch_kernel(
    ctx_ref,
    tok_ref,
    cot_far,
    mod_ref,
    wide_ref,
    wp_ref,
    we_ref,
    wr_ref,
    out_ref,
    mid_ref,
    gp_ref,
    ge_ref,
    gr_ref,
    sums_ref,
    wides_ref,
    both_ref,
    outgoing,
    sems,
    cot_ref,
    near,
):
    core = lax.axis_index("ctx")
    load = pltpu.make_async_copy(cot_far, cot_ref, near)
    load.start()
    signal_core()
    half = tok_ref.shape[0]
    block = 512
    gate_one = mod_ref[2:3, :]
    shift_two = mod_ref[3:4, :]
    scale_two = 1.0 + mod_ref[4:5, :]
    gate_two = mod_ref[5:6, :]
    gp_ref[...] = jnp.zeros_like(gp_ref)
    ge_ref[...] = jnp.zeros_like(ge_ref)
    gr_ref[...] = jnp.zeros_like(gr_ref)
    sums_ref[...] = jnp.zeros_like(sums_ref)
    wides_ref[...] = jnp.zeros_like(wides_ref)

    def step(index, _):
        rows = pl.ds(pl.multiple_of(index * block, block), block)
        ctx = jnp.concatenate([ctx_ref[0, rows, :], ctx_ref[1, rows, :]], axis=1)
        attended = dot_nt(ctx, wp_ref[...]) + mod_ref[6:7, :]
        middle = tok_ref[rows, :].astype(F32) + gate_one * attended
        normed, inverse = normalize(middle)
        expand_in = (normed * scale_two + shift_two).astype(BF)
        hidden = dot_nt(expand_in, we_ref[...]) + wide_ref[0:1, :]
        squared = hidden * hidden
        bend = jnp.tanh(0.7978845608028654 * (hidden + 0.044715 * squared * hidden))
        rise = 0.5 * (1.0 + bend)
        act = (hidden * rise).astype(BF)
        slope = rise + 0.5 * hidden * (1.0 - bend * bend) * (
            0.7978845608028654 * (1.0 + 3.0 * 0.044715 * squared)
        )
        mlp_out = dot(act, wr_ref[...]) + mod_ref[7:8, :]
        out_ref[rows, :] = (middle + gate_two * mlp_out).astype(BF)
        grad_out = cot_ref[rows, :].astype(F32)
        grad_mlp = (gate_two * grad_out).astype(BF)
        gr_ref[...] += dot_tn(act, grad_mlp)
        grad_hidden = (dot_nt(grad_mlp, wr_ref[...]) * slope).astype(BF)
        ge_ref[...] += dot_tn(grad_hidden, expand_in)
        grad_in = dot(grad_hidden, we_ref[...])
        grad_middle = grad_out + norm_back(grad_in * scale_two, normed, inverse)
        mid_ref[rows, :] = grad_middle
        grad_attended = (gate_one * grad_middle).astype(BF)
        gp_ref[...] += dot_tn(grad_attended, ctx)
        back = dot(grad_attended, wp_ref[...]).astype(BF)
        first, second = back[:, :HALF], back[:, HALF:]
        both_ref[core, rows, :] = jnp.where(core == 0, first, second)
        outgoing[rows, :] = jnp.where(core == 0, second, first)
        add = lambda value: jnp.sum(value, axis=0, keepdims=True)
        sums_ref[0:1, :] += add(grad_out * mlp_out)
        sums_ref[1:2, :] += add(grad_in)
        sums_ref[2:3, :] += add(grad_in * normed)
        sums_ref[3:4, :] += add(grad_middle * attended)
        sums_ref[4:5, :] += add(grad_attended.astype(F32))
        sums_ref[5:6, :] += add(grad_mlp.astype(F32))
        wides_ref[0:1, :] += add(grad_hidden.astype(F32))
        return 0

    load.wait()
    lax.fori_loop(0, half // block, step, 0)
    copy = remote(outgoing, both_ref.at[core], sems.at[0], sems.at[1], other_core())
    copy.start()
    copy.wait()


def branch(ctx, tok, cot, mod_rows, wide_rows, wp, we, wr):
    half = tok.shape[0]
    cot = pltpu.with_memory_space_constraint(cot, pltpu.HBM)
    shape = jax.ShapeDtypeStruct
    return pl.pallas_call(
        branch_kernel,
        out_shape=[
            shape((half, D), BF),
            shape((half, D), F32),
            shape((D, D), F32),
            shape((FF, D), F32),
            shape((FF, D), F32),
            shape((8, D), F32),
            shape((8, FF), F32),
            shape((2, half, HALF), BF),
        ],
        in_specs=[VM] * 2 + [FAR] + [VM] * 5,
        out_specs=[VM] * 8,
        scratch_shapes=[
            pltpu.VMEM((half, HALF), BF),
            pltpu.SemaphoreType.DMA((2,)),
            pltpu.VMEM((half, D), BF),
            pltpu.SemaphoreType.DMA,
        ],
        compiler_params=params(28, 2),
        name="branch",
    )(ctx, tok, cot, mod_rows, wide_rows, wp, we, wr)


def long_left(values):
    high, low = split_low(values)
    return jnp.concatenate([high, high, low], axis=1)


def long_right(values):
    high, low = split_low(values)
    return jnp.concatenate([high, low, high], axis=0)


def newton_factor(gram, eye, between):
    factor = None
    for sweep in range(NS_ITERS):
        right = long_right(gram)
        step = newton_a * eye + newton_b * gram + newton_c * dot(long_left(gram), right)
        left = long_left(step)
        if sweep < NS_ITERS - 1:
            gram = dot(long_left(dot(left, right)), long_right(step))
        factor = step if factor is None else dot(left, long_right(factor))
        for act in between.get(sweep, ()):
            act()
    return factor


def gram_of(turned):
    return lax.dot_general(
        turned,
        turned,
        (((0,), (0,)), ((), ())),
        precision=precise,
        preferred_element_type=F32,
    )


TILE = 128


def pack_gram(gram):
    tile = lambda r, c: gram[r * TILE : (r + 1) * TILE, c * TILE : (c + 1) * TILE]
    upper = jnp.concatenate([tile(0, 0), tile(1, 1), tile(2, 2)], axis=1)
    lower = jnp.concatenate([tile(1, 0), tile(2, 0), tile(2, 1)], axis=1)
    return upper, lower


def unpack_gram(upper, lower):
    tile = lambda packed, c: packed[:, c * TILE : (c + 1) * TILE]
    one, two, three = (tile(lower, c) for c in range(3))
    return jnp.concatenate(
        [
            jnp.concatenate([tile(upper, 0), one.T, two.T], axis=1),
            jnp.concatenate([one, tile(upper, 1), three.T], axis=1),
            jnp.concatenate([two, three, tile(upper, 2)], axis=1),
        ],
        axis=0,
    )


class Sum:
    def __init__(self, count, source, landed, whole, extra, send, recv, gsend, grecv, hsend, hrecv):
        self.pieces = source.shape[0]
        self.high = [b for b in range(count.bit_length() - 1) if (1 << b) >= self.pieces]
        self.source, self.landed, self.whole, self.extra = source, landed, whole, extra
        self.sems = send, recv, gsend, grecv, hsend, hrecv
        self.me = lax.axis_index("shard")
        self.low = lax.rem(self.me, self.pieces)

    def peer(self, step):
        place = lax.rem(self.low + step, self.pieces)
        return place, {"shard": self.me - self.low + place}

    def scatter(self, step):
        place, where = self.peer(step)
        send, recv = self.sems[:2]
        return remote(
            self.source.at[place], self.landed.at[self.low], send.at[step], recv.at[step], where
        )

    def spread(self, step):
        _, where = self.peer(step)
        send, recv = self.sems[2:4]
        part = self.whole.at[self.low]
        return remote(part, part, send.at[step], recv.at[step], where)

    def put(self, packed):
        self.source[...] = packed.reshape(self.source.shape)

    def start(self):
        for step in range(1, self.pieces):
            self.scatter(step).start()
        self.landed[self.low] = self.source[self.low]

    def land(self):
        for step in range(1, self.pieces):
            self.scatter(step).wait()
        return jnp.sum(self.landed[...], axis=0)

    def turn(self):
        self.give(self.land())

    def give(self, piece):
        self.whole[self.low] = piece
        send, recv = self.sems[4:]
        for at, bit in enumerate(self.high):
            copy = remote(
                self.whole.at[self.low],
                self.extra.at[at],
                send.at[at],
                recv.at[at],
                {"shard": flip(self.me, bit)},
            )
            copy.start()
            copy.wait()
            self.whole[self.low] += self.extra[at]
        for step in range(1, self.pieces):
            self.spread(step).start()

    def finish(self):
        for step in range(1, self.pieces):
            self.spread(step).wait()

    @staticmethod
    def scratch(count, rows):
        pieces = min(count, 16)
        high = max(count.bit_length() - pieces.bit_length(), 1)
        sems = pltpu.SemaphoreType.DMA
        block = pltpu.VMEM((pieces, rows // pieces, D), F32)
        return [block, block, block, pltpu.VMEM((high, rows // pieces, D), F32)] + [
            sems((pieces,))
        ] * 4 + [sems((high,))] * 2


SUM_REFS = 10


class FourSum:
    def __init__(self, count, source, first, between, second, whole, extra, *sems):
        self.source, self.first, self.between = source, first, between
        self.second, self.whole, self.extra = second, whole, extra
        self.sems = sems
        self.high = range(2, (count.bit_length() - 1) // 2)
        self.me = lax.axis_index("shard")
        self.plane, self.along = digit_of(self.me, 0), digit_of(self.me, 1)

    def copy(self, at, digit, step, pick):
        place, where = digit_peer(self.me, digit, step)
        src, dst = pick(place)
        return remote(src, dst, self.sems[2 * at].at[step], self.sems[2 * at + 1].at[step], where)

    def round(self, at):
        if at == 0:
            pick = lambda place: (self.source.at[:, place], self.first.at[self.plane])
        elif at == 1:
            pick = lambda place: (self.between.at[place], self.second.at[self.along])
        elif at == 2:
            part = self.whole.at[self.along, self.plane]
            pick = lambda place: (part, part)
        else:
            part = self.whole.at[:, self.plane]
            pick = lambda place: (part, part)
        return [self.copy(at, (0, 1, 1, 0)[at], step, pick) for step in range(1, 4)]

    def put(self, packed):
        self.source[...] = packed.reshape(self.source.shape)

    def start(self):
        for copy in self.round(0):
            copy.start()
        self.first[self.plane] = self.source[:, self.plane]

    def along_start(self):
        for copy in self.round(0):
            copy.wait()
        self.between[...] = jnp.sum(self.first[...], axis=0)
        for copy in self.round(1):
            copy.start()
        self.second[self.along] = self.between[self.along]

    def land(self):
        for copy in self.round(1):
            copy.wait()
        return jnp.sum(self.second[...], axis=0)

    def give(self, piece):
        self.whole[self.along, self.plane] = piece
        part = self.whole.at[self.along, self.plane]
        send, recv = self.sems[8:]
        for at, digit in enumerate(self.high):
            copies = []
            for step in range(1, 4):
                _, where = digit_peer(self.me, digit, step)
                slot = 4 * at + step
                copies.append(
                    remote(part, self.extra.at[slot], send.at[slot], recv.at[slot], where)
                )
            for copy in copies:
                copy.start()
            for copy in copies:
                copy.wait()
            for step in range(1, 4):
                self.whole[self.along, self.plane] += self.extra[4 * at + step]
        for copy in self.round(2):
            copy.start()

    def turn(self):
        self.give(self.land())

    def plane_start(self):
        for copy in self.round(2):
            copy.wait()
        for copy in self.round(3):
            copy.start()

    def finish(self):
        for copy in self.round(3):
            copy.wait()

    @staticmethod
    def scratch(count, rows):
        piece = (rows // 16, D)
        high = 4 * max((count.bit_length() - 1) // 2 - 2, 1)
        sems = pltpu.SemaphoreType.DMA
        return [
            pltpu.VMEM((4, 4) + piece, F32),
            pltpu.VMEM((4, 4) + piece, F32),
            pltpu.VMEM((4,) + piece, F32),
            pltpu.VMEM((4,) + piece, F32),
            pltpu.VMEM((4, 4) + piece, F32),
            pltpu.VMEM((high,) + piece, F32),
        ] + [sems((4,))] * 8 + [sems((high,))] * 2


FOUR_REFS = 16


def backward_kernel(
    nbits,
    scale_of,
    dctx_ref,
    xin_ref,
    q_ref,
    k_ref,
    v_ref,
    ctx_ref,
    lse_ref,
    w_ref,
    tok_ref,
    mid_ref,
    mod_ref,
    gp_ref,
    ge_ref,
    gr_ref,
    old_exp,
    old_red,
    sums_in,
    wides_in,
    grad_ref,
    att_ref,
    mine_ref,
    own_ref,
    piece_ref,
    *rest,
):
    stages = rest[:nbits]
    (
        low_out,
        first,
        total,
        k_turn,
        v_rows,
        dk_sum,
        dv_sum,
        dq_low,
        dk_low,
        dv_low,
        gw,
        bias_ref,
        outgoing,
        incoming,
        sems,
        asems,
        send,
        recv,
    ) = rest[nbits:-FOUR_REFS]
    one = FourSum(1 << nbits, *rest[-FOUR_REFS:])
    me = lax.axis_index("shard")
    core = lax.axis_index("ctx")
    signal_all(me, 1 << nbits)
    half = tok_ref.shape[0]
    lead = (slice(None),) * nbits
    wide = ge_ref.shape[-2]
    both = wide + gp_ref.shape[-2]
    last = nbits + 1
    main = lead + (slice(0, wide),)
    side_rows = lead + (slice(wide, both),)
    padded = low_out.shape[-2]
    spots = {1: 0, 2: 2, 3: 4, 4: 5}
    after = range(5, nbits + 2)

    def swap_main(which):
        return remote(
            (gr_ref, ge_ref)[which], first.at[main], send.at[0], recv.at[0], other_core()
        )

    swap_side = remote(gp_ref, first.at[side_rows], send.at[last], recv.at[last], other_core())

    def cube_step(which, step):
        order = scatter_orders(nbits)[which]
        bit = order[step]
        free = order[step + 1 :]
        there = flip(me, bit)
        if step < LOW_STEPS:
            rows = slice(0, padded if which == 0 else up_to(wide, 16))
            source = low_out
        else:
            rows = slice(0, both if which == 0 else wide)
            source = total
        return remote(
            source.at[cube_index(there, nbits, free, (rows,))],
            stages[step].at[(slice(None),) * len(free) + (rows,)],
            send.at[step + 1],
            recv.at[step + 1],
            {"shard": there},
        )

    def send_step(which, step):
        order = scatter_orders(nbits)[which]
        if step < LOW_STEPS:
            rows = slice(0, both if which == 0 else wide)
            index = cube_index(flip(me, order[step]), nbits, order[step + 1 :], (rows,))
            low_out[index] = total[index].astype(BF)
        cube_step(which, step).start()

    def last_swap(which):
        rows = slice(0, both if which == 0 else wide)
        return remote(
            own_ref.at[which, rows],
            own_ref.at[which, rows],
            send.at[nbits + 2],
            recv.at[nbits + 2],
            other_core(),
        )

    def progress(point):
        for which in range(2):

            @pl.when(core == which)
            def _():
                rows = slice(0, both if which == 0 else wide)
                order = scatter_orders(nbits)[which]
                if point == 0:
                    swap_main(which).start()
                    if which == 1:
                        swap_side.start()
                elif point == 1:
                    swap_main(which).wait()
                    if which == 0:
                        swap_side.wait_recv()
                        total[main] = ge_ref[...] + first[main]
                        total[side_rows] = gp_ref[...] + first[side_rows]
                        if padded > both:
                            low_out[lead + (slice(both, padded),)] = jnp.zeros(
                                (2,) * nbits + (padded - both, D), BF
                            )
                    else:
                        swap_side.wait_send()
                        total[main] = gr_ref[...] + first[main]
                elif point <= nbits + 1:
                    step = point - 2
                    cube_step(which, step).wait()
                    free = order[step + 1 :]
                    total[cube_index(me, nbits, free, (rows,))] += stages[step][
                        (slice(None),) * len(free) + (rows,)
                    ].astype(F32)
                if 1 <= point <= nbits:
                    send_step(which, point - 1)
                if point == nbits + 1:
                    own_ref[which, rows] = total[cube_index(me, nbits, (), (rows,))]
                    last_swap(which).start()
                if point == nbits + 2:
                    last_swap(which).wait_send()
                    last_swap(1 - which).wait_recv()

    turn = lambda value: jnp.transpose(value.astype(F32)).astype(BF)
    progress(0)
    for head in range(HALF_HEADS):
        k_turn[...] = turn(k_ref[head])
        v_rows[...] = turn(v_ref[head])
        dk_sum[...] = jnp.zeros_like(dk_sum)
        dv_sum[...] = jnp.zeros_like(dv_sum)

        def step(side, _):
            query = q_ref[head, side]
            down = dctx_ref[side, :, head * HEAD_DIM : (head + 1) * HEAD_DIM]
            down_turn = jnp.transpose(down.astype(F32))
            delta = jnp.sum(down_turn * ctx_ref[head, side], axis=0, keepdims=True)
            scores = dot(k_ref[head], query)
            probs = jnp.exp2(scores * LOG2E - lse_ref[head, side, 0:1, :])
            dv_sum[...] += dot(probs.astype(BF), down)
            grad_probs = dot(v_rows[...], down_turn.astype(BF))
            grad_scores = (probs * (grad_probs - delta)).astype(BF)
            dk_sum[...] += dot(grad_scores, turn(query))
            dq_low[head, side] = (
                jnp.transpose(dot(k_turn[...], grad_scores)) * (HEAD_DIM**-0.5)
            ).astype(BF)
            for at in range(2):
                for point in range(1, 5):
                    if spots[point] == head * 2 + at:
                        pl.when(side == at)(functools.partial(progress, point))
            return 0

        lax.fori_loop(0, 2, step, 0)
        dk_low[head] = dk_sum[...].reshape(2, half, HEAD_DIM).astype(BF)
        dv_low[head] = dv_sum[...].reshape(2, half, HEAD_DIM).astype(BF)

    def side_grads(side, fresh):
        pieces = [dq_low[h, side] for h in range(HALF_HEADS)]
        pieces += [dk_low[h, side] for h in range(HALF_HEADS)]
        pieces += [dv_low[h, side] for h in range(HALF_HEADS)]
        joined = jnp.concatenate(pieces, axis=1)
        grad = dot_tn(joined, xin_ref[side])
        sums = dot(jnp.ones((8, half), BF), joined)
        gw[...] = grad if fresh else gw[...] + grad
        bias_ref[...] = sums if fresh else bias_ref[...] + sums
        return dot(joined, w_ref[...])

    outgoing[...] = side_grads(1 - core, True)
    copy = remote(outgoing, incoming, sems.at[0], sems.at[1], other_core())
    copy.start()
    for point in after:
        progress(point)
    old = jnp.where(core == 0, old_exp[...], old_red[...])
    gram = gram_of(moment_decay * old + own_ref[core, 0:wide, :] * scale_of)
    one.put(jnp.concatenate(pack_gram(gram), axis=0))
    one.start()
    own = side_grads(core, False)

    def share(which):
        return [
            remote(
                att_ref.at[pl.ds(block * D + which * HALF, HALF), :],
                att_ref.at[pl.ds(block * D + which * HALF, HALF), :],
                asems.at[0, block],
                asems.at[1, block],
                other_core(),
            )
            for block in range(3)
        ]

    for which in range(2):

        @pl.when(core == which)
        def _():
            for block in range(3):
                att_ref[block * D + which * HALF : block * D + (which + 1) * HALF, :] = gw[
                    block * HALF : (block + 1) * HALF, :
                ]
            for part in share(which):
                part.start()

    one.along_start()
    copy.wait()
    grad_in = own + incoming[...]
    normed, inverse = normalize(tok_ref[...].astype(F32))
    scale = 1.0 + mod_ref[1:2, :]
    grad_ref[...] = mid_ref[...] + norm_back(grad_in * scale, normed, inverse)
    shift_sum = jnp.sum(grad_in, axis=0, keepdims=True)
    scale_sum = jnp.sum(grad_in * normed, axis=0, keepdims=True)
    row = lambda index: sums_in[index : index + 1, :]
    grad_mod = [shift_sum, scale_sum, row(3), row(1), row(2), row(0)]
    none = jnp.zeros((1, HALF), F32)

    def placed(part):
        return jnp.where(
            core == 0,
            jnp.concatenate([part, none], axis=1),
            jnp.concatenate([none, part], axis=1),
        )

    bias_grad = jnp.concatenate(
        grad_mod
        + [
            placed(bias_ref[0:1, 0:HALF]),
            placed(bias_ref[0:1, 2 * HALF :]),
            row(4),
            wides_in[0:1, :],
            row(5),
        ],
        axis=1,
    )
    grad_mod = jnp.concatenate(grad_mod, axis=1)
    count = 1 << nbits
    nbias, width = bias_grad.shape[1] // count, grad_mod.shape[1] // count
    mine_ref[...] = jnp.zeros_like(mine_ref)
    for to in range(count):
        mine_ref[to, :, 0:nbias] = bias_grad[:, to * nbias : (to + 1) * nbias]
        mine_ref[to, :, D : D + width] = grad_mod[:, to * width : (to + 1) * width]
    for which in range(2):

        @pl.when(core == which)
        def _():
            for part in share(which):
                part.wait_send()
            for part in share(1 - which):
                part.wait_recv()

    progress(nbits + 2)
    piece_ref[...] = one.land()


def attention_backward(
    dctx,
    xin,
    q,
    k,
    v,
    ctx,
    lse,
    weight,
    tok,
    mid,
    mod_rows,
    gp,
    ge,
    gr,
    old_exp,
    old_red,
    sums,
    wides,
    scale,
):
    half = tok.shape[0]
    full = 2 * half
    count, wide, _ = ge.shape
    both = wide + gp.shape[1]
    nbits = count.bit_length() - 1
    lead = (2,) * nbits
    shape = jax.ShapeDtypeStruct
    sems = pltpu.SemaphoreType.DMA
    return pl.pallas_call(
        functools.partial(backward_kernel, nbits, scale),
        out_shape=[
            shape((half, D), F32),
            shape((3 * D, D), F32),
            shape((count, 1, D + up_to(6 * D // count, 128)), F32),
            shape((2, both, D), F32),
            shape((2 * TILE // 16, D), F32),
        ],
        in_specs=[VM] * 18,
        out_specs=[VM] * 5,
        scratch_shapes=[
            pltpu.VMEM((2,) * (nbits - 1 - k) + ((up_to(both, 16), D) if k < LOW_STEPS else (both, D)), BF if k < LOW_STEPS else F32)
            for k in range(nbits)
        ]
        + [
            pltpu.VMEM(lead + (up_to(both, 16), D), BF),
            pltpu.VMEM(lead + (both, D), F32),
            pltpu.VMEM(lead + (both, D), F32),
            pltpu.VMEM((HEAD_DIM, full), BF),
            pltpu.VMEM((full, HEAD_DIM), BF),
            pltpu.VMEM((full, HEAD_DIM), F32),
            pltpu.VMEM((full, HEAD_DIM), F32),
            pltpu.VMEM((HALF_HEADS, 2, half, HEAD_DIM), BF),
            pltpu.VMEM((HALF_HEADS, 2, half, HEAD_DIM), BF),
            pltpu.VMEM((HALF_HEADS, 2, half, HEAD_DIM), BF),
            pltpu.VMEM((3 * HALF, D), F32),
            pltpu.VMEM((8, 3 * HALF), F32),
            pltpu.VMEM((half, D), F32),
            pltpu.VMEM((half, D), F32),
            sems((2,)),
            sems((2, 3)),
            sems((nbits + 3,)),
            sems((nbits + 3,)),
        ]
        + FourSum.scratch(count, 2 * TILE),
        compiler_params=params(35, 3),
        name="attend_backward",
    )(
        dctx,
        xin,
        q,
        k,
        v,
        ctx,
        lse,
        weight,
        tok,
        mid,
        mod_rows,
        gp.reshape(lead + gp.shape[1:]),
        ge.reshape(lead + ge.shape[1:]),
        gr.reshape(lead + gr.shape[1:]),
        old_exp,
        old_red,
        sums,
        wides,
    )


def tail_kernel(
    count,
    scale,
    local,
    att_ref,
    own_ref,
    piece_ref,
    mine_ref,
    small_ref,
    wmod_ref,
    old_mod,
    old_att,
    old_pro,
    fac_ref,
    rows_ref,
    modg_ref,
    bias_ref,
    cond_ref,
    *rest,
):
    digits = (count.bit_length() - 1) // 2
    lands, added = rest[:digits], rest[digits : 2 * digits]
    got, theirs, back_send, back, upper_half, other_half = rest[2 * digits : 2 * digits + 6]
    send, recv, msend, mrecv, bsend, brecv, csem, fsem = rest[2 * digits + 6 : 2 * digits + 14]
    sums = rest[2 * digits + 14 :]
    one = FourSum(count, *sums[:FOUR_REFS])
    two = Sum(count, *sums[FOUR_REFS : FOUR_REFS + SUM_REFS])
    late = Sum(count, *sums[FOUR_REFS + SUM_REFS :])
    me = lax.axis_index("shard")
    core = lax.axis_index("ctx")
    signal_all(me, count)
    n_att, n_pro, wide = local
    padded = att_ref.shape[-2]
    half_rows = rows_ref.shape[1]

    begin = pl.multiple_of(core * (padded - half_rows), 8)

    def rows_source(digit, place):
        lead = (slice(None),) * (digits - digit - 1) + (place,)
        if digit == 0:
            return att_ref.at[lead + (pl.ds(begin, half_rows),)]
        return added[digit - 1].at[lead]

    def rows_copies(digit):
        copies = []
        for step in range(1, 4):
            place, where = digit_peer(me, digit, step)
            copies.append(
                remote(
                    rows_source(digit, place),
                    lands[digit].at[digit_of(me, digit)],
                    send.at[digit, step],
                    recv.at[digit, step],
                    where,
                )
            )
        return copies

    def rows_start(digit):
        for copy in rows_copies(digit):
            copy.start()
        own = digit_of(me, digit)
        lands[digit][own] = rows_source(digit, own)[...]

    def rows_add(digit):
        for copy in rows_copies(digit):
            copy.wait()
        total = jnp.sum(lands[digit][...], axis=0)
        if digit < digits - 1:
            added[digit][...] = total
            rows_start(digit + 1)
        else:
            rows_ref[core] = total
            swap_rows(core).start()

    def swap_rows(which):
        part = rows_ref.at[which]
        return remote(part, part, csem.at[2], csem.at[3], other_core())

    copies = []
    for step in range(1, count):
        to = lax.rem(me + step, count)
        copy = remote(mine_ref.at[to], got.at[me], msend.at[step], mrecv.at[step], {"shard": to})
        copy.start()
        copies.append(copy)
    got[me] = mine_ref[me]
    one.give(piece_ref[...])
    rows_start(0)
    for copy in copies:
        copy.wait()
    swap = remote(got, theirs, csem.at[0], csem.at[1], other_core())
    swap.start()
    cond = small_ref[:, 0, 0:D]
    silu_low = silu_of(cond).astype(BF).astype(F32)
    one.plane_start()
    swap.wait()
    width = old_mod.shape[0]
    both = got[:, 0, :] + theirs[:, 0, :]
    grad_mod = both[:, D : D + width]
    bias_ref[...] = jnp.sum(both[:, 0:D], axis=0, keepdims=True)
    raw = lax.dot_general(
        grad_mod,
        silu_low,
        (((0,), (0,)), ((), ())),
        precision=precise,
        preferred_element_type=F32,
    )
    modg_ref[...] = raw

    @pl.when(core == 0)
    def _():
        grad = own_ref[0, wide : wide + n_pro, :] * scale
        two.put(jnp.concatenate(pack_gram(gram_of(moment_decay * old_pro[...] + grad)), axis=0))

    @pl.when(core == 1)
    def _():
        grad = modg_ref[...] * scale
        two.put(jnp.concatenate(pack_gram(gram_of(moment_decay * old_mod[...] + grad)), axis=0))

    two.start()
    part = jnp.dot(
        grad_mod, wmod_ref[...].astype(BF).astype(F32), precision=precise, preferred_element_type=F32
    )
    for row in range(count):
        back_send[row] = part[row : row + 1, :]
    back[me] = back_send[me]
    backs = []
    for step in range(1, count):
        to = lax.rem(me + step, count)
        copy = remote(
            back_send.at[to], back.at[me], bsend.at[step], brecv.at[step], {"shard": to}
        )
        copy.start()
        backs.append(copy)

    def condition_grads():
        for copy in backs:
            copy.wait()
        grad_silu = jnp.sum(back[...], axis=0)
        own = small_ref[me][:, 0:D]
        gate = jax.nn.sigmoid(own)
        cond_ref[...] = grad_silu * (gate + own * gate * (1.0 - gate))

    def late_start():
        swap_rows(core).wait_send()
        swap_rows(1 - core).wait_recv()
        skip = 2 * half_rows - padded
        grad = jnp.concatenate([rows_ref[0], rows_ref[1, skip:]], axis=0)[0:n_att] * scale
        upper, lower = pack_gram(gram_of(moment_decay * old_att[...] + grad))
        late.put(jnp.where(core == 0, upper, lower))
        late.start()

    halves = remote(upper_half, other_half, csem.at[4], csem.at[5], other_core())

    def late_swap():
        late.finish()
        upper_half[...] = late.whole[...].reshape(TILE, D)
        halves.start()

    row = lax.broadcasted_iota(jnp.int32, (D, D), 0)
    column = lax.broadcasted_iota(jnp.int32, (D, D), 1)
    eye = (row == column).astype(F32)

    def solve(gram, between):
        diagonal = jnp.sum(gram * eye, axis=0, keepdims=True)
        size = 1.0 / (jnp.sqrt(jnp.sum(diagonal, axis=1, keepdims=True)) + 1e-07)
        return newton_factor((gram * size) * size, eye, between) * size

    def solve_sum(item, between):
        packed = item.whole[...].reshape(2 * TILE, D)
        return solve(unpack_gram(packed[0:TILE], packed[TILE:]), between)

    def pass_factor(index, at):
        part = fac_ref.at[index]
        return remote(part, part, fsem.at[0, at], fsem.at[1, at], other_core())

    place_one, place_two = 3 + core, 2 - 2 * core
    rows_add(0)
    one.finish()
    last_rows = [functools.partial(rows_add, digit) for digit in range(1, digits)]
    fac_ref[place_one] = solve_sum(
        one,
        {
            0: [two.turn],
            1: last_rows,
            2: [late_start],
            4: [late.turn, condition_grads],
        },
    )
    first_pass = pass_factor(place_one, 0)
    first_pass.start()
    two.finish()
    fac_ref[place_two] = solve_sum(two, {2: [late_swap]})
    second_pass = pass_factor(place_two, 1)
    second_pass.start()
    halves.wait()
    mine_half, their_half = upper_half[...], other_half[...]
    fac_ref[1] = solve(
        unpack_gram(
            jnp.where(core == 0, mine_half, their_half),
            jnp.where(core == 0, their_half, mine_half),
        ),
        {},
    )
    first_pass.wait()
    second_pass.wait()


def tail(att, own, piece, mine, small_all, wmod, olds, scale, local):
    count, padded, _ = att.shape
    digits = (count.bit_length() - 1) // 2
    half_rows = up_to(padded // 2, 8)
    width = wmod.shape[0]
    sems = pltpu.SemaphoreType.DMA
    shape = jax.ShapeDtypeStruct
    return pl.pallas_call(
        functools.partial(tail_kernel, count, scale, local),
        out_shape=[
            shape((5, D, D), F32),
            shape((2, half_rows, D), F32),
            shape((width, D), F32),
            shape((1, D), F32),
            shape((1, D), F32),
        ],
        in_specs=[VM] * 9,
        out_specs=[VM] * 5,
        scratch_shapes=[
            pltpu.VMEM((4,) * (digits - d) + (half_rows, D), F32) for d in range(digits)
        ]
        + [pltpu.VMEM((4,) * (digits - d - 1) + (half_rows, D), F32) for d in range(digits)]
        + [
            pltpu.VMEM(mine.shape, F32),
            pltpu.VMEM(mine.shape, F32),
            pltpu.VMEM((count, 1, D), F32),
            pltpu.VMEM((count, 1, D), F32),
            pltpu.VMEM((TILE, D), F32),
            pltpu.VMEM((TILE, D), F32),
            sems((digits, 4)),
            sems((digits, 4)),
            sems((count,)),
            sems((count,)),
            sems((count,)),
            sems((count,)),
            sems((6,)),
            sems((2, 2)),
        ]
        + FourSum.scratch(count, 2 * TILE)
        + Sum.scratch(count, 2 * TILE)
        + Sum.scratch(count, TILE),
        compiler_params=params(14, 4),
        name="tail",
    )(att.reshape((4,) * digits + (padded, D)), own, piece, mine, small_all, wmod, *olds[:3])


def update_kernel(scale, rates, bounds, *refs):
    fac_ref, att_ref, modg_ref, own_ref = refs[:4]
    olds, masters, done = refs[4:9], refs[9:14], refs[14:16]
    outs, final, sem = refs[16:31], refs[31:33], refs[33]
    copies = [
        pltpu.make_async_copy(source, target, sem.at[at])
        for at, (source, target) in enumerate(zip(done, final))
    ]
    for copy in copies:
        copy.start()
    n_att, wide, n_pro = bounds
    first_rows = att_ref.shape[1]
    skip = 2 * first_rows - up_to(n_att, 8)
    joined = jnp.concatenate([att_ref[0], att_ref[1, skip:]], axis=0)
    grads = [
        modg_ref[...],
        joined[0:n_att],
        own_ref[0, wide : wide + n_pro, :],
        own_ref[0, 0:wide, :],
        own_ref[1, 0:wide, :],
    ]
    for index in range(5):
        grad = grads[index] * scale
        moment = moment_decay * olds[index][...] + grad
        direction = dot_three(moment, fac_ref[index])
        outs[3 * index][...] = grad
        outs[3 * index + 1][...] = masters[index][...] - rates[index] * direction
        outs[3 * index + 2][...] = moment
    for copy in copies:
        copy.wait()


def update(fac, att, modg, own, olds, masters, done, scale, count):
    shape = jax.ShapeDtypeStruct
    out = []
    for m in masters:
        out += [shape(m.shape, F32)] * 3
    out += [shape(value.shape, value.dtype) for value in done]
    anywhere = pl.BlockSpec(memory_space=pl.ANY)
    rates = [matrix_rate * 0.2 * math.sqrt(max(D, m.shape[0] * count)) for m in masters]
    bounds = (olds[1].shape[0], olds[3].shape[0], olds[2].shape[0])
    return pl.pallas_call(
        functools.partial(update_kernel, scale, rates, bounds),
        out_shape=out,
        in_specs=[VM] * 14 + [anywhere] * 2,
        out_specs=[VM] * 15 + [anywhere] * 2,
        scratch_shapes=[pltpu.SemaphoreType.DMA((2,))],
        compiler_params=params(8),
        name="update",
    )(fac, att, modg, own, *olds, *masters, *done)


def on_device(
    tokens,
    condition,
    cotangent,
    modulate_weight,
    attend_weight,
    project_weight,
    expand_weight,
    reduce_weight,
    bias_flat,
    modulate_moment,
    attend_moment,
    project_moment,
    expand_moment,
    reduce_moment,
    bias_moment,
):
    count = lax.axis_size("shard")
    full = tokens.shape[1] * lax.axis_size("ctx")
    olds = [
        m.T
        for m in (modulate_moment, attend_moment, project_moment, expand_moment, reduce_moment)
    ]
    masters = [
        w.T
        for w in (modulate_weight, attend_weight, project_weight, expand_weight, reduce_weight)
    ]
    n_att, n_pro, n_wide = (w.shape[0] for w in masters[1:4])
    nbias = bias_flat.shape[0]
    tok = tokens[0]
    (
        small_all,
        mod_rows,
        wide_rows,
        project_turn,
        expand_turn,
        reduce_turn,
        weight_core,
        xin,
        q,
        k,
        v,
        ctx_turn,
        lse,
        ctx,
    ) = front(masters[1:], masters[0], condition, bias_flat[None], tok, count)
    block_out, mid, gp, ge, gr, sums, wides, dctx = branch(
        ctx,
        tok,
        cotangent[0],
        mod_rows,
        wide_rows,
        project_turn,
        expand_turn[:, :n_wide].reshape(FF, D),
        reduce_turn[:, :n_wide].reshape(FF, D),
    )
    gp = pad_rows(gp.reshape(count, n_pro, D), up_to(n_pro, 8))
    scale = 1.0 / math.sqrt(tokens.shape[0] * count * full)
    tokens_grad, att, mine, mlp_rows, piece = attention_backward(
        dctx,
        xin,
        q,
        k,
        v,
        ctx_turn,
        lse,
        weight_core,
        tok,
        mid,
        mod_rows,
        gp,
        ge.reshape(count, n_wide, D),
        gr.reshape(count, n_wide, D),
        olds[3],
        olds[4],
        sums,
        wides,
        scale,
    )
    att = pad_rows(att.reshape(count, n_att, D), up_to(n_att, 8))
    fac, att_rows, modg, bias_sum, condition_rows = tail(
        att, mlp_rows, piece, mine, small_all, masters[0], olds, scale, (n_att, n_pro, n_wide)
    )
    done = (block_out[None], tokens_grad[None])
    out = update(fac, att_rows, modg, mlp_rows, olds, masters, done, scale, count)
    bias_grad = bias_sum[0, :nbias] * scale
    bias_new = moment_decay * bias_moment + bias_grad
    result = [*out[15:], condition_rows]
    result += [value.T for value in out[:15]]
    result += [bias_grad, bias_flat - bias_rate * bias_new, bias_new]
    return tuple(result)


def solution(mesh):
    tok = P("shard", "ctx", None)
    row = P("shard", None)
    col = P(None, "shard")
    flat = P("shard")
    return jax.shard_map(
        on_device,
        mesh=mesh,
        in_specs=(tok, row, tok) + (col,) * 5 + (flat,) + (col,) * 5 + (flat,),
        out_specs=(tok, tok, row) + (col,) * 15 + (flat,) * 3,
        check_vma=False,
    )
```
